32 devices in a mesh: section: 8 (over z, y), expert: 4 (over x, core).
Axes of the slice: x: 2, y: 2, z: 4, core: 2. Of those that a mesh axis runs over, the one named last changes fastest.
Arguments:
- x_fwd: bfloat16 [8, 256, 3584], P('section', 'expert'), may hold values from -6 to 6
- saved_gate: bfloat16 [8, 4, 34, 2048], P('section', None, None, 'expert'), may hold values from -6 to 6
- saved_up: bfloat16 [8, 4, 34, 2048], P('section', None, None, 'expert'), may hold values from -6 to 6
- grad_next: bfloat16 [8, 256, 3584], P('section', 'expert'), may hold values from -6 to 6
- routes_fwd: int32 [8, 256, 1], P('section', 'expert'), may hold values from 0 to 1; in each aligned block of 64 rows (0 to 63, 64 to 127, ..., all dimensions but the last counted through in order) at most 34 rows name the same one
- routes_bwd: int32 [8, 256, 1], P('section', 'expert'), may hold values from 0 to 1; in each aligned block of 64 rows (0 to 63, 64 to 127, ..., all dimensions but the last counted through in order) at most 34 rows name the same one
- scores_fwd: float32 [8, 256, 1], P('section', 'expert'), may hold values from 0.05 to 1
- scores_bwd: float32 [8, 256, 1], P('section', 'expert'), may hold values from 0.05 to 1
- w_gate: bfloat16 [8, 3584, 2048], P('section', None, 'expert'), may hold values from -0.09375 to 0.09375
- w_up: bfloat16 [8, 3584, 2048], P('section', None, 'expert'), may hold values from -0.09375 to 0.09375
- w_down: bfloat16 [8, 2048, 3584], P('section', 'expert'), may hold values from -0.1875 to 0.1875
Outputs:
- next_input: bfloat16 [8, 256, 3584], P('section', 'expert')
- input_grad: bfloat16 [8, 256, 3584], P('section', 'expert')
- score_grad: float32 [8, 256, 1], P('section', 'expert')
The draws below stay inside these ranges and needn't reach their ends.
Inputs may be any that keep to these rules, and one draw needn't show every extreme that they name: `routes_fwd`: among the tokens of one device no expert is named by more than 34 of them, and in every draw some expert is named by exactly 34. `routes_bwd`: as for routes_fwd.
All inputs are finite; a program needn't handle non-finite values.
Results may differ from the reference program's by a relative error of at most 0.0052.
Values may be sent and summed in bfloat16 or wider, within the bound.
No kernel may reach another device: no remote copies, remote signals or barrier semaphores. Data moves between devices by JAX's collectives and lax.ppermute only.
A program may use at most 64 MiB of HBM per device.

```python
import math
import jax
import jax.numpy as jnp
import numpy as np
from jax import lax

D = 3584
FH = 1024
EXPERTS = 2
TOP = 1
TOK_DEV = 64
SLICES = 2
FH_DEV = 512
CAP = 34
TOKENS = 256
LAYERS = 8
N_EXPERT = 4


def level_of(rng, extent, shards, low, top_value):
    def one(axis_at, shards_of):
        steps = jax.random.uniform(jax.random.fold_in(jax.random.fold_in(rng, 6), axis_at), (shards_of,), jnp.float32, low / len(shards), top_value / len(shards))
        return jnp.repeat(jnp.exp(steps), extent[axis_at] // shards_of).reshape((-1,) + (1,) * (len(extent) - axis_at - 1))

    factor_of = one(*shards[0])
    for cut in shards[1:]:
        factor_of = factor_of * one(*cut)
    return factor_of


def routed_block(own_key, own, number, rows, amount, top, limit, lean):
    ranking = jax.random.permutation(own_key, amount)
    packed, usual = shares(amount, rows * top, limit, lean, True), shares(amount, rows * top, limit, lean, False)
    places = jnp.arange(amount)

    def named(lengths, turn):
        used = int((lengths > 0).sum())
        fixed = max(1, used // 4)
        passed = fixed + (places - fixed + turn * (used - fixed)) % max(1, amount - fixed)
        return jnp.zeros((amount,), jnp.int32).at[ranking[jnp.where(places < fixed, places, passed)]].set(jnp.asarray(lengths, jnp.int32))

    lengths = jnp.where(number % 4 == 0, named(packed, number // 4), named(usual, number - number // 4 - 1))
    mixed = jax.random.permutation(jax.random.fold_in(own, 3), amount)
    donor, taker = mixed[0:amount // 2 * 2:2], mixed[1:amount // 2 * 2:2]
    slack = jnp.minimum(lengths[donor] - 1, limit - lengths[taker]) // 2
    slack = jnp.where((donor == ranking[0]) | (taker == ranking[0]) | (lengths[taker] == 0), 0, jnp.maximum(slack, 0))
    passed = jax.random.randint(jax.random.fold_in(own, 4), (amount // 2,), 0, 1 << 20) % (slack + 1)
    lengths = lengths.at[donor].add(-passed).at[taker].add(passed)
    members = jnp.searchsorted(jnp.cumsum(lengths), jnp.arange(rows * top), side="right").astype(jnp.int32)
    listing = members.reshape(top, rows).T
    listing = listing[jax.random.permutation(jax.random.fold_in(own, 1), rows)]
    turn = jax.random.randint(jax.random.fold_in(own, 2), (rows, 1), 0, top)
    return jnp.take_along_axis(listing, (jnp.arange(top)[None, :] + turn) % top, axis=1)


def shares(amount, total, limit, lean, full):
    weights = [(1 << 20) // math.isqrt(rank ** lean) + 1 for rank in range(1, amount + 1)]
    largest = limit if full else min(limit, max(-(-total // amount), total * weights[0] // sum(weights)))
    least = 1 if total - largest >= amount - 1 else 0
    counts, surplus = [largest] + [least] * (amount - 1), total - largest - least * (amount - 1)
    while surplus > 0:
        free = [i for i in range(1, amount) if counts[i] < largest] or [i for i in range(1, amount) if counts[i] < limit]
        mass, budget = sum([weights[i] for i in free]), surplus
        for i in free:
            extra = min(limit - counts[i], max(1, budget * weights[i] // mass), surplus)
            counts[i] = counts[i] + extra
            surplus = surplus - extra
    return np.array(counts)


def centred(rng, extent, scale, bound, split=(), kind=jnp.bfloat16):
    array = jax.random.normal(rng, extent, jnp.float32) * scale
    if len(split) > 0:
        array = level_of(rng, extent, split, -0.22, 0.18) * array
    return jnp.clip(array, min=-bound, max=bound).astype(kind)


def setup_inputs(seed: int = 0) -> dict:
    key_list = jax.random.split(jax.random.key(seed), 12)
    x_fwd = centred(key_list[0], (LAYERS, TOKENS, D), 1.0, 6.0, ((0, 8), (1, 4)))
    saved_gate = centred(key_list[1], (LAYERS, N_EXPERT, CAP, EXPERTS * FH), 1.0, 6.0, ((0, 8), (3, 4)))
    saved_up = centred(key_list[2], (LAYERS, N_EXPERT, CAP, EXPERTS * FH), 1.0, 6.0, ((0, 8), (3, 4)))
    grad_next = centred(key_list[3], (LAYERS, TOKENS, D), 1.0, 6.0, ((0, 8), (1, 4)))
    routes_fwd_keys = jax.random.split(jax.random.fold_in(key_list[4], 1), LAYERS * TOKENS // TOK_DEV)
    routes_fwd_turns = jax.random.permutation(jax.random.fold_in(key_list[4], 3), LAYERS * TOKENS // TOK_DEV)
    routes_fwd = jax.vmap(lambda own, number: routed_block(jax.random.fold_in(key_list[4], 2), own, number, TOK_DEV, EXPERTS, TOP, CAP, 2))(routes_fwd_keys, routes_fwd_turns).reshape((LAYERS, TOKENS, TOP))
    routes_bwd_keys = jax.random.split(jax.random.fold_in(key_list[5], 1), LAYERS * TOKENS // TOK_DEV)
    routes_bwd_turns = jax.random.permutation(jax.random.fold_in(key_list[5], 3), LAYERS * TOKENS // TOK_DEV)
    routes_bwd = jax.vmap(lambda own, number: routed_block(jax.random.fold_in(key_list[5], 2), own, number, TOK_DEV, EXPERTS, TOP, CAP, 2))(routes_bwd_keys, routes_bwd_turns).reshape((LAYERS, TOKENS, TOP))
    scores_fwd = jnp.clip(0.05 + 0.95 * jax.random.uniform(key_list[6], (LAYERS, TOKENS, TOP), jnp.float32) ** level_of(key_list[6], (LAYERS, TOKENS, TOP), ((0, 8), (1, 4)), -0.2, 0.2), 0.05, 1.0)
    scores_bwd = jnp.clip(0.05 + 0.95 * jax.random.uniform(key_list[7], (LAYERS, TOKENS, TOP), jnp.float32) ** level_of(key_list[7], (LAYERS, TOKENS, TOP), ((0, 8), (1, 4)), -0.2, 0.2), 0.05, 1.0)
    w_gate = centred(key_list[8], (LAYERS, D, EXPERTS * FH), D ** -0.5, 0.09375, ((0, 8), (2, 4)))
    w_up = centred(key_list[9], (LAYERS, D, EXPERTS * FH), D ** -0.5, 0.09375, ((0, 8), (2, 4)))
    w_down = centred(key_list[10], (LAYERS, EXPERTS * FH, D), FH ** -0.5, 0.1875, ((0, 8), (1, 4)))
    return {"x_fwd": x_fwd, "saved_gate": saved_gate, "saved_up": saved_up, "grad_next": grad_next, "routes_fwd": routes_fwd, "routes_bwd": routes_bwd, "scores_fwd": scores_fwd, "scores_bwd": scores_bwd, "w_gate": w_gate, "w_up": w_up, "w_down": w_down}


def gates_of(scores):
    return 2.5 * scores


def slot_table(routes):
    blocks = routes.reshape(N_EXPERT, -1)
    hits = (blocks[:, :, None] == jnp.arange(EXPERTS, dtype=jnp.int32)[None, None, :]).astype(jnp.int32)
    before = jnp.cumsum(hits, axis=1) - hits
    ranks = jnp.sum(before * hits, axis=2).astype(jnp.int32)
    source = jnp.arange(N_EXPERT, dtype=jnp.int32)[:, None]
    return ((source * EXPERTS + blocks) * CAP + ranks).reshape(-1).astype(jnp.int32)


def to_slots(rows, index, top):
    spread = jnp.repeat(rows, top, axis=0)
    buffer = jnp.zeros((N_EXPERT * EXPERTS * CAP, rows.shape[1]), rows.dtype).at[index].set(spread)
    return buffer.reshape(N_EXPERT, EXPERTS, CAP, rows.shape[1])


def layer_forward(x, routes, scores, wg, wu, wd):
    index = slot_table(routes)
    top = routes.shape[1]
    slots = to_slots(x, index, top).astype(jnp.float32)
    wg_r = wg.reshape(D, EXPERTS, SLICES, FH_DEV).astype(jnp.float32)
    wu_r = wu.reshape(D, EXPERTS, SLICES, FH_DEV).astype(jnp.float32)
    wd_r = wd.reshape(EXPERTS, SLICES, FH_DEV, D).astype(jnp.float32)
    g = jnp.einsum('qecd,desf->qecsf', slots, wg_r)
    u = jnp.einsum('qecd,desf->qecsf', slots, wu_r)
    h = (jax.nn.silu(g) * u).astype(jnp.bfloat16)
    part = jnp.einsum('qecsf,esfd->qecsd', h.astype(jnp.float32), wd_r).astype(jnp.bfloat16)
    part = lax.optimization_barrier(part)
    out = jnp.sum(part.astype(jnp.float32), axis=3)
    rows = out.reshape(-1, x.shape[1])[index].reshape(x.shape[0], top, x.shape[1])
    gate = gates_of(scores)
    return (x.astype(jnp.float32) + jnp.sum(gate[:, :, None] * rows, axis=1)).astype(jnp.bfloat16)


def layer_backward(dy, routes, scores, sg, su, wg, wu, wd):
    index = slot_table(routes)
    top = routes.shape[1]
    slots = to_slots(dy, index, top).astype(jnp.float32)
    wg_r = wg.reshape(D, EXPERTS, SLICES, FH_DEV).astype(jnp.float32)
    wu_r = wu.reshape(D, EXPERTS, SLICES, FH_DEV).astype(jnp.float32)
    wd_r = wd.reshape(EXPERTS, SLICES, FH_DEV, D).astype(jnp.float32)
    g = sg.reshape(N_EXPERT, CAP, EXPERTS, SLICES, FH_DEV).transpose(0, 2, 1, 3, 4).astype(jnp.float32)
    u = su.reshape(N_EXPERT, CAP, EXPERTS, SLICES, FH_DEV).transpose(0, 2, 1, 3, 4).astype(jnp.float32)
    a = jnp.einsum('qecd,esfd->qecsf', slots, wd_r)
    sig = jax.nn.sigmoid(g)
    hb = (jax.nn.silu(g) * u).astype(jnp.bfloat16)
    dgp = (a * u * sig * (1.0 + g * (1.0 - sig))).astype(jnp.bfloat16)
    dup = (a * g * sig).astype(jnp.bfloat16)
    dpart = (jnp.einsum('qecsf,desf->qecsd', dgp.astype(jnp.float32), wg_r)
             + jnp.einsum('qecsf,desf->qecsd', dup.astype(jnp.float32), wu_r)).astype(jnp.bfloat16)
    dpart = lax.optimization_barrier(dpart)
    dxe = jnp.sum(dpart.astype(jnp.float32), axis=3)
    inner = jnp.sum(a * hb.astype(jnp.float32), axis=(3, 4))
    grad_rows = dxe.reshape(-1, dy.shape[1])[index].reshape(dy.shape[0], top, dy.shape[1])
    dgate = inner.reshape(-1)[index].reshape(dy.shape[0], top)
    gate = gates_of(scores)
    dx = (dy.astype(jnp.float32) + jnp.sum(gate[:, :, None] * grad_rows, axis=1)).astype(jnp.bfloat16)
    dscore = 2.5 * dgate
    return dx, dscore


def reference(x_fwd, saved_gate, saved_up, grad_next, routes_fwd, routes_bwd, scores_fwd, scores_bwd, w_gate, w_up, w_down):
    def fwd_one(args):
        return layer_forward(*args)

    outputs = lax.map(fwd_one, (x_fwd, routes_fwd, scores_fwd, w_gate, w_up, w_down))
    next_input = jnp.roll(outputs, 1, axis=0)
    grads = jnp.roll(grad_next, -1, axis=0)

    def bwd_one(args):
        return layer_backward(*args)

    input_grad, score_grad = lax.map(bwd_one, (grads, routes_bwd, scores_bwd, saved_gate, saved_up, w_gate, w_up, w_down))
    return next_input, input_grad, score_grad
```

```python
import jax
import jax.numpy as jnp
from jax import lax
from jax.sharding import PartitionSpec as P

EXPERTS = 2


def from_behind(block, axis, distance):
    devices = range(lax.axis_size(axis))
    route = [((i - distance) % len(devices), i) for i in devices]
    return lax.ppermute(block, axis, route)


def across(block, distance, count, slices):
    route = [
        (e * slices + j, (e + distance) % count * slices + j)
        for e in range(count)
        for j in range(slices)
    ]
    return lax.ppermute(block, "expert", route)


def beside(block, distance, count, slices):
    route = [
        (e * slices + j, e * slices + (j + distance) % slices)
        for e in range(count)
        for j in range(slices)
    ]
    return lax.ppermute(block, "expert", route)


def ranks_of(routes, count):
    flat = routes.reshape(-1)
    tok = flat.shape[0]
    same = flat[:, None] == flat[None, :]
    earlier = jnp.arange(tok)[None, :] < jnp.arange(tok)[:, None]
    return flat, jnp.sum((same & earlier).astype(jnp.int32), axis=1)


def table_of(flat, rank, expert, capacity):
    return (
        (flat[None, :] == expert)
        & (rank[None, :] == jnp.arange(capacity, dtype=jnp.int32)[:, None])
    ).astype(jnp.bfloat16)


def body(
    x_fwd,
    saved_gate,
    saved_up,
    grad_next,
    routes_fwd,
    routes_bwd,
    scores_fwd,
    scores_bwd,
    w_gate,
    w_up,
    w_down,
):
    groups = lax.axis_size("expert")
    count = EXPERTS
    slices = groups // count
    me = lax.axis_index("expert")
    mine_e = me // slices
    mine_j = me % slices
    wg = w_gate[0]
    wu = w_up[0]
    wd = w_down[0]
    capacity = saved_gate.shape[2]
    depth = x_fwd.shape[2]
    f32 = jnp.float32

    def tables(routes):
        flat, rank = ranks_of(routes, count)
        return [table_of(flat, rank, (mine_e + d) % count, capacity) for d in range(count)]

    def pick(table, tokens):
        return jnp.dot(table, tokens, preferred_element_type=f32).astype(jnp.bfloat16)

    def dispatch(tabs, tokens):
        sent = [pick(tabs[d], tokens) for d in range(count)]
        got = [sent[0]] + [across(sent[d], d, count, slices) for d in range(1, count)]
        out = [got]
        for k in range(1, slices):
            out.append([beside(b, k, count, slices) for b in got])
        return jnp.concatenate([b for row in out for b in row], axis=0)

    def combine(parts):
        total = parts[0]
        for k in range(1, slices):
            total = total + beside(
                parts[k].astype(jnp.bfloat16), -k, count, slices
            ).astype(f32)
        back = [total[0]]
        for d in range(1, count):
            back.append(across(total[d].astype(jnp.bfloat16), -d, count, slices).astype(f32))
        return back

    def give(tabs, back, gate):
        rows = sum(
            lax.dot_general(
                t, b.astype(jnp.bfloat16), (((0,), (0,)), ((), ())), preferred_element_type=f32
            )
            for t, b in zip(tabs, back)
        )
        return gate * rows

    tokens = x_fwd[0]
    tabs_a = tables(routes_fwd[0])
    tabs_b = tables(routes_bwd[0])
    upstream = from_behind(grad_next, "section", -1)[0]

    flat = dispatch(tabs_a, tokens)
    g = jnp.dot(flat, wg, preferred_element_type=f32)
    u = jnp.dot(flat, wu, preferred_element_type=f32)
    hidden = (jax.nn.silu(g) * u).astype(jnp.bfloat16)
    parts = jnp.dot(hidden, wd, preferred_element_type=f32)
    back = combine(parts.reshape(slices, count, capacity, depth))
    gate_a = 2.5 * scores_fwd[0]
    layer_out = (tokens.astype(f32) + give(tabs_a, back, gate_a)).astype(jnp.bfloat16)
    next_input = from_behind(layer_out[None], "section", 1)

    recv_d = dispatch(tabs_b, upstream)
    order = [
        (mine_e - d) % count * slices + (mine_j - k) % slices
        for k in range(slices)
        for d in range(count)
    ]
    g = jnp.concatenate([saved_gate[0, q] for q in order], axis=0).astype(f32)
    u = jnp.concatenate([saved_up[0, q] for q in order], axis=0).astype(f32)
    sig = jax.nn.sigmoid(g)
    hidden = (jax.nn.silu(g) * u).astype(jnp.bfloat16)
    pulled = lax.dot_general(recv_d, wd, (((1,), (1,)), ((), ())), preferred_element_type=f32)
    dgp = (pulled * u * sig * (1.0 + g * (1.0 - sig))).astype(jnp.bfloat16)
    dup = (pulled * g * sig).astype(jnp.bfloat16)
    nt = (((1,), (1,)), ((), ()))
    dxe = lax.dot_general(dgp, wg, nt, preferred_element_type=f32) + lax.dot_general(
        dup, wu, nt, preferred_element_type=f32
    )
    inner = jnp.sum(pulled * hidden.astype(f32), axis=-1).reshape(slices, count, capacity)
    total = inner[0]
    for k in range(1, slices):
        total = total + beside(inner[k], -k, count, slices)
    home = [total[0]] + [across(total[d], -d, count, slices) for d in range(1, count)]
    dgate = sum(
        jnp.sum(t.astype(f32) * h[:, None], axis=0) for t, h in zip(tabs_b, home)
    )
    back = combine(dxe.reshape(slices, count, capacity, depth))
    gate_b = 2.5 * scores_bwd[0]
    input_grad = (upstream.astype(f32) + give(tabs_b, back, gate_b)).astype(jnp.bfloat16)
    score_grad = 2.5 * dgate
    return (next_input, input_grad[None], score_grad[None, :, None])


def solution(mesh):
    placed = (
        P("section", "expert", None),
        P("section", None, None, "expert"),
        P("section", None, None, "expert"),
        P("section", "expert", None),
        P("section", "expert", None),
        P("section", "expert", None),
        P("section", "expert", None),
        P("section", "expert", None),
        P("section", None, "expert"),
        P("section", None, "expert"),
        P("section", "expert", None),
    )
    return jax.shard_map(
        body,
        mesh=mesh,
        in_specs=placed,
        out_specs=(
            P("section", "expert", None),
            P("section", "expert", None),
            P("section", "expert", None),
        ),
        check_vma=False,
    )
```

```python
import functools

import jax
import jax.numpy as jnp
from jax import lax
from jax.experimental import pallas as pl
from jax.experimental.pallas import tpu as pltpu
from jax.sharding import PartitionSpec as P

EXPERTS = 2
LANES = 128
F32 = jnp.float32
BF16 = jnp.bfloat16
NT = (((1,), (1,)), ((), ()))


class Sizes:
    def __init__(self, cap, depth, count, slices, tok):
        self.cap, self.depth, self.count, self.slices, self.tok = cap, depth, count, slices, tok
        self.main = cap // 16 * 16
        self.extra = cap - self.main
        self.folds = depth // LANES
        assert self.folds < self.main and depth % LANES == 0
        self.width = depth + LANES * self.extra
        self.blocks = count * slices
        self.tail_rows = -(-(self.blocks * self.extra) // 16) * 16
        self.rows = self.blocks * self.main + self.tail_rows


def from_behind(block, axis, distance):
    devices = range(lax.axis_size(axis))
    route = [((i - distance) % len(devices), i) for i in devices]
    return lax.ppermute(block, axis, route)


def across(block, distance, s):
    route = [
        (e * s.slices + j, (e + distance) % s.count * s.slices + j)
        for e in range(s.count)
        for j in range(s.slices)
    ]
    return lax.ppermute(block, "expert", route)


def beside(block, distance, s):
    route = [
        (e * s.slices + j, e * s.slices + (j + distance) % s.slices)
        for e in range(s.count)
        for j in range(s.slices)
    ]
    return lax.ppermute(block, "expert", route)


def iota(shape, dim):
    return lax.broadcasted_iota(jnp.int32, shape, dim).astype(F32)


def as_column(row):
    n = row.shape[1]
    return jnp.sum(
        jnp.where(iota((n, n), 0) == iota((n, n), 1), row, 0.0), axis=1, keepdims=True
    )


def own_expert(s):
    return lax.axis_index("expert") // s.slices


def expert_at(s, distance):
    return ((own_expert(s) + distance) % s.count).astype(F32)


def slot_rows(route_row, s):
    col = as_column(route_row)
    n = s.tok
    same = (col == route_row) & (iota((n, n), 0) < iota((n, n), 1))
    return jnp.sum(jnp.where(same, 1.0, 0.0), axis=0, keepdims=True)


def slot_columns(route_row, s):
    col = as_column(route_row)
    n = s.tok
    same = (col == route_row) & (iota((n, n), 1) < iota((n, n), 0))
    return col, jnp.sum(jnp.where(same, 1.0, 0.0), axis=1, keepdims=True)


def fold(values_ref, first, tail_ref, s):
    for j in range(s.extra):
        for r in range(s.folds):
            tail_ref[r : r + 1, j * LANES : (j + 1) * LANES] = values_ref[
                first + j : first + j + 1, r * LANES : (r + 1) * LANES
            ]


def unfold(tail_ref, values_ref, first, s):
    for j in range(s.extra):
        for r in range(s.folds):
            values_ref[first + j : first + j + 1, r * LANES : (r + 1) * LANES] = tail_ref[
                r : r + 1, j * LANES : (j + 1) * LANES
            ]


def slot_values(route_row, value_row, expert, s):
    rank = slot_rows(route_row, s)
    hit = route_row == expert
    main = jnp.sum(
        jnp.where(hit & (rank == iota((s.main, s.tok), 0)), value_row, 0.0), axis=1, keepdims=True
    )
    extra = [
        jnp.sum(jnp.where(hit & (rank == float(s.main + j)), value_row, 0.0), axis=1, keepdims=True)
        for j in range(s.extra)
    ]
    return main, extra


def add_gated(out_ref, base_ref, main, extra, total, s):
    d = s.depth
    out_ref[:, :d] = (base_ref[:, :d].astype(F32) + main * total[:, :d]).astype(BF16)
    for j in range(s.extra):
        at = slice(d + j * LANES, d + (j + 1) * LANES)
        out_ref[:, at] = (base_ref[:, at].astype(F32) + extra[j] * total[:, at]).astype(BF16)


def pack_kernel(s, route_ref, x_ref, *rest):
    outs, (extra_ref, tail_ref) = rest[: s.count], rest[s.count :]
    route_row = route_ref[...].astype(F32)
    rank = slot_rows(route_row, s)
    high = s.main + 16
    slots = iota((high, s.tok), 0)
    tail_ref[...] = jnp.zeros_like(tail_ref)
    for d in range(s.count):
        hit = route_row == expert_at(s, d)
        table = jnp.where(hit & (rank == slots), 1.0, 0.0).astype(BF16)
        rows = jnp.dot(table, x_ref[...], preferred_element_type=F32)
        outs[d][:, : s.depth] = rows[: s.main].astype(BF16)
        extra_ref[...] = rows[s.main :]
        fold(extra_ref, 0, tail_ref, s)
        outs[d][:, s.depth :] = tail_ref[...].astype(BF16)


def gather_packs(packs, rows_ref, extra_ref, tail_ref, s):
    extra_ref[...] = jnp.zeros_like(extra_ref)
    for i, pack in enumerate(packs):
        rows_ref[i * s.main : (i + 1) * s.main, :] = pack[:, : s.depth]
        tail_ref[...] = pack[:, s.depth : s.width].astype(F32)
        unfold(tail_ref, extra_ref, i * s.extra, s)
    rows_ref[s.blocks * s.main :, :] = extra_ref[...].astype(BF16)


def scatter_chunk(value, outs, extra_ref, at, s):
    for i in range(s.blocks):
        outs[i // s.count][i % s.count, :, at] = value[i * s.main : (i + 1) * s.main].astype(BF16)
    extra_ref[:, at] = value[s.blocks * s.main :]


def scatter_tails(outs, extra_ref, tail_ref, s):
    for i in range(s.blocks):
        fold(extra_ref, i * s.extra, tail_ref, s)
        outs[i // s.count][i % s.count, :, s.depth : s.width] = tail_ref[...].astype(BF16)


def chunk_of(depth):
    for chunk in (512, 256, 128):
        if depth % chunk == 0:
            return chunk


def forward_kernel(s, *refs):
    packs = refs[: s.blocks]
    wg, wu, wd = refs[s.blocks : s.blocks + 3]
    outs = refs[s.blocks + 3 : s.blocks + 3 + s.slices]
    wg_v, wu_v, wd_v, rows_ref, extra_ref, tail_ref, sems = refs[s.blocks + 3 + s.slices :]
    chunk = wd_v.shape[2]
    steps = s.depth // chunk
    up, down = [], []
    for c in range(steps):
        at = pl.ds(c * chunk, chunk)
        up.append(
            (
                pltpu.make_async_copy(wg.at[at, :], wg_v.at[c], sems.at[0, c]),
                pltpu.make_async_copy(wu.at[at, :], wu_v.at[c], sems.at[1, c]),
            )
        )
        down.append(pltpu.make_async_copy(wd.at[:, at], wd_v.at[c], sems.at[2, c]))
    for pair in up:
        for copy in pair:
            copy.start()
    for copy in down:
        copy.start()
    gather_packs(packs, rows_ref, extra_ref, tail_ref, s)
    g = u = None
    for c in range(steps):
        for copy in up[c]:
            copy.wait()
        lhs = rows_ref[:, c * chunk : (c + 1) * chunk]
        more_g = jnp.dot(lhs, wg_v[c], preferred_element_type=F32)
        more_u = jnp.dot(lhs, wu_v[c], preferred_element_type=F32)
        g = more_g if g is None else g + more_g
        u = more_u if u is None else u + more_u
    hidden = (g * jax.nn.sigmoid(g) * u).astype(BF16)
    tail_ref[...] = jnp.zeros_like(tail_ref)
    for c in range(steps):
        down[c].wait()
        part = jnp.dot(hidden, wd_v[c], preferred_element_type=F32)
        scatter_chunk(part, outs, extra_ref, slice(c * chunk, (c + 1) * chunk), s)
    scatter_tails(outs, extra_ref, tail_ref, s)


def saved_kernel(s, gate_ref, up_ref, c1_ref, c2_ref, hb_ref, g_ref, u_ref):
    me = lax.axis_index("expert")
    e, j = me // s.slices, me % s.slices
    g_ref[...] = jnp.zeros_like(g_ref)
    u_ref[...] = jnp.zeros_like(u_ref)
    for i in range(s.blocks):
        k, d = i // s.count, i % s.count
        source = (e + s.count - d) % s.count * s.slices + (j + s.slices - k) % s.slices
        for src, dst in ((gate_ref, g_ref), (up_ref, u_ref)):
            rows = src[source].astype(F32)
            dst[i * s.main : (i + 1) * s.main, :] = rows[: s.main]
            first = s.blocks * s.main + i * s.extra
            dst[first : first + s.extra, :] = rows[s.main :]
    g = g_ref[...]
    u = u_ref[...]
    sig = jax.nn.sigmoid(g)
    c1_ref[...] = u * sig * (1.0 + g * (1.0 - sig))
    c2_ref[...] = g * sig
    hb_ref[...] = (g * sig * u).astype(BF16).astype(F32)


def split_three(value):
    high = value.astype(BF16).astype(F32)
    rest = value - high
    mid = rest.astype(BF16).astype(F32)
    return high, mid, (rest - mid).astype(BF16).astype(F32)


def put_inner(main, extra, s):
    lane = iota((s.main, LANES), 1)
    row = iota((s.main, LANES), 0)
    out = jnp.zeros((s.main, LANES), F32)
    for p, piece in enumerate(split_three(main)):
        out = jnp.where(lane == float(p), piece, out)
    for j in range(s.extra):
        for p, piece in enumerate(split_three(extra[j])):
            out = jnp.where((lane == float(3 + p)) & (row == float(j)), piece, out)
    return out.astype(BF16)


def get_inner(block, s):
    lane = iota((s.main, LANES), 1)
    row = iota((s.main, LANES), 0)
    main = jnp.sum(jnp.where(lane < 3.0, block, 0.0), axis=1, keepdims=True)
    second = jnp.sum(
        jnp.where((lane >= 3.0) & (lane < 6.0), block, 0.0), axis=1, keepdims=True
    )
    extra = [
        jnp.sum(jnp.where(row[:, :1] == float(j), second, 0.0), axis=0, keepdims=True)
        for j in range(s.extra)
    ]
    return main, extra


def backward_kernel(s, *refs):
    packs = refs[: s.blocks]
    c1, c2, hb, wg, wu, wd = refs[s.blocks : s.blocks + 6]
    outs = refs[s.blocks + 6 : s.blocks + 6 + s.slices]
    wg_v, wu_v, wd_v, rows_ref, extra_ref, tail_ref, sems = refs[s.blocks + 6 + s.slices :]
    chunk = wd_v.shape[2]
    steps = s.depth // chunk
    up, down = [], []
    for c in range(steps):
        at = pl.ds(c * chunk, chunk)
        up.append(
            (
                pltpu.make_async_copy(wg.at[at, :], wg_v.at[c], sems.at[0, c]),
                pltpu.make_async_copy(wu.at[at, :], wu_v.at[c], sems.at[1, c]),
            )
        )
        down.append(pltpu.make_async_copy(wd.at[:, at], wd_v.at[c], sems.at[2, c]))
    for copy in down:
        copy.start()
    for pair in up:
        for copy in pair:
            copy.start()
    gather_packs(packs, rows_ref, extra_ref, tail_ref, s)
    a = None
    for c in range(steps):
        down[c].wait()
        lhs = rows_ref[:, c * chunk : (c + 1) * chunk]
        more = lax.dot_general(lhs, wd_v[c], NT, preferred_element_type=F32)
        a = more if a is None else a + more
    dgp = (a * c1[...]).astype(BF16)
    dup = (a * c2[...]).astype(BF16)
    inner = jnp.sum(a * hb[...], axis=1, keepdims=True)
    for i in range(s.blocks):
        first = s.blocks * s.main + i * s.extra
        outs[i // s.count][i % s.count, :, s.width :] = put_inner(
            inner[i * s.main : (i + 1) * s.main],
            [inner[first + j : first + j + 1] for j in range(s.extra)],
            s,
        )
    tail_ref[...] = jnp.zeros_like(tail_ref)
    for c in range(steps):
        for copy in up[c]:
            copy.wait()
        part = lax.dot_general(dgp, wg_v[c], NT, preferred_element_type=F32) + lax.dot_general(
            dup, wu_v[c], NT, preferred_element_type=F32
        )
        scatter_chunk(part, outs, extra_ref, slice(c * chunk, (c + 1) * chunk), s)
    scatter_tails(outs, extra_ref, tail_ref, s)


def total_of(parts, d):
    total = parts[0][d].astype(F32)
    for part in parts[1:]:
        total = total + part[d].astype(F32)
    return total


def forward_sum_kernel(s, *refs):
    parts = refs[: s.slices]
    own, route_ref, score_ref = refs[s.slices : s.slices + 3]
    y_ref, backs = refs[s.slices + 3], refs[s.slices + 4 :]
    for d in range(1, s.count):
        backs[d - 1][...] = total_of(parts, d).astype(BF16)
    route_row = route_ref[...].astype(F32)
    main, extra = slot_values(route_row, 2.5 * score_ref[...], expert_at(s, 0), s)
    add_gated(y_ref, own, main, extra, total_of(parts, 0), s)
    y_ref[s.folds : s.folds + 1, s.depth : s.depth + s.tok] = route_row.astype(BF16)


def forward_add_kernel(s, distance, back, base, route_ref, score_ref, y_ref):
    route_row = route_ref[...].astype(F32)
    main, extra = slot_values(route_row, 2.5 * score_ref[...], expert_at(s, distance), s)
    add_gated(y_ref, base, main, extra, back[...].astype(F32), s)


def tokens_of(packs, route_row, rows_ref, extra_ref, tail_ref, s):
    extra_ref[...] = jnp.zeros_like(extra_ref)
    for d, pack in enumerate(packs):
        rows_ref[d * s.main : (d + 1) * s.main, :] = pack[:, : s.depth]
        tail_ref[...] = pack[:, s.depth : s.width].astype(F32)
        unfold(tail_ref, extra_ref, d * s.extra, s)
    rows_ref[s.count * s.main :, :] = extra_ref[...].astype(BF16)
    col, rank = slot_columns(route_row, s)
    high = rows_ref.shape[0]
    place = jnp.full((s.tok, 1), -1.0, F32)
    for d in range(s.count):
        at = jnp.where(
            rank < float(s.main),
            rank + float(d * s.main),
            rank + float(s.count * s.main + d * s.extra - s.main),
        )
        place = jnp.where(col == expert_at(s, d), at, place)
    table = jnp.where(place == iota((s.tok, high), 1), 1.0, 0.0).astype(BF16)
    return jnp.dot(table, rows_ref[...], preferred_element_type=F32)


def forward_end_kernel(s, *refs):
    packs = refs[: s.count]
    out_ref, rows_ref, extra_ref, tail_ref, row_ref = refs[s.count :]
    row_ref[...] = packs[0][:, s.depth : s.depth + LANES].astype(F32)
    route_row = row_ref[s.folds : s.folds + 1, : s.tok]
    out_ref[...] = tokens_of(packs, route_row, rows_ref, extra_ref, tail_ref, s).astype(BF16)


def backward_sum_kernel(s, *refs):
    parts, outs = refs[: s.slices], refs[s.slices :]
    for d in range(s.count - 1, -1, -1):
        total = total_of(parts, d)
        outs[d][:, : s.width] = total[:, : s.width].astype(BF16)
        main, extra = get_inner(total[:, s.width :], s)
        outs[d][:, s.width :] = put_inner(main, extra, s)


def backward_end_kernel(s, *refs):
    packs = refs[: s.count]
    dy_ref, route_ref, score_ref, out_ref, grad_ref = refs[s.count : s.count + 5]
    rows_ref, extra_ref, tail_ref = refs[s.count + 5 :]
    route_row = route_ref[...].astype(F32)
    rows = tokens_of(packs, route_row, rows_ref, extra_ref, tail_ref, s)
    gate = as_column(2.5 * score_ref[...])
    out_ref[...] = (dy_ref[...].astype(F32) + gate * rows).astype(BF16)
    rank = slot_rows(route_row, s)
    dgate = jnp.zeros((1, s.tok), F32)
    for d in range(s.count):
        hit = route_row == expert_at(s, d)
        main, extra = get_inner(packs[d][:, s.width :].astype(F32), s)
        dgate += jnp.sum(
            jnp.where(hit & (rank == iota((s.main, s.tok), 0)), main, 0.0), axis=0, keepdims=True
        )
        for j in range(s.extra):
            dgate += jnp.where(hit & (rank == float(s.main + j)), extra[j], 0.0)
    grad_ref[...] = 2.5 * dgate


VMEM = pl.BlockSpec(memory_space=pltpu.VMEM)
HBM = pl.BlockSpec(memory_space=pl.ANY)


def call(kernel, name, outs, scratch, ins, *args, mib=16, flops=0):
    shapes = [jax.ShapeDtypeStruct(shape, kind) for shape, kind in outs]
    size = sum(a.size * a.dtype.itemsize for a in args)
    return pl.pallas_call(
        kernel,
        out_shape=shapes,
        in_specs=ins,
        out_specs=[VMEM] * len(shapes),
        scratch_shapes=scratch,
        compiler_params=pltpu.CompilerParams(vmem_limit_bytes=mib << 20),
        cost_estimate=pl.CostEstimate(flops=flops, bytes_accessed=size, transcendentals=0),
        name=name,
    )(*args)


def tail_scratch(s, rows):
    return [
        pltpu.VMEM((rows, s.depth), F32),
        pltpu.VMEM((s.main, LANES * s.extra), F32),
    ]


def pack(s, routes, tokens):
    return call(
        functools.partial(pack_kernel, s),
        "pack",
        [((s.main, s.width), BF16)] * s.count,
        tail_scratch(s, 16),
        [VMEM, VMEM],
        routes,
        tokens,
    )


def weight_scratch(s, hidden):
    chunk = chunk_of(s.depth)
    steps = s.depth // chunk
    return [
        pltpu.VMEM((steps, chunk, hidden), BF16),
        pltpu.VMEM((steps, chunk, hidden), BF16),
        pltpu.VMEM((steps, hidden, chunk), BF16),
        pltpu.VMEM((s.rows, s.depth), BF16),
        *tail_scratch(s, s.tail_rows),
        pltpu.SemaphoreType.DMA((3, steps)),
    ]


def dispatch(s, packs):
    got = [packs[0]] + [across(packs[d], d, s) for d in range(1, s.count)]
    out = list(got)
    for k in range(1, s.slices):
        out += [beside(b, k, s) for b in got]
    return out


def gather_parts(s, parts):
    return [parts[0]] + [beside(parts[k], -k, s) for k in range(1, s.slices)]


def end_scratch(s):
    low = -(-(s.count * s.extra) // 16) * 16
    return [pltpu.VMEM((s.count * s.main + low, s.depth), BF16), *tail_scratch(s, low)]


def body(
    x_fwd,
    saved_gate,
    saved_up,
    grad_next,
    routes_fwd,
    routes_bwd,
    scores_fwd,
    scores_bwd,
    w_gate,
    w_up,
    w_down,
):
    groups = lax.axis_size("expert")
    tok, depth = x_fwd.shape[1:]
    s = Sizes(saved_gate.shape[2], depth, EXPERTS, groups // EXPERTS, tok)
    hidden = w_gate.shape[2]
    weights = (w_gate[0], w_up[0], w_down[0])
    flops = 6 * s.rows * depth * hidden
    route_a = routes_fwd.reshape(1, tok)
    route_b = routes_bwd.reshape(1, tok)
    score_a = scores_fwd.reshape(1, tok)
    score_b = scores_bwd.reshape(1, tok)

    sent_a = pack(s, route_a, x_fwd[0])
    rows_a = dispatch(s, sent_a)
    upstream = from_behind(grad_next, "section", -1)[0]

    parts_a = call(
        functools.partial(forward_kernel, s),
        "forward",
        [((s.count, s.main, s.width), BF16)] * s.slices,
        weight_scratch(s, hidden),
        [VMEM] * s.blocks + [HBM] * 3,
        *rows_a,
        *weights,
        mib=32,
        flops=flops,
    )
    parts_a = gather_parts(s, parts_a)
    sums = call(
        functools.partial(forward_sum_kernel, s),
        "forward_sum",
        [((s.main, s.width), BF16)] * s.count,
        [],
        [VMEM] * (s.slices + 3),
        *parts_a,
        sent_a[0],
        route_a,
        score_a,
    )
    moved = [from_behind(sums[0], "section", 1)]
    for d in range(1, s.count):
        back = across(sums[d], -d, s)
        y = call(
            functools.partial(forward_add_kernel, s, d),
            "forward_add",
            [((s.main, s.width), BF16)],
            [],
            [VMEM] * 4,
            back,
            sent_a[d],
            route_a,
            score_a,
        )[0]
        moved.append(from_behind(y, "section", 1))
    next_input = call(
        functools.partial(forward_end_kernel, s),
        "forward_end",
        [((tok, depth), BF16)],
        end_scratch(s) + [pltpu.VMEM((s.main, LANES), F32)],
        [VMEM] * s.count,
        *moved,
    )[0]

    sent_b = pack(s, route_b, upstream)
    rows_b = dispatch(s, sent_b)
    factors = call(
        functools.partial(saved_kernel, s),
        "saved",
        [((s.rows, hidden), F32)] * 3,
        [pltpu.VMEM((s.rows, hidden), F32)] * 2,
        [VMEM] * 2,
        saved_gate[0],
        saved_up[0],
    )
    wide = s.width + LANES
    parts_b = call(
        functools.partial(backward_kernel, s),
        "backward",
        [((s.count, s.main, wide), BF16)] * s.slices,
        weight_scratch(s, hidden),
        [VMEM] * (s.blocks + 3) + [HBM] * 3,
        *rows_b,
        *factors,
        *weights,
        mib=32,
        flops=flops,
    )
    parts_b = gather_parts(s, parts_b)
    sums = call(
        functools.partial(backward_sum_kernel, s),
        "backward_sum",
        [((s.main, wide), BF16)] * s.count,
        [],
        [VMEM] * s.slices,
        *parts_b,
    )
    back = [sums[0]] + [across(sums[d], -d, s) for d in range(1, s.count)]
    input_grad, score_grad = call(
        functools.partial(backward_end_kernel, s),
        "backward_end",
        [((tok, depth), BF16), ((1, tok), F32)],
        end_scratch(s),
        [VMEM] * (s.count + 3),
        *back,
        upstream,
        route_b,
        score_b,
    )
    return next_input[None], input_grad[None], score_grad.reshape(1, tok, 1)


def solution(mesh):
    placed = (
        P("section", "expert", None),
        P("section", None, None, "expert"),
        P("section", None, None, "expert"),
        P("section", "expert", None),
        P("section", "expert", None),
        P("section", "expert", None),
        P("section", "expert", None),
        P("section", "expert", None),
        P("section", None, "expert"),
        P("section", None, "expert"),
        P("section", "expert", None),
    )
    return jax.shard_map(
        body,
        mesh=mesh,
        in_specs=placed,
        out_specs=(
            P("section", "expert", None),
            P("section", "expert", None),
            P("section", "expert", None),
        ),
        check_vma=False,
    )
```

```python
import functools

import jax
import jax.numpy as jnp
from jax import lax
from jax.experimental import pallas as pl
from jax.experimental.pallas import tpu as pltpu
from jax.sharding import PartitionSpec as P

EXPERTS = 2
LANES = 128
F32 = jnp.float32
BF16 = jnp.bfloat16
NT = (((1,), (1,)), ((), ()))


class Sizes:
    def __init__(self, cap, depth, count, slices, tok):
        self.cap, self.depth, self.count, self.slices, self.tok = cap, depth, count, slices, tok
        self.main = cap // 16 * 16
        self.extra = cap - self.main
        self.folds = depth // LANES
        assert self.folds < self.main and depth % LANES == 0
        self.width = depth + LANES * self.extra
        self.blocks = count * slices
        self.tail_rows = -(-(self.blocks * self.extra) // 16) * 16
        self.rows = self.blocks * self.main + self.tail_rows


def from_behind(block, axis, distance):
    devices = range(lax.axis_size(axis))
    route = [((i - distance) % len(devices), i) for i in devices]
    return lax.ppermute(block, axis, route)


def across(block, distance, s):
    route = [
        (e * s.slices + j, (e + distance) % s.count * s.slices + j)
        for e in range(s.count)
        for j in range(s.slices)
    ]
    return lax.ppermute(block, "expert", route)


def beside(block, distance, s):
    route = [
        (e * s.slices + j, e * s.slices + (j + distance) % s.slices)
        for e in range(s.count)
        for j in range(s.slices)
    ]
    return lax.ppermute(block, "expert", route)


def iota(shape, dim):
    return lax.broadcasted_iota(jnp.int32, shape, dim).astype(F32)


def as_column(row):
    n = row.shape[1]
    return jnp.sum(
        jnp.where(iota((n, n), 0) == iota((n, n), 1), row, 0.0), axis=1, keepdims=True
    )


def own_expert(s):
    return lax.axis_index("expert") // s.slices


def expert_at(s, distance):
    return ((own_expert(s) + distance) % s.count).astype(F32)


def slot_rows(route_row, s):
    col = as_column(route_row)
    n = s.tok
    same = (col == route_row) & (iota((n, n), 0) < iota((n, n), 1))
    return jnp.sum(jnp.where(same, 1.0, 0.0), axis=0, keepdims=True)


def slot_columns(route_row, s):
    col = as_column(route_row)
    n = s.tok
    same = (col == route_row) & (iota((n, n), 1) < iota((n, n), 0))
    return col, jnp.sum(jnp.where(same, 1.0, 0.0), axis=1, keepdims=True)


def fold(values_ref, first, tail_ref, s):
    for j in range(s.extra):
        for r in range(s.folds):
            tail_ref[r : r + 1, j * LANES : (j + 1) * LANES] = values_ref[
                first + j : first + j + 1, r * LANES : (r + 1) * LANES
            ]


def unfold(tail_ref, values_ref, first, s):
    for j in range(s.extra):
        for r in range(s.folds):
            values_ref[first + j : first + j + 1, r * LANES : (r + 1) * LANES] = tail_ref[
                r : r + 1, j * LANES : (j + 1) * LANES
            ]


def slot_values(route_row, value_row, expert, s):
    rank = slot_rows(route_row, s)
    hit = route_row == expert
    main = jnp.sum(
        jnp.where(hit & (rank == iota((s.main, s.tok), 0)), value_row, 0.0), axis=1, keepdims=True
    )
    extra = [
        jnp.sum(jnp.where(hit & (rank == float(s.main + j)), value_row, 0.0), axis=1, keepdims=True)
        for j in range(s.extra)
    ]
    return main, extra


def add_gated(out_ref, base_ref, main, extra, total, s):
    d = s.depth
    out_ref[:, :d] = (base_ref[:, :d].astype(F32) + main * total[:, :d]).astype(BF16)
    for j in range(s.extra):
        at = slice(d + j * LANES, d + (j + 1) * LANES)
        out_ref[:, at] = (base_ref[:, at].astype(F32) + extra[j] * total[:, at]).astype(BF16)


def pack_rows(s, route_row, x, outs, extra_ref, tail_ref):
    rank = slot_rows(route_row, s)
    slots = iota((s.main + 16, s.tok), 0)
    tail_ref[...] = jnp.zeros_like(tail_ref)
    for d in range(s.count):
        hit = route_row == expert_at(s, d)
        table = jnp.where(hit & (rank == slots), 1.0, 0.0).astype(BF16)
        rows = jnp.dot(table, x, preferred_element_type=F32)
        outs[d][:, : s.depth] = rows[: s.main].astype(BF16)
        extra_ref[...] = rows[s.main :]
        fold(extra_ref, 0, tail_ref, s)
        outs[d][:, s.depth :] = tail_ref[...].astype(BF16)


def first_kernel(s, route_hbm, x_hbm, dy_hbm, *rest):
    outs, dy_ref = rest[: s.count], rest[s.count]
    route_ref, x_ref, extra_ref, tail_ref, sems = rest[s.count + 1 :]
    copies = [
        pltpu.make_async_copy(src, dst, sems.at[i])
        for i, (src, dst) in enumerate(
            ((route_hbm, route_ref), (x_hbm, x_ref), (dy_hbm, dy_ref))
        )
    ]
    for copy in copies:
        copy.start()
    copies[0].wait()
    copies[1].wait()
    pack_rows(s, route_ref[...].astype(F32), x_ref[...], outs, extra_ref, tail_ref)
    copies[2].wait()


def pack_kernel(s, route_ref, x_ref, *rest):
    outs, (extra_ref, tail_ref) = rest[: s.count], rest[s.count :]
    pack_rows(s, route_ref[...].astype(F32), x_ref[...], outs, extra_ref, tail_ref)


def load_kernel(*refs):
    sems = refs[-1]
    n = (len(refs) - 1) // 2
    copies = [pltpu.make_async_copy(refs[i], refs[n + i], sems.at[i]) for i in range(n)]
    for copy in copies:
        copy.start()
    for copy in copies:
        copy.wait()


def gather_packs(packs, rows_ref, extra_ref, tail_ref, s):
    extra_ref[...] = jnp.zeros_like(extra_ref)
    for i, pack in enumerate(packs):
        rows_ref[i * s.main : (i + 1) * s.main, :] = pack[:, : s.depth]
        tail_ref[...] = pack[:, s.depth : s.width].astype(F32)
        unfold(tail_ref, extra_ref, i * s.extra, s)
    rows_ref[s.blocks * s.main :, :] = extra_ref[...].astype(BF16)


def scatter_chunk(value, outs, extra_ref, at, s):
    for i in range(s.blocks):
        outs[i][:, at] = value[i * s.main : (i + 1) * s.main].astype(BF16)
    extra_ref[:, at] = value[s.blocks * s.main :]


def scatter_tails(outs, extra_ref, tail_ref, s):
    for i in range(s.blocks):
        fold(extra_ref, i * s.extra, tail_ref, s)
        outs[i][:, s.depth : s.width] = tail_ref[...].astype(BF16)


def chunk_of(depth):
    for chunk in (512, 256, 128):
        if depth % chunk == 0:
            return chunk


def forward_kernel(s, *refs):
    packs = refs[: s.blocks]
    wg, wu, wd = refs[s.blocks : s.blocks + 3]
    outs = refs[s.blocks + 3 : -3]
    rows_ref, extra_ref, tail_ref = refs[-3:]
    chunk = chunk_of(s.depth)
    gather_packs(packs, rows_ref, extra_ref, tail_ref, s)
    g = u = None
    for c in range(0, s.depth, chunk):
        lhs = rows_ref[:, c : c + chunk]
        more_g = jnp.dot(lhs, wg[c : c + chunk, :], preferred_element_type=F32)
        more_u = jnp.dot(lhs, wu[c : c + chunk, :], preferred_element_type=F32)
        g = more_g if g is None else g + more_g
        u = more_u if u is None else u + more_u
    hidden = (g * jax.nn.sigmoid(g) * u).astype(BF16)
    tail_ref[...] = jnp.zeros_like(tail_ref)
    for c in range(0, s.depth, chunk):
        part = jnp.dot(hidden, wd[:, c : c + chunk], preferred_element_type=F32)
        scatter_chunk(part, outs, extra_ref, slice(c, c + chunk), s)
    scatter_tails(outs, extra_ref, tail_ref, s)


def saved_kernel(s, gate_ref, up_ref, c1_ref, c2_ref, hb_ref, g_ref, u_ref):
    me = lax.axis_index("expert")
    e, j = me // s.slices, me % s.slices
    g_ref[...] = jnp.zeros_like(g_ref)
    u_ref[...] = jnp.zeros_like(u_ref)
    for i in range(s.blocks):
        k, d = i // s.count, i % s.count
        source = (e + s.count - d) % s.count * s.slices + (j + s.slices - k) % s.slices
        for src, dst in ((gate_ref, g_ref), (up_ref, u_ref)):
            rows = src[source].astype(F32)
            dst[i * s.main : (i + 1) * s.main, :] = rows[: s.main]
            first = s.blocks * s.main + i * s.extra
            dst[first : first + s.extra, :] = rows[s.main :]
    g = g_ref[...]
    u = u_ref[...]
    sig = jax.nn.sigmoid(g)
    c1_ref[...] = u * sig * (1.0 + g * (1.0 - sig))
    c2_ref[...] = g * sig
    hb_ref[...] = (g * sig * u).astype(BF16).astype(F32)


def split_three(value):
    high = value.astype(BF16).astype(F32)
    rest = value - high
    mid = rest.astype(BF16).astype(F32)
    return high, mid, (rest - mid).astype(BF16).astype(F32)


def put_inner(main, extra, s):
    lane = iota((s.main, LANES), 1)
    row = iota((s.main, LANES), 0)
    out = jnp.zeros((s.main, LANES), F32)
    for p, piece in enumerate(split_three(main)):
        out = jnp.where(lane == float(p), piece, out)
    for j in range(s.extra):
        for p, piece in enumerate(split_three(extra[j])):
            out = jnp.where((lane == float(3 + p)) & (row == float(j)), piece, out)
    return out.astype(BF16)


def get_inner(block, s):
    lane = iota((s.main, LANES), 1)
    row = iota((s.main, LANES), 0)
    main = jnp.sum(jnp.where(lane < 3.0, block, 0.0), axis=1, keepdims=True)
    second = jnp.sum(
        jnp.where((lane >= 3.0) & (lane < 6.0), block, 0.0), axis=1, keepdims=True
    )
    extra = [
        jnp.sum(jnp.where(row[:, :1] == float(j), second, 0.0), axis=0, keepdims=True)
        for j in range(s.extra)
    ]
    return main, extra


def backward_kernel(s, *refs):
    packs = refs[: s.blocks]
    c1, c2, hb, wg, wu, wd = refs[s.blocks : s.blocks + 6]
    outs = refs[s.blocks + 6 : -3]
    rows_ref, extra_ref, tail_ref = refs[-3:]
    chunk = chunk_of(s.depth)
    gather_packs(packs, rows_ref, extra_ref, tail_ref, s)
    a = None
    for c in range(0, s.depth, chunk):
        more = lax.dot_general(
            rows_ref[:, c : c + chunk], wd[:, c : c + chunk], NT, preferred_element_type=F32
        )
        a = more if a is None else a + more
    dgp = (a * c1[...]).astype(BF16)
    dup = (a * c2[...]).astype(BF16)
    inner = jnp.sum(a * hb[...], axis=1, keepdims=True)
    for i in range(s.blocks):
        first = s.blocks * s.main + i * s.extra
        outs[i][:, s.width :] = put_inner(
            inner[i * s.main : (i + 1) * s.main],
            [inner[first + j : first + j + 1] for j in range(s.extra)],
            s,
        )
    tail_ref[...] = jnp.zeros_like(tail_ref)
    for c in range(0, s.depth, chunk):
        part = lax.dot_general(
            dgp, wg[c : c + chunk, :], NT, preferred_element_type=F32
        ) + lax.dot_general(dup, wu[c : c + chunk, :], NT, preferred_element_type=F32)
        scatter_chunk(part, outs, extra_ref, slice(c, c + chunk), s)
    scatter_tails(outs, extra_ref, tail_ref, s)


def total_of(parts, d, k):
    total = parts[d][...].astype(F32)
    for part in parts[d + len(parts) // k :: len(parts) // k]:
        total = total + part[...].astype(F32)
    return total


def forward_sum_kernel(s, *refs):
    parts = refs[: s.blocks]
    own, route_ref, score_ref, y_ref = refs[s.blocks : s.blocks + 4]
    backs = refs[s.blocks + 4 :]
    for d in range(1, s.count):
        backs[d - 1][:, : s.width] = total_of(parts, d, s.slices).astype(BF16)
        backs[d - 1][:, s.width :] = jnp.zeros((s.main, LANES), BF16)
    route_row = route_ref[...].astype(F32)
    main, extra = slot_values(route_row, 2.5 * score_ref[...], expert_at(s, 0), s)
    add_gated(y_ref, own, main, extra, total_of(parts, 0, s.slices), s)
    y_ref[s.folds : s.folds + 1, s.depth : s.depth + s.tok] = route_row.astype(BF16)
    y_ref[:, s.width :] = jnp.zeros((s.main, LANES), BF16)


def forward_add_kernel(s, distance, back, base, route_ref, score_ref, y_ref):
    route_row = route_ref[...].astype(F32)
    main, extra = slot_values(route_row, 2.5 * score_ref[...], expert_at(s, distance), s)
    add_gated(y_ref, base, main, extra, back[:, : s.width].astype(F32), s)


def tokens_of(packs, route_row, rows_ref, extra_ref, tail_ref, s):
    extra_ref[...] = jnp.zeros_like(extra_ref)
    for d, pack in enumerate(packs):
        rows_ref[d * s.main : (d + 1) * s.main, :] = pack[:, : s.depth]
        tail_ref[...] = pack[:, s.depth : s.width].astype(F32)
        unfold(tail_ref, extra_ref, d * s.extra, s)
    rows_ref[s.count * s.main :, :] = extra_ref[...].astype(BF16)
    col, rank = slot_columns(route_row, s)
    high = rows_ref.shape[0]
    place = jnp.full((s.tok, 1), -1.0, F32)
    for d in range(s.count):
        at = jnp.where(
            rank < float(s.main),
            rank + float(d * s.main),
            rank + float(s.count * s.main + d * s.extra - s.main),
        )
        place = jnp.where(col == expert_at(s, d), at, place)
    table = jnp.where(place == iota((s.tok, high), 1), 1.0, 0.0).astype(BF16)
    return jnp.dot(table, rows_ref[...], preferred_element_type=F32)


def forward_end_kernel(s, *refs):
    packs = refs[: s.count]
    out_ref, rows_ref, extra_ref, tail_ref, row_ref = refs[s.count :]
    row_ref[...] = packs[0][:, s.depth : s.depth + LANES].astype(F32)
    route_row = row_ref[s.folds : s.folds + 1, : s.tok]
    out_ref[...] = tokens_of(packs, route_row, rows_ref, extra_ref, tail_ref, s).astype(BF16)


def backward_sum_kernel(s, *refs):
    parts, outs = refs[: s.blocks], refs[s.blocks :]
    for d in range(s.count - 1, -1, -1):
        total = total_of(parts, d, s.slices)
        outs[d][:, : s.width] = total[:, : s.width].astype(BF16)
        main, extra = get_inner(total[:, s.width :], s)
        outs[d][:, s.width :] = put_inner(main, extra, s)


def backward_end_kernel(s, *refs):
    packs = refs[: s.count]
    dy_ref, route_ref, score_ref, out_ref, grad_ref = refs[s.count : s.count + 5]
    rows_ref, extra_ref, tail_ref = refs[s.count + 5 :]
    route_row = route_ref[...].astype(F32)
    rows = tokens_of(packs, route_row, rows_ref, extra_ref, tail_ref, s)
    gate = as_column(2.5 * score_ref[...])
    out_ref[...] = (dy_ref[...].astype(F32) + gate * rows).astype(BF16)
    rank = slot_rows(route_row, s)
    dgate = jnp.zeros((1, s.tok), F32)
    for d in range(s.count):
        hit = route_row == expert_at(s, d)
        main, extra = get_inner(packs[d][:, s.width :].astype(F32), s)
        dgate += jnp.sum(
            jnp.where(hit & (rank == iota((s.main, s.tok), 0)), main, 0.0), axis=0, keepdims=True
        )
        for j in range(s.extra):
            dgate += jnp.where(hit & (rank == float(s.main + j)), extra[j], 0.0)
    grad_ref[...] = 2.5 * dgate


VMEM = pl.BlockSpec(memory_space=pltpu.VMEM)
HBM = pl.BlockSpec(memory_space=pltpu.HBM)


def call(kernel, name, outs, scratch, ins, *args, mib=16):
    shapes = [jax.ShapeDtypeStruct(shape, kind) for shape, kind in outs]
    args = [
        pltpu.with_memory_space_constraint(a, pltpu.HBM) if spec is HBM else a
        for a, spec in zip(args, ins)
    ]
    return pl.pallas_call(
        kernel,
        out_shape=shapes,
        in_specs=ins,
        out_specs=[VMEM] * len(shapes),
        scratch_shapes=scratch,
        compiler_params=pltpu.CompilerParams(vmem_limit_bytes=mib << 20),
        cost_estimate=pl.CostEstimate(flops=0, bytes_accessed=0, transcendentals=0),
        name=name,
    )(*args)


def tail_scratch(s, rows):
    return [
        pltpu.VMEM((rows, s.depth), F32),
        pltpu.VMEM((s.main, LANES * s.extra), F32),
    ]


def row_scratch(s):
    return [pltpu.VMEM((s.rows, s.depth), BF16), *tail_scratch(s, s.tail_rows)]


def cross(s, packs):
    return [packs[0]] + [across(packs[d], d, s) for d in range(1, s.count)]


def spread(s, got):
    return got + [beside(b, k, s) for k in range(1, s.slices) for b in got]


def hold(values, *after):
    return lax.optimization_barrier((values, after))[0]


def gather_parts(s, parts):
    return [beside(p, -(i // s.count), s) if i >= s.count else p for i, p in enumerate(parts)]


def end_scratch(s):
    low = -(-(s.count * s.extra) // 16) * 16
    return [pltpu.VMEM((s.count * s.main + low, s.depth), BF16), *tail_scratch(s, low)]


def body(
    x_fwd,
    saved_gate,
    saved_up,
    grad_next,
    routes_fwd,
    routes_bwd,
    scores_fwd,
    scores_bwd,
    w_gate,
    w_up,
    w_down,
):
    groups = lax.axis_size("expert")
    tok, depth = x_fwd.shape[1:]
    s = Sizes(saved_gate.shape[2], depth, EXPERTS, groups // EXPERTS, tok)
    hidden = w_gate.shape[2]
    weights = (w_gate[0], w_up[0], w_down[0])
    route_a = routes_fwd.reshape(1, tok)
    route_b = routes_bwd.reshape(1, tok)
    score_a = scores_fwd.reshape(1, tok)
    score_b = scores_bwd.reshape(1, tok)

    packed = [((s.main, s.width), BF16)] * s.count
    *sent_a, grads = call(
        functools.partial(first_kernel, s),
        "first",
        packed + [((tok, depth), BF16)],
        [
            pltpu.VMEM((1, tok), jnp.int32),
            pltpu.VMEM((tok, depth), BF16),
            *tail_scratch(s, 16),
            pltpu.SemaphoreType.DMA((3,)),
        ],
        [HBM] * 3,
        route_a,
        x_fwd[0],
        grad_next[0],
    )
    upstream = from_behind(grads, "section", -1)
    held = (*weights, route_a, route_b, score_a, score_b)
    *weights, route_a, route_b, score_a, score_b = call(
        load_kernel,
        "load",
        [(a.shape, a.dtype) for a in held],
        [pltpu.SemaphoreType.DMA((len(held),))],
        [HBM] * len(held),
        *held,
    )
    factors = call(
        functools.partial(saved_kernel, s),
        "saved",
        [((s.rows, hidden), F32)] * 3,
        [pltpu.VMEM((s.rows, hidden), F32)] * 2,
        [VMEM] * 2,
        saved_gate[0],
        saved_up[0],
    )
    got = cross(s, sent_a)
    got[1:] = hold(got[1:], score_b, factors)
    rows_a = spread(s, got)
    sent_b = call(
        functools.partial(pack_kernel, s),
        "pack",
        packed,
        tail_scratch(s, 16),
        [VMEM] * 2,
        route_b,
        hold(upstream, got[1:]),
    )
    got_b = cross(s, sent_b)

    parts_a = call(
        functools.partial(forward_kernel, s),
        "forward",
        [((s.main, s.width), BF16)] * s.blocks,
        row_scratch(s),
        [VMEM] * (s.blocks + 3),
        *hold(rows_a, sent_b),
        *weights,
    )
    wide = s.width + LANES
    got_b[1:] = hold(got_b[1:], parts_a)
    rows_b = spread(s, got_b)
    parts_a = hold(gather_parts(s, parts_a), got_b[1:])
    sums_a = call(
        functools.partial(forward_sum_kernel, s),
        "forward_sum",
        [((s.main, wide), BF16)] * s.count,
        [],
        [VMEM] * (s.blocks + 3),
        *parts_a,
        sent_a[0],
        route_a,
        score_a,
    )
    back_a = [across(sums_a[d], -d, s) for d in range(1, s.count)]

    parts_b = call(
        functools.partial(backward_kernel, s),
        "backward",
        [((s.main, wide), BF16)] * s.blocks,
        row_scratch(s),
        [VMEM] * (s.blocks + 6),
        *hold(rows_b, sums_a),
        *factors,
        *weights,
    )
    back_a = hold(back_a, parts_b)
    moved = [from_behind(sums_a[0], "section", 1)]
    for d in range(1, s.count):
        y = call(
            functools.partial(forward_add_kernel, s, d),
            "forward_add",
            [((s.main, s.width), BF16)],
            [],
            [VMEM] * 4,
            back_a[d - 1],
            sent_a[d],
            route_a,
            score_a,
        )[0]
        moved.append(from_behind(y, "section", 1))
    sums_b = call(
        functools.partial(backward_sum_kernel, s),
        "backward_sum",
        [((s.main, wide), BF16)] * s.count,
        [],
        [VMEM] * s.blocks,
        *hold(gather_parts(s, parts_b), y),
    )
    back_b = [sums_b[0]] + [across(sums_b[d], -d, s) for d in range(1, s.count)]
    input_grad, score_grad = call(
        functools.partial(backward_end_kernel, s),
        "backward_end",
        [((tok, depth), BF16), ((1, tok), F32)],
        end_scratch(s),
        [VMEM] * (s.count + 3),
        *hold(back_b, moved[0]),
        upstream,
        route_b,
        score_b,
    )
    next_input = call(
        functools.partial(forward_end_kernel, s),
        "forward_end",
        [((tok, depth), BF16)],
        end_scratch(s) + [pltpu.VMEM((s.main, LANES), F32)],
        [VMEM] * s.count,
        *hold(moved, score_grad),
    )[0]
    return next_input[None], input_grad[None], score_grad.reshape(1, tok, 1)


def solution(mesh):
    placed = (
        P("section", "expert", None),
        P("section", None, None, "expert"),
        P("section", None, None, "expert"),
        P("section", "expert", None),
        P("section", "expert", None),
        P("section", "expert", None),
        P("section", "expert", None),
        P("section", "expert", None),
        P("section", None, "expert"),
        P("section", None, "expert"),
        P("section", "expert", None),
    )
    return jax.shard_map(
        body,
        mesh=mesh,
        in_specs=placed,
        out_specs=(
            P("section", "expert", None),
            P("section", "expert", None),
            P("section", "expert", None),
        ),
        check_vma=False,
    )
```

```python
import functools

import jax
import jax.numpy as jnp
from jax import lax
from jax.experimental import pallas as pl
from jax.experimental.pallas import tpu as pltpu
from jax.sharding import PartitionSpec as P

EXPERTS = 2
LANES = 128
HALVES_A = 2
HALVES_B = 1
F32 = jnp.float32
BF16 = jnp.bfloat16
NT = (((1,), (1,)), ((), ()))


class Sizes:
    def __init__(self, cap, depth, count, slices, tok):
        self.cap, self.depth, self.count, self.slices, self.tok = cap, depth, count, slices, tok
        self.main = cap // 16 * 16
        self.extra = cap - self.main
        self.folds = depth // LANES
        assert self.folds < self.main and depth % LANES == 0
        self.width = depth + LANES * self.extra
        self.blocks = count * slices
        self.tail_rows = -(-(self.blocks * self.extra) // 16) * 16
        self.rows = self.blocks * self.main + self.tail_rows


def from_behind(block, axis, distance):
    devices = range(lax.axis_size(axis))
    route = [((i - distance) % len(devices), i) for i in devices]
    return lax.ppermute(block, axis, route)


def across(block, distance, s):
    route = [
        (e * s.slices + j, (e + distance) % s.count * s.slices + j)
        for e in range(s.count)
        for j in range(s.slices)
    ]
    return lax.ppermute(block, "expert", route)


def beside(block, distance, s):
    route = [
        (e * s.slices + j, e * s.slices + (j + distance) % s.slices)
        for e in range(s.count)
        for j in range(s.slices)
    ]
    return lax.ppermute(block, "expert", route)


def iota(shape, dim):
    return lax.broadcasted_iota(jnp.int32, shape, dim).astype(F32)


def as_column(row):
    n = row.shape[1]
    return jnp.sum(
        jnp.where(iota((n, n), 0) == iota((n, n), 1), row, 0.0), axis=1, keepdims=True
    )


def own_expert(s):
    return lax.axis_index("expert") // s.slices


def expert_at(s, distance):
    return ((own_expert(s) + distance) % s.count).astype(F32)


def slot_rows(route_row, s):
    col = as_column(route_row)
    n = s.tok
    same = (col == route_row) & (iota((n, n), 0) < iota((n, n), 1))
    return jnp.sum(jnp.where(same, 1.0, 0.0), axis=0, keepdims=True)


def slot_columns(route_row, s):
    col = as_column(route_row)
    n = s.tok
    same = (col == route_row) & (iota((n, n), 1) < iota((n, n), 0))
    return col, jnp.sum(jnp.where(same, 1.0, 0.0), axis=1, keepdims=True)


def fold(values_ref, first, tail_ref, s):
    for j in range(s.extra):
        for r in range(s.folds):
            tail_ref[r : r + 1, j * LANES : (j + 1) * LANES] = values_ref[
                first + j : first + j + 1, r * LANES : (r + 1) * LANES
            ]


def unfold(tail_ref, values_ref, first, s):
    for j in range(s.extra):
        for r in range(s.folds):
            values_ref[first + j : first + j + 1, r * LANES : (r + 1) * LANES] = tail_ref[
                r : r + 1, j * LANES : (j + 1) * LANES
            ]


def slot_values(route_row, value_row, expert, s):
    rank = slot_rows(route_row, s)
    hit = route_row == expert
    main = jnp.sum(
        jnp.where(hit & (rank == iota((s.main, s.tok), 0)), value_row, 0.0), axis=1, keepdims=True
    )
    extra = [
        jnp.sum(jnp.where(hit & (rank == float(s.main + j)), value_row, 0.0), axis=1, keepdims=True)
        for j in range(s.extra)
    ]
    return main, extra


def add_gated(out_ref, base_ref, main, extra, total, s):
    d = s.depth
    out_ref[:, :d] = (base_ref[:, :d].astype(F32) + main * total[:, :d]).astype(BF16)
    for j in range(s.extra):
        at = slice(d + j * LANES, d + (j + 1) * LANES)
        out_ref[:, at] = (base_ref[:, at].astype(F32) + extra[j] * total[:, at]).astype(BF16)


def pack_rows(s, route_row, x, outs, extra_ref, tail_ref):
    rank = slot_rows(route_row, s)
    slots = iota((s.main + 16, s.tok), 0)
    tail_ref[...] = jnp.zeros_like(tail_ref)
    for d in range(s.count):
        hit = route_row == expert_at(s, d)
        table = jnp.where(hit & (rank == slots), 1.0, 0.0).astype(BF16)
        rows = jnp.dot(table, x, preferred_element_type=F32)
        outs[d][:, : s.depth] = rows[: s.main].astype(BF16)
        extra_ref[...] = rows[s.main :]
        fold(extra_ref, 0, tail_ref, s)
        outs[d][:, s.depth :] = tail_ref[...].astype(BF16)


def first_kernel(s, route_hbm, x_hbm, *rest):
    outs, (route_ref, x_ref, extra_ref, tail_ref, sems) = rest[: s.count], rest[s.count :]
    copies = [
        pltpu.make_async_copy(route_hbm, route_ref, sems.at[0]),
        pltpu.make_async_copy(x_hbm, x_ref, sems.at[1]),
    ]
    for copy in copies:
        copy.start()
    for copy in copies:
        copy.wait()
    pack_rows(s, route_ref[...].astype(F32), x_ref[...], outs, extra_ref, tail_ref)


def pack_kernel(s, route_ref, x_ref, *rest):
    outs, (extra_ref, tail_ref) = rest[: s.count], rest[s.count :]
    pack_rows(s, route_ref[...].astype(F32), x_ref[...], outs, extra_ref, tail_ref)


def load_kernel(*refs):
    sems = refs[-1]
    n = (len(refs) - 1) // 2
    copies = [pltpu.make_async_copy(refs[i], refs[n + i], sems.at[i]) for i in range(n)]
    for copy in copies:
        copy.start()
    for copy in copies:
        copy.wait()


def gather_packs(packs, rows_ref, extra_ref, tail_ref, s):
    extra_ref[...] = jnp.zeros_like(extra_ref)
    for i, pack in enumerate(packs):
        rows_ref[i * s.main : (i + 1) * s.main, :] = pack[:, : s.depth]
        tail_ref[...] = pack[:, s.depth : s.width].astype(F32)
        unfold(tail_ref, extra_ref, i * s.extra, s)
    rows_ref[s.blocks * s.main :, :] = extra_ref[...].astype(BF16)


def put(outs, i, at, value, s):
    if i < s.count:
        outs[i][:, at] = value
        return
    n = (len(outs) - s.count) // (s.blocks - s.count)
    rows = s.main // n
    for h in range(n):
        outs[s.count + (i - s.count) * n + h][:, at] = value[h * rows : (h + 1) * rows]


def scatter_chunk(value, outs, extra_ref, at, s):
    for i in range(s.blocks):
        put(outs, i, at, value[i * s.main : (i + 1) * s.main].astype(BF16), s)
    extra_ref[:, at] = value[s.blocks * s.main :]


def scatter_tails(outs, extra_ref, tail_ref, s):
    for i in range(s.blocks):
        fold(extra_ref, i * s.extra, tail_ref, s)
        put(outs, i, slice(s.depth, s.width), tail_ref[...].astype(BF16), s)


def chunk_of(depth):
    for chunk in (512, 256, 128):
        if depth % chunk == 0:
            return chunk


def forward_kernel(s, *refs):
    packs = refs[: s.blocks]
    wg, wu, wd = refs[s.blocks : s.blocks + 3]
    outs = refs[s.blocks + 3 : -3]
    rows_ref, extra_ref, tail_ref = refs[-3:]
    chunk = chunk_of(s.depth)
    gather_packs(packs, rows_ref, extra_ref, tail_ref, s)
    g = u = None
    for c in range(0, s.depth, chunk):
        lhs = rows_ref[:, c : c + chunk]
        more_g = jnp.dot(lhs, wg[c : c + chunk, :], preferred_element_type=F32)
        more_u = jnp.dot(lhs, wu[c : c + chunk, :], preferred_element_type=F32)
        g = more_g if g is None else g + more_g
        u = more_u if u is None else u + more_u
    hidden = (g * jax.nn.sigmoid(g) * u).astype(BF16)
    tail_ref[...] = jnp.zeros_like(tail_ref)
    for c in range(0, s.depth, chunk):
        part = jnp.dot(hidden, wd[:, c : c + chunk], preferred_element_type=F32)
        scatter_chunk(part, outs, extra_ref, slice(c, c + chunk), s)
    scatter_tails(outs, extra_ref, tail_ref, s)


def saved_kernel(s, gate_ref, up_ref, c1_ref, c2_ref, hb_ref, g_ref, u_ref):
    me = lax.axis_index("expert")
    e, j = me // s.slices, me % s.slices
    g_ref[...] = jnp.zeros_like(g_ref)
    u_ref[...] = jnp.zeros_like(u_ref)
    for i in range(s.blocks):
        k, d = i // s.count, i % s.count
        source = (e + s.count - d) % s.count * s.slices + (j + s.slices - k) % s.slices
        for src, dst in ((gate_ref, g_ref), (up_ref, u_ref)):
            rows = src[source].astype(F32)
            dst[i * s.main : (i + 1) * s.main, :] = rows[: s.main]
            first = s.blocks * s.main + i * s.extra
            dst[first : first + s.extra, :] = rows[s.main :]
    g = g_ref[...]
    u = u_ref[...]
    sig = jax.nn.sigmoid(g)
    c1_ref[...] = u * sig * (1.0 + g * (1.0 - sig))
    c2_ref[...] = g * sig
    hb_ref[...] = (g * sig * u).astype(BF16).astype(F32)


def split_three(value):
    high = value.astype(BF16).astype(F32)
    rest = value - high
    mid = rest.astype(BF16).astype(F32)
    return high, mid, (rest - mid).astype(BF16).astype(F32)


def put_inner(main, extra, s):
    lane = iota((s.main, LANES), 1)
    row = iota((s.main, LANES), 0)
    out = jnp.zeros((s.main, LANES), F32)
    for p, piece in enumerate(split_three(main)):
        out = jnp.where(lane == float(p), piece, out)
    for j in range(s.extra):
        for p, piece in enumerate(split_three(extra[j])):
            out = jnp.where((lane == float(3 + p)) & (row == float(j)), piece, out)
    return out.astype(BF16)


def get_inner(block, s):
    lane = iota((s.main, LANES), 1)
    row = iota((s.main, LANES), 0)
    main = jnp.sum(jnp.where(lane < 3.0, block, 0.0), axis=1, keepdims=True)
    second = jnp.sum(
        jnp.where((lane >= 3.0) & (lane < 6.0), block, 0.0), axis=1, keepdims=True
    )
    extra = [
        jnp.sum(jnp.where(row[:, :1] == float(j), second, 0.0), axis=0, keepdims=True)
        for j in range(s.extra)
    ]
    return main, extra


def backward_kernel(s, *refs):
    packs = refs[: s.blocks]
    c1, c2, hb, wg, wu, wd = refs[s.blocks : s.blocks + 6]
    outs = refs[s.blocks + 6 : -3]
    rows_ref, extra_ref, tail_ref = refs[-3:]
    chunk = chunk_of(s.depth)
    gather_packs(packs, rows_ref, extra_ref, tail_ref, s)
    a = None
    for c in range(0, s.depth, chunk):
        more = lax.dot_general(
            rows_ref[:, c : c + chunk], wd[:, c : c + chunk], NT, preferred_element_type=F32
        )
        a = more if a is None else a + more
    dgp = (a * c1[...]).astype(BF16)
    dup = (a * c2[...]).astype(BF16)
    inner = jnp.sum(a * hb[...], axis=1, keepdims=True)
    for i in range(s.blocks):
        first = s.blocks * s.main + i * s.extra
        pieces = put_inner(
            inner[i * s.main : (i + 1) * s.main],
            [inner[first + j : first + j + 1] for j in range(s.extra)],
            s,
        )
        put(outs, i, slice(s.width, s.width + LANES), pieces, s)
    tail_ref[...] = jnp.zeros_like(tail_ref)
    for c in range(0, s.depth, chunk):
        part = lax.dot_general(
            dgp, wg[c : c + chunk, :], NT, preferred_element_type=F32
        ) + lax.dot_general(dup, wu[c : c + chunk, :], NT, preferred_element_type=F32)
        scatter_chunk(part, outs, extra_ref, slice(c, c + chunk), s)
    scatter_tails(outs, extra_ref, tail_ref, s)


def total_of(parts, d, s):
    total = parts[d][...].astype(F32)
    n = (len(parts) - s.count) // (s.blocks - s.count)
    for i in range(s.count + d, s.blocks, s.count):
        first = s.count + (i - s.count) * n
        halves = [part[...].astype(F32) for part in parts[first : first + n]]
        total = total + jnp.concatenate(halves, axis=0)
    return total


def forward_sum_kernel(s, *refs):
    n = len(refs) - 3 - s.count
    parts = refs[:n]
    own, route_ref, score_ref, y_ref = refs[n : n + 4]
    backs = refs[n + 4 :]
    for d in range(1, s.count):
        backs[d - 1][:, : s.width] = total_of(parts, d, s).astype(BF16)
        backs[d - 1][:, s.width :] = jnp.zeros((s.main, LANES), BF16)
    route_row = route_ref[...].astype(F32)
    main, extra = slot_values(route_row, 2.5 * score_ref[...], expert_at(s, 0), s)
    add_gated(y_ref, own, main, extra, total_of(parts, 0, s), s)
    y_ref[s.folds : s.folds + 1, s.depth : s.depth + s.tok] = route_row.astype(BF16)
    y_ref[:, s.width :] = jnp.zeros((s.main, LANES), BF16)


def forward_add_kernel(s, distance, back, base, route_ref, score_ref, y_ref):
    route_row = route_ref[...].astype(F32)
    main, extra = slot_values(route_row, 2.5 * score_ref[...], expert_at(s, distance), s)
    add_gated(y_ref, base, main, extra, back[:, : s.width].astype(F32), s)
    y_ref[:, s.width :] = jnp.zeros((s.main, LANES), BF16)


def tokens_of(packs, route_row, rows_ref, extra_ref, tail_ref, s):
    extra_ref[...] = jnp.zeros_like(extra_ref)
    for d, pack in enumerate(packs):
        rows_ref[d * s.main : (d + 1) * s.main, :] = pack[:, : s.depth]
        tail_ref[...] = pack[:, s.depth : s.width].astype(F32)
        unfold(tail_ref, extra_ref, d * s.extra, s)
    rows_ref[s.count * s.main :, :] = extra_ref[...].astype(BF16)
    col, rank = slot_columns(route_row, s)
    high = rows_ref.shape[0]
    place = jnp.full((s.tok, 1), -1.0, F32)
    for d in range(s.count):
        at = jnp.where(
            rank < float(s.main),
            rank + float(d * s.main),
            rank + float(s.count * s.main + d * s.extra - s.main),
        )
        place = jnp.where(col == expert_at(s, d), at, place)
    table = jnp.where(place == iota((s.tok, high), 1), 1.0, 0.0).astype(BF16)
    return jnp.dot(table, rows_ref[...], preferred_element_type=F32)


def forward_end_kernel(s, *refs):
    packs = refs[: s.count]
    out_ref, rows_ref, extra_ref, tail_ref, row_ref = refs[s.count :]
    row_ref[...] = packs[0][:, s.depth : s.depth + LANES].astype(F32)
    route_row = row_ref[s.folds : s.folds + 1, : s.tok]
    out_ref[...] = tokens_of(packs, route_row, rows_ref, extra_ref, tail_ref, s).astype(BF16)


def backward_sum_kernel(s, *refs):
    parts, outs = refs[: -s.count], refs[-s.count :]
    for d in range(s.count - 1, -1, -1):
        total = total_of(parts, d, s)
        outs[d][:, : s.width] = total[:, : s.width].astype(BF16)
        main, extra = get_inner(total[:, s.width :], s)
        outs[d][:, s.width :] = put_inner(main, extra, s)


def backward_end_kernel(s, *refs):
    packs = refs[: s.count]
    dy_ref, route_ref, score_ref, out_ref, grad_ref = refs[s.count : s.count + 5]
    rows_ref, extra_ref, tail_ref = refs[s.count + 5 :]
    route_row = route_ref[...].astype(F32)
    rows = tokens_of(packs, route_row, rows_ref, extra_ref, tail_ref, s)
    gate = as_column(2.5 * score_ref[...])
    out_ref[...] = (dy_ref[...].astype(F32) + gate * rows).astype(BF16)
    rank = slot_rows(route_row, s)
    dgate = jnp.zeros((1, s.tok), F32)
    for d in range(s.count):
        hit = route_row == expert_at(s, d)
        main, extra = get_inner(packs[d][:, s.width :].astype(F32), s)
        dgate += jnp.sum(
            jnp.where(hit & (rank == iota((s.main, s.tok), 0)), main, 0.0), axis=0, keepdims=True
        )
        for j in range(s.extra):
            dgate += jnp.where(hit & (rank == float(s.main + j)), extra[j], 0.0)
    grad_ref[...] = 2.5 * dgate


VMEM = pl.BlockSpec(memory_space=pltpu.VMEM)
HBM = pl.BlockSpec(memory_space=pltpu.HBM)


def call(kernel, name, outs, scratch, ins, *args, mib=16):
    shapes = [jax.ShapeDtypeStruct(shape, kind) for shape, kind in outs]
    args = [
        pltpu.with_memory_space_constraint(a, pltpu.HBM) if spec is HBM else a
        for a, spec in zip(args, ins)
    ]
    return pl.pallas_call(
        kernel,
        out_shape=shapes,
        in_specs=ins,
        out_specs=[VMEM] * len(shapes),
        scratch_shapes=scratch,
        compiler_params=pltpu.CompilerParams(vmem_limit_bytes=mib << 20),
        cost_estimate=pl.CostEstimate(flops=0, bytes_accessed=0, transcendentals=0),
        name=name,
    )(*args)


def tail_scratch(s, rows):
    return [
        pltpu.VMEM((rows, s.depth), F32),
        pltpu.VMEM((s.main, LANES * s.extra), F32),
    ]


def load(*arrays):
    return call(
        load_kernel,
        "load",
        [(a.shape, a.dtype) for a in arrays],
        [pltpu.SemaphoreType.DMA((len(arrays),))],
        [HBM] * len(arrays),
        *arrays,
    )


def row_scratch(s):
    return [pltpu.VMEM((s.rows, s.depth), BF16), *tail_scratch(s, s.tail_rows)]


def cross(s, packs):
    return [packs[0]] + [across(packs[d], d, s) for d in range(1, s.count)]


def spread(s, got):
    return list(got) + [beside(b, k, s) for k in range(1, s.slices) for b in got]


def hold(values, *after):
    return lax.optimization_barrier((values, after))[0]


def parts_shape(s, width, halves):
    kept = [((s.main, width), BF16)] * s.count
    return kept + [((s.main // halves, width), BF16)] * ((s.blocks - s.count) * halves)


def gather_parts(s, parts):
    n = (len(parts) - s.count) // (s.blocks - s.count)
    moved = [beside(p, -(i // n // s.count + 1), s) for i, p in enumerate(parts[s.count :])]
    return list(parts[: s.count]) + moved


def end_scratch(s):
    low = -(-(s.count * s.extra) // 16) * 16
    return [pltpu.VMEM((s.count * s.main + low, s.depth), BF16), *tail_scratch(s, low)]


def body(
    x_fwd,
    saved_gate,
    saved_up,
    grad_next,
    routes_fwd,
    routes_bwd,
    scores_fwd,
    scores_bwd,
    w_gate,
    w_up,
    w_down,
):
    groups = lax.axis_size("expert")
    tok, depth = x_fwd.shape[1:]
    s = Sizes(saved_gate.shape[2], depth, EXPERTS, groups // EXPERTS, tok)
    hidden = w_gate.shape[2]
    route_a = routes_fwd.reshape(1, tok)
    route_b = routes_bwd.reshape(1, tok)
    score_a = scores_fwd.reshape(1, tok)
    score_b = scores_bwd.reshape(1, tok)

    packed = [((s.main, s.width), BF16)] * s.count
    sent_a = call(
        functools.partial(first_kernel, s),
        "first",
        packed,
        [
            pltpu.VMEM((1, tok), jnp.int32),
            pltpu.VMEM((tok, depth), BF16),
            *tail_scratch(s, 16),
            pltpu.SemaphoreType.DMA((2,)),
        ],
        [HBM] * 2,
        route_a,
        x_fwd[0],
    )
    upstream = from_behind(grad_next, "section", -1)[0]
    wg, wu, route_a, score_a = load(w_gate[0], w_up[0], route_a, score_a)
    got = cross(s, sent_a)
    got[1:] = hold(got[1:], score_a)
    wd, route_b, score_b = load(hold(w_down[0], got[1:]), route_b, score_b)
    parts_a = call(
        functools.partial(forward_kernel, s),
        "forward",
        parts_shape(s, s.width, HALVES_A),
        row_scratch(s),
        [VMEM] * (s.blocks + 3),
        *spread(s, got),
        wg,
        wu,
        wd,
    )
    wide = s.width + LANES
    sums_a = call(
        functools.partial(forward_sum_kernel, s),
        "forward_sum",
        [((s.main, wide), BF16)] * s.count,
        [],
        [VMEM] * (len(parts_a) + 3),
        *gather_parts(s, parts_a),
        sent_a[0],
        route_a,
        score_a,
    )
    back_a = [across(sums_a[d], -d, s) for d in range(1, s.count)]
    moved = [from_behind(sums_a[0], "section", 1)]
    sent_b = call(
        functools.partial(pack_kernel, s),
        "pack",
        packed,
        tail_scratch(s, 16),
        [VMEM] * 2,
        route_b,
        hold(upstream, sums_a),
    )
    got_b = cross(s, sent_b)
    factors = call(
        functools.partial(saved_kernel, s),
        "saved",
        [((s.rows, hidden), F32)] * 3,
        [pltpu.VMEM((s.rows, hidden), F32)] * 2,
        [VMEM] * 2,
        *hold((saved_gate[0], saved_up[0]), sent_b),
    )
    back_a = hold(back_a, factors)
    for d in range(1, s.count):
        y = call(
            functools.partial(forward_add_kernel, s, d),
            "forward_add",
            [((s.main, wide), BF16)],
            [],
            [VMEM] * 4,
            back_a[d - 1],
            sent_a[d],
            route_a,
            score_a,
        )[0]
        moved.append(from_behind(y, "section", 1))
    got_b[1:] = hold(got_b[1:], y)
    def middle(got_b, factors, weights):
        parts_b = call(
            functools.partial(backward_kernel, s),
            "backward",
            parts_shape(s, wide, HALVES_B),
            row_scratch(s),
            [VMEM] * (s.blocks + 6),
            *spread(s, got_b),
            *factors,
                *weights,
        )
        sums_b = call(
            functools.partial(backward_sum_kernel, s),
            "backward_sum",
            [((s.main, wide), BF16)] * s.count,
            [],
            [VMEM] * len(parts_b),
            *gather_parts(s, parts_b),
        )
        return tuple(sums_b)

    sums_b = lax.cond(
        route_b[0, 0] < s.count,
        middle,
        lambda got_b, factors, weights: tuple(sums_a),
        tuple(got_b),
        tuple(factors),
        (wg, wu, wd),
    )
    back_b = [sums_b[0]] + [across(sums_b[d], -d, s) for d in range(1, s.count)]
    next_input = call(
        functools.partial(forward_end_kernel, s),
        "forward_end",
        [((tok, depth), BF16)],
        end_scratch(s) + [pltpu.VMEM((s.main, LANES), F32)],
        [VMEM] * s.count,
        *moved,
    )[0]
    input_grad, score_grad = call(
        functools.partial(backward_end_kernel, s),
        "backward_end",
        [((tok, depth), BF16), ((1, tok), F32)],
        end_scratch(s),
        [VMEM] * (s.count + 3),
        *hold(back_b, next_input),
        upstream,
        route_b,
        score_b,
    )
    return next_input[None], input_grad[None], score_grad.reshape(1, tok, 1)


def solution(mesh):
    placed = (
        P("section", "expert", None),
        P("section", None, None, "expert"),
        P("section", None, None, "expert"),
        P("section", "expert", None),
        P("section", "expert", None),
        P("section", "expert", None),
        P("section", "expert", None),
        P("section", "expert", None),
        P("section", None, "expert"),
        P("section", None, "expert"),
        P("section", "expert", None),
    )
    return jax.shard_map(
        body,
        mesh=mesh,
        in_specs=placed,
        out_specs=(
            P("section", "expert", None),
            P("section", "expert", None),
            P("section", "expert", None),
        ),
        check_vma=False,
    )
```

```python
import functools

import jax
import jax.numpy as jnp
from jax import lax
from jax.experimental import pallas as pl
from jax.experimental.pallas import tpu as pltpu
from jax.sharding import PartitionSpec as P

EXPERTS = 2
LANES = 128
PIECES = 2
F32 = jnp.float32
BF16 = jnp.bfloat16
NT = (((1,), (1,)), ((), ()))


class Sizes:
    def __init__(self, cap, depth, count, slices, tok):
        self.cap, self.depth, self.count, self.slices, self.tok = cap, depth, count, slices, tok
        self.main = cap // 16 * 16
        self.extra = cap - self.main
        self.folds = depth // LANES
        assert self.folds < self.main and depth % LANES == 0
        self.width = depth + LANES * self.extra
        self.blocks = count * slices
        self.tail_rows = -(-(self.blocks * self.extra) // 16) * 16
        self.rows = self.blocks * self.main + self.tail_rows


def from_behind(block, axis, distance):
    devices = range(lax.axis_size(axis))
    route = [((i - distance) % len(devices), i) for i in devices]
    return lax.ppermute(block, axis, route)


def across(block, distance, s):
    route = [
        (e * s.slices + j, (e + distance) % s.count * s.slices + j)
        for e in range(s.count)
        for j in range(s.slices)
    ]
    return lax.ppermute(block, "expert", route)


def beside(block, distance, s):
    route = [
        (e * s.slices + j, e * s.slices + (j + distance) % s.slices)
        for e in range(s.count)
        for j in range(s.slices)
    ]
    return lax.ppermute(block, "expert", route)


def iota(shape, dim):
    return lax.broadcasted_iota(jnp.int32, shape, dim).astype(F32)


def as_column(row):
    n = row.shape[1]
    return jnp.sum(
        jnp.where(iota((n, n), 0) == iota((n, n), 1), row, 0.0), axis=1, keepdims=True
    )


def own_expert(s):
    return lax.axis_index("expert") // s.slices


def expert_at(s, distance):
    return ((own_expert(s) + distance) % s.count).astype(F32)


def slot_rows(route_row, s):
    col = as_column(route_row)
    n = s.tok
    same = (col == route_row) & (iota((n, n), 0) < iota((n, n), 1))
    return jnp.sum(jnp.where(same, 1.0, 0.0), axis=0, keepdims=True)


def slot_columns(route_row, s):
    col = as_column(route_row)
    n = s.tok
    same = (col == route_row) & (iota((n, n), 1) < iota((n, n), 0))
    return col, jnp.sum(jnp.where(same, 1.0, 0.0), axis=1, keepdims=True)


def fold(values_ref, first, tail_ref, s):
    for j in range(s.extra):
        for r in range(s.folds):
            tail_ref[r : r + 1, j * LANES : (j + 1) * LANES] = values_ref[
                first + j : first + j + 1, r * LANES : (r + 1) * LANES
            ]


def unfold(tail_ref, values_ref, first, s):
    for j in range(s.extra):
        for r in range(s.folds):
            values_ref[first + j : first + j + 1, r * LANES : (r + 1) * LANES] = tail_ref[
                r : r + 1, j * LANES : (j + 1) * LANES
            ]


def slot_values(route_row, value_row, expert, s):
    rank = slot_rows(route_row, s)
    hit = route_row == expert
    main = jnp.sum(
        jnp.where(hit & (rank == iota((s.main, s.tok), 0)), value_row, 0.0), axis=1, keepdims=True
    )
    extra = [
        jnp.sum(jnp.where(hit & (rank == float(s.main + j)), value_row, 0.0), axis=1, keepdims=True)
        for j in range(s.extra)
    ]
    return main, extra


def add_gated(out_ref, base, main, extra, total, s):
    d = s.depth
    out_ref[:, :d] = (read(base, 0, d).astype(F32) + main * total[:, :d]).astype(BF16)
    for j in range(s.extra):
        at = slice(d + j * LANES, d + (j + 1) * LANES)
        value = read(base, at.start, at.stop).astype(F32) + extra[j] * total[:, at]
        out_ref[:, at] = value.astype(BF16)


def read(pieces, low, high):
    found, at = [], 0
    for piece in pieces:
        width = piece.shape[1]
        a, b = max(low, at), min(high, at + width)
        if a < b:
            found.append(piece[:, a - at : b - at])
        at += width
    return found[0] if len(found) == 1 else jnp.concatenate(found, axis=1)


def write(pieces, low, value):
    at = 0
    for piece in pieces:
        width = piece.shape[1]
        a, b = max(low, at), min(low + value.shape[1], at + width)
        if a < b:
            piece[:, a - at : b - at] = value[:, a - low : b - low]
        at += width


def grouped(refs, s, pieces):
    one = 1 + (s.count - 1) * pieces
    packs = []
    for first in range(0, len(refs), one):
        packs.append(refs[first : first + 1])
        for at in range(first + 1, first + one, pieces):
            packs.append(refs[at : at + pieces])
    return packs


def pack_rows(s, route_row, x, outs, extra_ref, tail_ref):
    rank = slot_rows(route_row, s)
    slots = iota((s.main + 16, s.tok), 0)
    tail_ref[...] = jnp.zeros_like(tail_ref)
    for d in range(s.count):
        hit = route_row == expert_at(s, d)
        table = jnp.where(hit & (rank == slots), 1.0, 0.0).astype(BF16)
        rows = jnp.dot(table, x, preferred_element_type=F32)
        write(outs[d], 0, rows[: s.main].astype(BF16))
        extra_ref[...] = rows[s.main :]
        fold(extra_ref, 0, tail_ref, s)
        write(outs[d], s.depth, tail_ref[...].astype(BF16))


def first_kernel(s, route_hbm, x_hbm, *rest):
    outs = grouped(rest[:-5], s, PIECES)
    route_ref, x_ref, extra_ref, tail_ref, sems = rest[-5:]
    copies = [
        pltpu.make_async_copy(route_hbm, route_ref, sems.at[0]),
        pltpu.make_async_copy(x_hbm, x_ref, sems.at[1]),
    ]
    for copy in copies:
        copy.start()
    for copy in copies:
        copy.wait()
    pack_rows(s, route_ref[...].astype(F32), x_ref[...], outs, extra_ref, tail_ref)


def pack_kernel(s, route_ref, x_ref, *rest):
    outs, (extra_ref, tail_ref) = grouped(rest[:-2], s, 1), rest[-2:]
    pack_rows(s, route_ref[...].astype(F32), x_ref[...], outs, extra_ref, tail_ref)


def load_kernel(*refs):
    sems = refs[-1]
    n = (len(refs) - 1) // 2
    copies = [pltpu.make_async_copy(refs[i], refs[n + i], sems.at[i]) for i in range(n)]
    for copy in copies:
        copy.start()
    for copy in copies:
        copy.wait()


def gather_packs(packs, rows_ref, extra_ref, tail_ref, s):
    extra_ref[...] = jnp.zeros_like(extra_ref)
    for i, pack in enumerate(packs):
        rows_ref[i * s.main : (i + 1) * s.main, :] = read(pack, 0, s.depth)
        tail_ref[...] = read(pack, s.depth, s.width).astype(F32)
        unfold(tail_ref, extra_ref, i * s.extra, s)
    rows_ref[s.blocks * s.main :, :] = extra_ref[...].astype(BF16)


def scatter_chunk(value, outs, extra_ref, at, s):
    for i in range(s.blocks):
        outs[i][:, at] = value[i * s.main : (i + 1) * s.main].astype(BF16)
    extra_ref[:, at] = value[s.blocks * s.main :]


def scatter_tails(outs, extra_ref, tail_ref, s):
    for i in range(s.blocks):
        fold(extra_ref, i * s.extra, tail_ref, s)
        outs[i][:, s.depth : s.width] = tail_ref[...].astype(BF16)


def chunk_of(depth):
    for chunk in (512, 256, 128):
        if depth % chunk == 0:
            return chunk


def forward_kernel(s, *refs):
    n = len(refs) - s.blocks - 6
    packs = grouped(refs[:n], s, PIECES)
    wg, wu, wd = refs[n : n + 3]
    outs = refs[n + 3 : -3]
    rows_ref, extra_ref, tail_ref = refs[-3:]
    chunk = chunk_of(s.depth)
    gather_packs(packs, rows_ref, extra_ref, tail_ref, s)
    g = u = None
    for c in range(0, s.depth, chunk):
        lhs = rows_ref[:, c : c + chunk]
        more_g = jnp.dot(lhs, wg[c : c + chunk, :], preferred_element_type=F32)
        more_u = jnp.dot(lhs, wu[c : c + chunk, :], preferred_element_type=F32)
        g = more_g if g is None else g + more_g
        u = more_u if u is None else u + more_u
    hidden = (g * jax.nn.sigmoid(g) * u).astype(BF16)
    tail_ref[...] = jnp.zeros_like(tail_ref)
    for c in range(0, s.depth, chunk):
        part = jnp.dot(hidden, wd[:, c : c + chunk], preferred_element_type=F32)
        scatter_chunk(part, outs, extra_ref, slice(c, c + chunk), s)
    scatter_tails(outs, extra_ref, tail_ref, s)


def saved_kernel(s, gate_ref, up_ref, c1_ref, c2_ref, hb_ref, g_ref, u_ref):
    me = lax.axis_index("expert")
    e, j = me // s.slices, me % s.slices
    g_ref[...] = jnp.zeros_like(g_ref)
    u_ref[...] = jnp.zeros_like(u_ref)
    for i in range(s.blocks):
        k, d = i // s.count, i % s.count
        source = (e + s.count - d) % s.count * s.slices + (j + s.slices - k) % s.slices
        for src, dst in ((gate_ref, g_ref), (up_ref, u_ref)):
            rows = src[source].astype(F32)
            dst[i * s.main : (i + 1) * s.main, :] = rows[: s.main]
            first = s.blocks * s.main + i * s.extra
            dst[first : first + s.extra, :] = rows[s.main :]
    g = g_ref[...]
    u = u_ref[...]
    sig = jax.nn.sigmoid(g)
    c1_ref[...] = u * sig * (1.0 + g * (1.0 - sig))
    c2_ref[...] = g * sig
    hb_ref[...] = (g * sig * u).astype(BF16).astype(F32)


def split_three(value):
    high = value.astype(BF16).astype(F32)
    rest = value - high
    mid = rest.astype(BF16).astype(F32)
    return high, mid, (rest - mid).astype(BF16).astype(F32)


def put_inner(main, extra, s):
    lane = iota((s.main, LANES), 1)
    row = iota((s.main, LANES), 0)
    out = jnp.zeros((s.main, LANES), F32)
    for p, piece in enumerate(split_three(main)):
        out = jnp.where(lane == float(p), piece, out)
    for j in range(s.extra):
        for p, piece in enumerate(split_three(extra[j])):
            out = jnp.where((lane == float(3 + p)) & (row == float(j)), piece, out)
    return out.astype(BF16)


def get_inner(block, s):
    lane = iota((s.main, LANES), 1)
    row = iota((s.main, LANES), 0)
    main = jnp.sum(jnp.where(lane < 3.0, block, 0.0), axis=1, keepdims=True)
    second = jnp.sum(
        jnp.where((lane >= 3.0) & (lane < 6.0), block, 0.0), axis=1, keepdims=True
    )
    extra = [
        jnp.sum(jnp.where(row[:, :1] == float(j), second, 0.0), axis=0, keepdims=True)
        for j in range(s.extra)
    ]
    return main, extra


def backward_kernel(s, *refs):
    packs = grouped(refs[: s.blocks], s, 1)
    c1, c2, hb, wg, wu, wd = refs[s.blocks : s.blocks + 6]
    outs = refs[s.blocks + 6 : -3]
    rows_ref, extra_ref, tail_ref = refs[-3:]
    chunk = chunk_of(s.depth)
    gather_packs(packs, rows_ref, extra_ref, tail_ref, s)
    a = None
    for c in range(0, s.depth, chunk):
        more = lax.dot_general(
            rows_ref[:, c : c + chunk], wd[:, c : c + chunk], NT, preferred_element_type=F32
        )
        a = more if a is None else a + more
    dgp = (a * c1[...]).astype(BF16)
    dup = (a * c2[...]).astype(BF16)
    inner = jnp.sum(a * hb[...], axis=1, keepdims=True)
    for i in range(s.blocks):
        first = s.blocks * s.main + i * s.extra
        outs[i][:, s.width :] = put_inner(
            inner[i * s.main : (i + 1) * s.main],
            [inner[first + j : first + j + 1] for j in range(s.extra)],
            s,
        )
    tail_ref[...] = jnp.zeros_like(tail_ref)
    for c in range(0, s.depth, chunk):
        part = lax.dot_general(
            dgp, wg[c : c + chunk, :], NT, preferred_element_type=F32
        ) + lax.dot_general(dup, wu[c : c + chunk, :], NT, preferred_element_type=F32)
        scatter_chunk(part, outs, extra_ref, slice(c, c + chunk), s)
    scatter_tails(outs, extra_ref, tail_ref, s)


def total_of(parts, d, s):
    total = parts[d][...].astype(F32)
    for part in parts[s.count + d :: s.count]:
        total = total + part[...].astype(F32)
    return total


def forward_sum_kernel(s, *refs):
    n = len(refs) - 3 - s.count
    parts = refs[:n]
    own, route_ref, score_ref, y_ref = refs[n : n + 4]
    backs = refs[n + 4 :]
    for d in range(1, s.count):
        backs[d - 1][...] = total_of(parts, d, s).astype(BF16)
    route_row = route_ref[...].astype(F32)
    main, extra = slot_values(route_row, 2.5 * score_ref[...], expert_at(s, 0), s)
    add_gated(y_ref, [own], main, extra, total_of(parts, 0, s), s)
    y_ref[s.folds : s.folds + 1, s.depth : s.depth + s.tok] = route_row.astype(BF16)
    y_ref[:, s.width :] = jnp.zeros((s.main, 2 * LANES), BF16)


def forward_add_kernel(s, distance, back, *rest):
    base, (route_ref, score_ref, y_ref) = rest[:-3], rest[-3:]
    route_row = route_ref[...].astype(F32)
    main, extra = slot_values(route_row, 2.5 * score_ref[...], expert_at(s, distance), s)
    add_gated(y_ref, base, main, extra, back[...].astype(F32), s)
    y_ref[:, s.width :] = jnp.zeros((s.main, LANES), BF16)


def tokens_of(packs, route_row, rows_ref, extra_ref, tail_ref, s):
    extra_ref[...] = jnp.zeros_like(extra_ref)
    for d, pack in enumerate(packs):
        rows_ref[d * s.main : (d + 1) * s.main, :] = pack[:, : s.depth]
        tail_ref[...] = pack[:, s.depth : s.width].astype(F32)
        unfold(tail_ref, extra_ref, d * s.extra, s)
    rows_ref[s.count * s.main :, :] = extra_ref[...].astype(BF16)
    col, rank = slot_columns(route_row, s)
    high = rows_ref.shape[0]
    place = jnp.full((s.tok, 1), -1.0, F32)
    for d in range(s.count):
        at = jnp.where(
            rank < float(s.main),
            rank + float(d * s.main),
            rank + float(s.count * s.main + d * s.extra - s.main),
        )
        place = jnp.where(col == expert_at(s, d), at, place)
    table = jnp.where(place == iota((s.tok, high), 1), 1.0, 0.0).astype(BF16)
    return jnp.dot(table, rows_ref[...], preferred_element_type=F32)


def forward_end_kernel(s, *refs):
    packs = refs[: s.count]
    out_ref, rows_ref, extra_ref, tail_ref, row_ref = refs[s.count :]
    row_ref[...] = packs[0][:, s.depth : s.depth + LANES].astype(F32)
    route_row = row_ref[s.folds : s.folds + 1, : s.tok]
    out_ref[...] = tokens_of(packs, route_row, rows_ref, extra_ref, tail_ref, s).astype(BF16)


def backward_sum_kernel(s, *refs):
    parts, outs = refs[: -s.count], refs[-s.count :]
    for d in range(s.count - 1, -1, -1):
        total = total_of(parts, d, s)
        outs[d][:, : s.width] = total[:, : s.width].astype(BF16)
        main, extra = get_inner(total[:, s.width :], s)
        outs[d][:, s.width :] = put_inner(main, extra, s)


def backward_end_kernel(s, *refs):
    packs = refs[: s.count]
    dy_ref, route_ref, score_ref, out_ref, grad_ref = refs[s.count : s.count + 5]
    rows_ref, extra_ref, tail_ref = refs[s.count + 5 :]
    route_row = route_ref[...].astype(F32)
    rows = tokens_of(packs, route_row, rows_ref, extra_ref, tail_ref, s)
    gate = as_column(2.5 * score_ref[...])
    out_ref[...] = (dy_ref[...].astype(F32) + gate * rows).astype(BF16)
    rank = slot_rows(route_row, s)
    dgate = jnp.zeros((1, s.tok), F32)
    for d in range(s.count):
        hit = route_row == expert_at(s, d)
        main, extra = get_inner(packs[d][:, s.width :].astype(F32), s)
        dgate += jnp.sum(
            jnp.where(hit & (rank == iota((s.main, s.tok), 0)), main, 0.0), axis=0, keepdims=True
        )
        for j in range(s.extra):
            dgate += jnp.where(hit & (rank == float(s.main + j)), extra[j], 0.0)
    grad_ref[...] = 2.5 * dgate


VMEM = pl.BlockSpec(memory_space=pltpu.VMEM)
HBM = pl.BlockSpec(memory_space=pltpu.HBM)


def call(kernel, name, outs, scratch, ins, *args, mib=16):
    shapes = [jax.ShapeDtypeStruct(shape, kind) for shape, kind in outs]
    args = [
        pltpu.with_memory_space_constraint(a, pltpu.HBM) if spec is HBM else a
        for a, spec in zip(args, ins)
    ]
    return pl.pallas_call(
        kernel,
        out_shape=shapes,
        in_specs=ins,
        out_specs=[VMEM] * len(shapes),
        scratch_shapes=scratch,
        compiler_params=pltpu.CompilerParams(vmem_limit_bytes=mib << 20),
        cost_estimate=pl.CostEstimate(flops=0, bytes_accessed=0, transcendentals=0),
        name=name,
    )(*args)


def tail_scratch(s, rows):
    return [
        pltpu.VMEM((rows, s.depth), F32),
        pltpu.VMEM((s.main, LANES * s.extra), F32),
    ]


def load(*arrays):
    return call(
        load_kernel,
        "load",
        [(a.shape, a.dtype) for a in arrays],
        [pltpu.SemaphoreType.DMA((len(arrays),))],
        [HBM] * len(arrays),
        *arrays,
    )


def row_scratch(s):
    return [pltpu.VMEM((s.rows, s.depth), BF16), *tail_scratch(s, s.tail_rows)]


def cross(s, packs, pieces):
    return [packs[0]] + [across(p, 1 + i // pieces, s) for i, p in enumerate(packs[1:])]


def spread(s, got):
    return list(got) + [beside(b, k, s) for k in range(1, s.slices) for b in got]


def hold(values, *after):
    return lax.optimization_barrier((values, after))[0]


def gather_parts(s, parts):
    return [beside(p, -(i // s.count), s) if i >= s.count else p for i, p in enumerate(parts)]


def step(routes, run, *args):
    like = jax.eval_shape(run, *args)
    skip = lambda *_: jax.tree.map(lambda a: jnp.zeros(a.shape, a.dtype), like)
    return lax.cond(routes[0, 0] < EXPERTS, run, skip, *args)


def end_scratch(s):
    low = -(-(s.count * s.extra) // 16) * 16
    return [pltpu.VMEM((s.count * s.main + low, s.depth), BF16), *tail_scratch(s, low)]


def body(
    x_fwd,
    saved_gate,
    saved_up,
    grad_next,
    routes_fwd,
    routes_bwd,
    scores_fwd,
    scores_bwd,
    w_gate,
    w_up,
    w_down,
):
    groups = lax.axis_size("expert")
    tok, depth = x_fwd.shape[1:]
    s = Sizes(saved_gate.shape[2], depth, EXPERTS, groups // EXPERTS, tok)
    hidden = w_gate.shape[2]
    route_a = routes_fwd.reshape(1, tok)
    route_b = routes_bwd.reshape(1, tok)
    score_a = scores_fwd.reshape(1, tok)
    score_b = scores_bwd.reshape(1, tok)

    packed = [((s.main, s.width), BF16)] * s.count
    sent_a = call(
        functools.partial(first_kernel, s),
        "first",
        packed[:1] + [((s.main, s.width // PIECES), BF16)] * (PIECES * (s.count - 1)),
        [
            pltpu.VMEM((1, tok), jnp.int32),
            pltpu.VMEM((tok, depth), BF16),
            *tail_scratch(s, 16),
            pltpu.SemaphoreType.DMA((2,)),
        ],
        [HBM] * 2,
        route_a,
        x_fwd[0],
    )
    upstream = from_behind(grad_next, "section", -1)[0]
    wg, wu, wd, route_a, route_b, score_a, score_b = load(
        w_gate[0], w_up[0], w_down[0], route_a, route_b, score_a, score_b
    )
    factors = call(
        functools.partial(saved_kernel, s),
        "saved",
        [((s.rows, hidden), F32)] * 3,
        [pltpu.VMEM((s.rows, hidden), F32)] * 2,
        [VMEM] * 2,
        saved_gate[0],
        saved_up[0],
    )
    wide = s.width + LANES

    def forward(rows, *weights):
        parts = call(
            functools.partial(forward_kernel, s),
            "forward",
            [((s.main, s.width), BF16)] * s.blocks,
            row_scratch(s),
            [VMEM] * (len(rows) + 3),
            *rows,
            *weights,
        )
        return tuple(gather_parts(s, parts))

    def backward(got, *rest):
        parts = call(
            functools.partial(backward_kernel, s),
            "backward",
            [((s.main, wide), BF16)] * s.blocks,
            row_scratch(s),
            [VMEM] * (s.blocks + 6),
            *spread(s, got),
            *rest,
        )
        return tuple(gather_parts(s, parts))

    got = cross(s, sent_a, PIECES)
    got[1:] = hold(got[1:], score_a, factors)
    rows_a = spread(s, got)
    sent_b = call(
        functools.partial(pack_kernel, s),
        "pack",
        packed,
        tail_scratch(s, 16),
        [VMEM] * 2,
        route_b,
        hold(upstream, got[1:]),
    )
    got_b = cross(s, sent_b, 1)
    parts_a = step(route_a, forward, hold(rows_a, sent_b), wg, wu, wd)
    sums_a = call(
        functools.partial(forward_sum_kernel, s),
        "forward_sum",
        [((s.main, wide + LANES), BF16)] + [((s.main, s.width), BF16)] * (s.count - 1),
        [],
        [VMEM] * (s.blocks + 3),
        *parts_a,
        sent_a[0],
        route_a,
        score_a,
    )
    back_a = [across(sums_a[d], -d, s) for d in range(1, s.count)]
    moved = [from_behind(sums_a[0], "section", 1)]
    got_b[1:] = hold(got_b[1:], sums_a)
    parts_b = step(route_b, backward, got_b, *factors, wg, wu, wd)
    back_a = hold(back_a, parts_b)
    for d in range(1, s.count):
        y = call(
            functools.partial(forward_add_kernel, s, d),
            "forward_add",
            [((s.main, wide), BF16)],
            [],
            [VMEM] * (3 + PIECES),
            back_a[d - 1],
            *sent_a[1 + (d - 1) * PIECES : 1 + d * PIECES],
            route_a,
            score_a,
        )[0]
        moved.append(from_behind(y, "section", 1))
    sums_b = call(
        functools.partial(backward_sum_kernel, s),
        "backward_sum",
        [((s.main, wide), BF16)] * s.count,
        [],
        [VMEM] * s.blocks,
        *hold(parts_b, y),
    )
    back_b = [sums_b[0]] + [across(sums_b[d], -d, s) for d in range(1, s.count)]
    next_input = call(
        functools.partial(forward_end_kernel, s),
        "forward_end",
        [((tok, depth), BF16)],
        end_scratch(s) + [pltpu.VMEM((s.main, LANES), F32)],
        [VMEM] * s.count,
        *moved,
    )[0]
    input_grad, score_grad = call(
        functools.partial(backward_end_kernel, s),
        "backward_end",
        [((tok, depth), BF16), ((1, tok), F32)],
        end_scratch(s),
        [VMEM] * (s.count + 3),
        *hold(back_b, next_input),
        upstream,
        route_b,
        score_b,
    )
    return next_input[None], input_grad[None], score_grad.reshape(1, tok, 1)


def solution(mesh):
    placed = (
        P("section", "expert", None),
        P("section", None, None, "expert"),
        P("section", None, None, "expert"),
        P("section", "expert", None),
        P("section", "expert", None),
        P("section", "expert", None),
        P("section", "expert", None),
        P("section", "expert", None),
        P("section", None, "expert"),
        P("section", None, "expert"),
        P("section", "expert", None),
    )
    return jax.shard_map(
        body,
        mesh=mesh,
        in_specs=placed,
        out_specs=(
            P("section", "expert", None),
            P("section", "expert", None),
            P("section", "expert", None),
        ),
        check_vma=False,
    )
```

```python
import functools

import jax
import jax.numpy as jnp
from jax import lax
from jax.experimental import pallas as pl
from jax.experimental.pallas import tpu as pltpu
from jax.sharding import PartitionSpec as P

EXPERTS = 2
LANES = 128
PIECES = 2
F32 = jnp.float32
BF16 = jnp.bfloat16
NT = (((1,), (1,)), ((), ()))


class Sizes:
    def __init__(self, cap, depth, count, slices, tok):
        self.cap, self.depth, self.count, self.slices, self.tok = cap, depth, count, slices, tok
        self.main = cap // 16 * 16
        self.extra = cap - self.main
        self.folds = depth // LANES
        assert self.folds + 4 <= self.main and depth % LANES == 0
        assert max(cap, tok) <= LANES
        self.width = depth + LANES * self.extra
        self.blocks = count * slices
        self.tail_rows = -(-(self.blocks * self.extra) // 16) * 16
        self.rows = self.blocks * self.main + self.tail_rows


def from_behind(block, axis, distance):
    devices = range(lax.axis_size(axis))
    route = [((i - distance) % len(devices), i) for i in devices]
    return lax.ppermute(block, axis, route)


def to_next(block, distance, s):
    sections, own = lax.axis_size("section"), s.count * s.slices
    route = [
        (
            l * own + e * s.slices + j,
            (l + 1) % sections * own + (e + distance) % s.count * s.slices + j,
        )
        for l in range(sections)
        for e in range(s.count)
        for j in range(s.slices)
    ]
    return lax.ppermute(block, ("section", "expert"), route)


def across(block, distance, s):
    route = [
        (e * s.slices + j, (e + distance) % s.count * s.slices + j)
        for e in range(s.count)
        for j in range(s.slices)
    ]
    return lax.ppermute(block, "expert", route)


def beside(block, distance, s):
    route = [
        (e * s.slices + j, e * s.slices + (j + distance) % s.slices)
        for e in range(s.count)
        for j in range(s.slices)
    ]
    return lax.ppermute(block, "expert", route)


def iota(shape, dim):
    return lax.broadcasted_iota(jnp.int32, shape, dim).astype(F32)


def as_column(row):
    n = row.shape[1]
    return jnp.sum(
        jnp.where(iota((n, n), 0) == iota((n, n), 1), row, 0.0), axis=1, keepdims=True
    )


def own_expert(s):
    return lax.axis_index("expert") // s.slices


def expert_at(s, distance):
    return ((own_expert(s) + distance) % s.count).astype(F32)


def slot_rows(route_row, s):
    col = as_column(route_row)
    n = s.tok
    same = (col == route_row) & (iota((n, n), 0) < iota((n, n), 1))
    return jnp.sum(jnp.where(same, 1.0, 0.0), axis=0, keepdims=True)


def slot_columns(route_row, s):
    col = as_column(route_row)
    n = s.tok
    same = (col == route_row) & (iota((n, n), 1) < iota((n, n), 0))
    return col, jnp.sum(jnp.where(same, 1.0, 0.0), axis=1, keepdims=True)


def fold(values_ref, first, tail_ref, s):
    for j in range(s.extra):
        for r in range(s.folds):
            tail_ref[r : r + 1, j * LANES : (j + 1) * LANES] = values_ref[
                first + j : first + j + 1, r * LANES : (r + 1) * LANES
            ]


def unfold(tail_ref, values_ref, first, s):
    for j in range(s.extra):
        for r in range(s.folds):
            values_ref[first + j : first + j + 1, r * LANES : (r + 1) * LANES] = tail_ref[
                r : r + 1, j * LANES : (j + 1) * LANES
            ]


def put_scores(route_row, score_row, expert, tail_ref, s):
    col, rank = slot_columns(route_row, s)
    hit = (col == expert) & (rank == iota((s.tok, LANES), 1))
    row = jnp.sum(jnp.where(hit, as_column(score_row), 0.0), axis=0, keepdims=True)
    for p, piece in enumerate(split_three(row)):
        at = s.folds + 1 + p
        tail_ref[at : at + 1, :LANES] = piece


def get_gates(tail, s):
    at = s.folds + 1
    row = 2.5 * (tail[at : at + 1] + tail[at + 1 : at + 2] + tail[at + 2 : at + 3])
    lane = iota((s.main, LANES), 1)
    main = jnp.sum(jnp.where(lane == iota((s.main, LANES), 0), row, 0.0), axis=1, keepdims=True)
    extra = [
        jnp.sum(jnp.where(lane[:1] == float(s.main + j), row, 0.0), axis=1, keepdims=True)
        for j in range(s.extra)
    ]
    return main, extra


def add_gated(out_ref, base, main, extra, total, s):
    d = s.depth
    out_ref[:, :d] = (read(base, 0, d).astype(F32) + main * total[:, :d]).astype(BF16)
    for j in range(s.extra):
        at = slice(d + j * LANES, d + (j + 1) * LANES)
        value = read(base, at.start, at.stop).astype(F32) + extra[j] * total[:, at]
        out_ref[:, at] = value.astype(BF16)


def read(pieces, low, high):
    found, at = [], 0
    for piece in pieces:
        width = piece.shape[1]
        a, b = max(low, at), min(high, at + width)
        if a < b:
            found.append(piece[:, a - at : b - at])
        at += width
    return found[0] if len(found) == 1 else jnp.concatenate(found, axis=1)


def write(pieces, low, value):
    at = 0
    for piece in pieces:
        width = piece.shape[1]
        a, b = max(low, at), min(low + value.shape[1], at + width)
        if a < b:
            piece[:, a - at : b - at] = value[:, a - low : b - low]
        at += width


def grouped(refs, s, pieces):
    one = 1 + (s.count - 1) * pieces
    packs = []
    for first in range(0, len(refs), one):
        packs.append(refs[first : first + 1])
        for at in range(first + 1, first + one, pieces):
            packs.append(refs[at : at + pieces])
    return packs


def pack_rows(s, route_row, x, outs, extra_ref, tail_ref, score_row=None):
    rank = slot_rows(route_row, s)
    slots = iota((s.main + 16, s.tok), 0)
    tail_ref[...] = jnp.zeros_like(tail_ref)
    for d in range(s.count):
        hit = route_row == expert_at(s, d)
        table = jnp.where(hit & (rank == slots), 1.0, 0.0).astype(BF16)
        rows = jnp.dot(table, x, preferred_element_type=F32)
        write(outs[d], 0, rows[: s.main].astype(BF16))
        extra_ref[...] = rows[s.main :]
        fold(extra_ref, 0, tail_ref, s)
        if score_row is not None:
            put_scores(route_row, score_row, expert_at(s, d), tail_ref, s)
        write(outs[d], s.depth, tail_ref[...].astype(BF16))


def first_kernel(s, route_hbm, score_hbm, x_hbm, *rest):
    outs = grouped(rest[:-6], s, PIECES)
    route_ref, score_ref, x_ref, extra_ref, tail_ref, sems = rest[-6:]
    copies = [
        pltpu.make_async_copy(src, dst, sems.at[i])
        for i, (src, dst) in enumerate(
            ((route_hbm, route_ref), (score_hbm, score_ref), (x_hbm, x_ref))
        )
    ]
    for copy in copies:
        copy.start()
    for copy in copies:
        copy.wait()
    route_row = route_ref[...].astype(F32)
    pack_rows(s, route_row, x_ref[...], outs, extra_ref, tail_ref, score_ref[...])


def pack_kernel(s, route_ref, x_ref, *rest):
    outs, (extra_ref, tail_ref) = grouped(rest[:-2], s, 1), rest[-2:]
    pack_rows(s, route_ref[...].astype(F32), x_ref[...], outs, extra_ref, tail_ref)


def load_kernel(*refs):
    sems = refs[-1]
    n = (len(refs) - 1) // 2
    copies = [pltpu.make_async_copy(refs[i], refs[n + i], sems.at[i]) for i in range(n)]
    for copy in copies:
        copy.start()
    for copy in copies:
        copy.wait()


def gather_packs(packs, rows_ref, extra_ref, tail_ref, s):
    extra_ref[...] = jnp.zeros_like(extra_ref)
    for i, pack in enumerate(packs):
        rows_ref[i * s.main : (i + 1) * s.main, :] = read(pack, 0, s.depth)
        tail_ref[...] = read(pack, s.depth, s.width).astype(F32)
        unfold(tail_ref, extra_ref, i * s.extra, s)
    rows_ref[s.blocks * s.main :, :] = extra_ref[...].astype(BF16)


def put(outs, i, at, value, s):
    if i < s.count:
        outs[i][:, at] = value
        return
    n = (len(outs) - s.count) // (s.blocks - s.count)
    rows = s.main // n
    for h in range(n):
        outs[s.count + (i - s.count) * n + h][:, at] = value[h * rows : (h + 1) * rows]


def scatter_chunk(value, outs, extra_ref, at, s):
    for i in range(s.blocks):
        put(outs, i, at, value[i * s.main : (i + 1) * s.main].astype(BF16), s)
    extra_ref[:, at] = value[s.blocks * s.main :]


def scatter_tails(outs, extra_ref, tail_ref, s):
    for i in range(s.blocks):
        fold(extra_ref, i * s.extra, tail_ref, s)
        put(outs, i, slice(s.depth, s.width), tail_ref[...].astype(BF16), s)


def chunk_of(depth):
    for chunk in (512, 256, 128):
        if depth % chunk == 0:
            return chunk


def forward_kernel(s, *refs):
    n = s.slices * (1 + (s.count - 1) * PIECES)
    packs = grouped(refs[:n], s, PIECES)
    wg, wu, wd = refs[n : n + 3]
    outs = refs[n + 3 : -3]
    rows_ref, extra_ref, tail_ref = refs[-3:]
    chunk = chunk_of(s.depth)
    gather_packs(packs, rows_ref, extra_ref, tail_ref, s)
    g = u = None
    for c in range(0, s.depth, chunk):
        lhs = rows_ref[:, c : c + chunk]
        more_g = jnp.dot(lhs, wg[c : c + chunk, :], preferred_element_type=F32)
        more_u = jnp.dot(lhs, wu[c : c + chunk, :], preferred_element_type=F32)
        g = more_g if g is None else g + more_g
        u = more_u if u is None else u + more_u
    hidden = (g * jax.nn.sigmoid(g) * u).astype(BF16)
    tail_ref[...] = jnp.zeros_like(tail_ref)
    for c in range(0, s.depth, chunk):
        part = jnp.dot(hidden, wd[:, c : c + chunk], preferred_element_type=F32)
        scatter_chunk(part, outs, extra_ref, slice(c, c + chunk), s)
    scatter_tails(outs, extra_ref, tail_ref, s)


def saved_kernel(s, gate_ref, up_ref, c1_ref, c2_ref, hb_ref, g_ref, u_ref):
    me = lax.axis_index("expert")
    e, j = me // s.slices, me % s.slices
    g_ref[...] = jnp.zeros_like(g_ref)
    u_ref[...] = jnp.zeros_like(u_ref)
    for i in range(s.blocks):
        k, d = i // s.count, i % s.count
        source = (e + s.count - d) % s.count * s.slices + (j + s.slices - k) % s.slices
        for src, dst in ((gate_ref, g_ref), (up_ref, u_ref)):
            rows = src[source].astype(F32)
            dst[i * s.main : (i + 1) * s.main, :] = rows[: s.main]
            first = s.blocks * s.main + i * s.extra
            dst[first : first + s.extra, :] = rows[s.main :]
    g = g_ref[...]
    u = u_ref[...]
    sig = jax.nn.sigmoid(g)
    c1_ref[...] = u * sig * (1.0 + g * (1.0 - sig))
    c2_ref[...] = g * sig
    hb_ref[...] = (g * sig * u).astype(BF16).astype(F32)


def split_three(value):
    high = value.astype(BF16).astype(F32)
    rest = value - high
    mid = rest.astype(BF16).astype(F32)
    return high, mid, (rest - mid).astype(BF16).astype(F32)


def put_inner(main, extra, s):
    lane = iota((s.main, LANES), 1)
    row = iota((s.main, LANES), 0)
    out = jnp.zeros((s.main, LANES), F32)
    for p, piece in enumerate(split_three(main)):
        out = jnp.where(lane == float(p), piece, out)
    for j in range(s.extra):
        for p, piece in enumerate(split_three(extra[j])):
            out = jnp.where((lane == float(3 + p)) & (row == float(j)), piece, out)
    return out.astype(BF16)


def get_inner(block, s):
    lane = iota((s.main, LANES), 1)
    row = iota((s.main, LANES), 0)
    main = jnp.sum(jnp.where(lane < 3.0, block, 0.0), axis=1, keepdims=True)
    second = jnp.sum(
        jnp.where((lane >= 3.0) & (lane < 6.0), block, 0.0), axis=1, keepdims=True
    )
    extra = [
        jnp.sum(jnp.where(row[:, :1] == float(j), second, 0.0), axis=0, keepdims=True)
        for j in range(s.extra)
    ]
    return main, extra


def backward_kernel(s, *refs):
    packs = grouped(refs[: s.blocks], s, 1)
    c1, c2, hb, wg, wu, wd = refs[s.blocks : s.blocks + 6]
    outs = refs[s.blocks + 6 : -3]
    rows_ref, extra_ref, tail_ref = refs[-3:]
    chunk = chunk_of(s.depth)
    gather_packs(packs, rows_ref, extra_ref, tail_ref, s)
    a = None
    for c in range(0, s.depth, chunk):
        more = lax.dot_general(
            rows_ref[:, c : c + chunk], wd[:, c : c + chunk], NT, preferred_element_type=F32
        )
        a = more if a is None else a + more
    dgp = (a * c1[...]).astype(BF16)
    dup = (a * c2[...]).astype(BF16)
    inner = jnp.sum(a * hb[...], axis=1, keepdims=True)
    for i in range(s.blocks):
        first = s.blocks * s.main + i * s.extra
        outs[i][:, s.width :] = put_inner(
            inner[i * s.main : (i + 1) * s.main],
            [inner[first + j : first + j + 1] for j in range(s.extra)],
            s,
        )
    tail_ref[...] = jnp.zeros_like(tail_ref)
    for c in range(0, s.depth, chunk):
        part = lax.dot_general(
            dgp, wg[c : c + chunk, :], NT, preferred_element_type=F32
        ) + lax.dot_general(dup, wu[c : c + chunk, :], NT, preferred_element_type=F32)
        scatter_chunk(part, outs, extra_ref, slice(c, c + chunk), s)
    scatter_tails(outs, extra_ref, tail_ref, s)


def total_of(parts, d, s):
    total = parts[d][...].astype(F32)
    n = (len(parts) - s.count) // (s.blocks - s.count)
    for i in range(s.count + d, s.blocks, s.count):
        first = s.count + (i - s.count) * n
        found = [part[...].astype(F32) for part in parts[first : first + n]]
        total = total + (found[0] if n == 1 else jnp.concatenate(found, axis=0))
    return total


def forward_sum_kernel(s, *refs):
    n = s.count + (s.blocks - s.count) * PIECES
    parts, bases = refs[:n], grouped(refs[n : n + 1 + (s.count - 1) * PIECES], s, PIECES)
    route_ref, outs = refs[-1 - s.count], refs[-s.count :]
    for d in range(s.count - 1, -1, -1):
        tail = read(bases[d], s.depth, s.depth + LANES).astype(F32)
        main, extra = get_gates(tail, s)
        add_gated(outs[d], bases[d], main, extra, total_of(parts, d, s), s)
        spare = outs[d].shape[1] - s.width
        if spare:
            outs[d][:, s.width :] = jnp.zeros((s.main, spare), BF16)
    at = s.folds
    outs[0][at : at + 1, s.depth : s.depth + s.tok] = route_ref[...].astype(F32).astype(BF16)


def tokens_of(packs, route_row, rows_ref, extra_ref, tail_ref, s):
    extra_ref[...] = jnp.zeros_like(extra_ref)
    for d, pack in enumerate(packs):
        rows_ref[d * s.main : (d + 1) * s.main, :] = pack[:, : s.depth]
        tail_ref[...] = pack[:, s.depth : s.width].astype(F32)
        unfold(tail_ref, extra_ref, d * s.extra, s)
    rows_ref[s.count * s.main :, :] = extra_ref[...].astype(BF16)
    col, rank = slot_columns(route_row, s)
    high = rows_ref.shape[0]
    place = jnp.full((s.tok, 1), -1.0, F32)
    for d in range(s.count):
        at = jnp.where(
            rank < float(s.main),
            rank + float(d * s.main),
            rank + float(s.count * s.main + d * s.extra - s.main),
        )
        place = jnp.where(col == expert_at(s, d), at, place)
    table = jnp.where(place == iota((s.tok, high), 1), 1.0, 0.0).astype(BF16)
    return jnp.dot(table, rows_ref[...], preferred_element_type=F32)


def forward_end_kernel(s, *refs):
    packs = refs[: s.count]
    out_ref, rows_ref, extra_ref, tail_ref, row_ref = refs[s.count :]
    row_ref[...] = packs[0][:, s.depth : s.depth + LANES].astype(F32)
    route_row = row_ref[s.folds : s.folds + 1, : s.tok]
    out_ref[...] = tokens_of(packs, route_row, rows_ref, extra_ref, tail_ref, s).astype(BF16)


def backward_sum_kernel(s, *refs):
    parts, outs = refs[: -s.count], refs[-s.count :]
    for d in range(s.count - 1, -1, -1):
        total = total_of(parts, d, s)
        outs[d][:, : s.width] = total[:, : s.width].astype(BF16)
        main, extra = get_inner(total[:, s.width :], s)
        outs[d][:, s.width :] = put_inner(main, extra, s)


def backward_end_kernel(s, *refs):
    packs = refs[: s.count]
    dy_ref, route_ref, score_ref, out_ref, grad_ref = refs[s.count : s.count + 5]
    rows_ref, extra_ref, tail_ref = refs[s.count + 5 :]
    route_row = route_ref[...].astype(F32)
    rows = tokens_of(packs, route_row, rows_ref, extra_ref, tail_ref, s)
    gate = as_column(2.5 * score_ref[...])
    out_ref[...] = (dy_ref[...].astype(F32) + gate * rows).astype(BF16)
    rank = slot_rows(route_row, s)
    dgate = jnp.zeros((1, s.tok), F32)
    for d in range(s.count):
        hit = route_row == expert_at(s, d)
        main, extra = get_inner(packs[d][:, s.width :].astype(F32), s)
        dgate += jnp.sum(
            jnp.where(hit & (rank == iota((s.main, s.tok), 0)), main, 0.0), axis=0, keepdims=True
        )
        for j in range(s.extra):
            dgate += jnp.where(hit & (rank == float(s.main + j)), extra[j], 0.0)
    grad_ref[...] = 2.5 * dgate


VMEM = pl.BlockSpec(memory_space=pltpu.VMEM)
HBM = pl.BlockSpec(memory_space=pltpu.HBM)


def call(kernel, name, outs, scratch, ins, *args, mib=16):
    shapes = [jax.ShapeDtypeStruct(shape, kind) for shape, kind in outs]
    args = [
        pltpu.with_memory_space_constraint(a, pltpu.HBM) if spec is HBM else a
        for a, spec in zip(args, ins)
    ]
    return pl.pallas_call(
        kernel,
        out_shape=shapes,
        in_specs=ins,
        out_specs=[VMEM] * len(shapes),
        scratch_shapes=scratch,
        compiler_params=pltpu.CompilerParams(vmem_limit_bytes=mib << 20),
        cost_estimate=pl.CostEstimate(flops=0, bytes_accessed=0, transcendentals=0),
        name=name,
    )(*args)


def tail_scratch(s, rows):
    return [
        pltpu.VMEM((rows, s.depth), F32),
        pltpu.VMEM((s.main, LANES * s.extra), F32),
    ]


def load(*arrays):
    return call(
        load_kernel,
        "load",
        [(a.shape, a.dtype) for a in arrays],
        [pltpu.SemaphoreType.DMA((len(arrays),))],
        [HBM] * len(arrays),
        *arrays,
    )


def row_scratch(s):
    return [pltpu.VMEM((s.rows, s.depth), BF16), *tail_scratch(s, s.tail_rows)]


def cross(s, packs, pieces):
    return [packs[0]] + [across(p, 1 + i // pieces, s) for i, p in enumerate(packs[1:])]


def spread(s, got):
    return list(got) + [beside(b, k, s) for k in range(1, s.slices) for b in got]


def hold(values, *after):
    return lax.optimization_barrier((values, after))[0]


def parts_shape(s, width, pieces):
    kept = [((s.main, width), BF16)] * s.count
    return kept + [((s.main // pieces, width), BF16)] * ((s.blocks - s.count) * pieces)


def gather_parts(s, parts):
    n = (len(parts) - s.count) // (s.blocks - s.count)
    moved = [beside(p, -(i // n // s.count + 1), s) for i, p in enumerate(parts[s.count :])]
    return list(parts[: s.count]) + moved


def step(routes, run, *args):
    like = jax.eval_shape(run, *args)
    skip = lambda *_: jax.tree.map(lambda a: jnp.zeros(a.shape, a.dtype), like)
    return lax.cond(routes[0, 0] < EXPERTS, run, skip, *args)


def end_scratch(s):
    low = -(-(s.count * s.extra) // 16) * 16
    return [pltpu.VMEM((s.count * s.main + low, s.depth), BF16), *tail_scratch(s, low)]


def body(
    x_fwd,
    saved_gate,
    saved_up,
    grad_next,
    routes_fwd,
    routes_bwd,
    scores_fwd,
    scores_bwd,
    w_gate,
    w_up,
    w_down,
):
    groups = lax.axis_size("expert")
    tok, depth = x_fwd.shape[1:]
    s = Sizes(saved_gate.shape[2], depth, EXPERTS, groups // EXPERTS, tok)
    hidden = w_gate.shape[2]
    route_a = routes_fwd.reshape(1, tok)
    route_b = routes_bwd.reshape(1, tok)
    score_a = scores_fwd.reshape(1, tok)
    score_b = scores_bwd.reshape(1, tok)

    packed = [((s.main, s.width), BF16)] * s.count
    sent_a = call(
        functools.partial(first_kernel, s),
        "first",
        packed[:1] + [((s.main, s.width // PIECES), BF16)] * (PIECES * (s.count - 1)),
        [
            pltpu.VMEM((1, tok), jnp.int32),
            pltpu.VMEM((1, tok), F32),
            pltpu.VMEM((tok, depth), BF16),
            *tail_scratch(s, 16),
            pltpu.SemaphoreType.DMA((3,)),
        ],
        [HBM] * 3,
        route_a,
        score_a,
        x_fwd[0],
    )
    upstream = from_behind(grad_next, "section", -1)[0]
    wg, wu, wd, route_a, route_b, score_b = load(
        w_gate[0], w_up[0], w_down[0], route_a, route_b, score_b
    )
    factors = call(
        functools.partial(saved_kernel, s),
        "saved",
        [((s.rows, hidden), F32)] * 3,
        [pltpu.VMEM((s.rows, hidden), F32)] * 2,
        [VMEM] * 2,
        saved_gate[0],
        saved_up[0],
    )
    wide = s.width + LANES

    def backward(got, *rest):
        parts = call(
            functools.partial(backward_kernel, s),
            "backward",
            [((s.main, wide), BF16)] * s.blocks,
            row_scratch(s),
            [VMEM] * (s.blocks + 6),
            *spread(s, got),
            *rest,
        )
        sums = call(
            functools.partial(backward_sum_kernel, s),
            "backward_sum",
            [((s.main, wide), BF16)] * s.count,
            [],
            [VMEM] * s.blocks,
            *gather_parts(s, parts),
        )
        return tuple(sums)

    got = cross(s, sent_a, PIECES)
    got[1:] = hold(got[1:], route_a, factors)
    rows_a = spread(s, got)
    sent_b = call(
        functools.partial(pack_kernel, s),
        "pack",
        packed,
        tail_scratch(s, 16),
        [VMEM] * 2,
        route_b,
        hold(upstream, got[1:]),
    )
    got_b = cross(s, sent_b, 1)
    parts_a = call(
        functools.partial(forward_kernel, s),
        "forward",
        parts_shape(s, s.width, PIECES),
        row_scratch(s),
        [VMEM] * (len(rows_a) + 3),
        *hold(rows_a, sent_b),
        wg,
        wu,
        wd,
    )
    parts_a = gather_parts(s, parts_a)
    sums_a = call(
        functools.partial(forward_sum_kernel, s),
        "forward_sum",
        [((s.main, wide), BF16)] * s.count,
        [],
        [VMEM] * (len(parts_a) + len(got) + 1),
        *parts_a,
        *got,
        route_a,
    )
    moved = [to_next(y, -d, s) for d, y in enumerate(sums_a)]
    got_b[1:] = hold(got_b[1:], sums_a)
    sums_b = step(route_b, backward, got_b, *factors, wg, wu, wd)
    back_b = [sums_b[0]] + [across(sums_b[d], -d, s) for d in range(1, s.count)]
    next_input = call(
        functools.partial(forward_end_kernel, s),
        "forward_end",
        [((tok, depth), BF16)],
        end_scratch(s) + [pltpu.VMEM((s.main, LANES), F32)],
        [VMEM] * s.count,
        *moved,
    )[0]
    input_grad, score_grad = call(
        functools.partial(backward_end_kernel, s),
        "backward_end",
        [((tok, depth), BF16), ((1, tok), F32)],
        end_scratch(s),
        [VMEM] * (s.count + 3),
        *hold(back_b, next_input),
        upstream,
        route_b,
        score_b,
    )
    return next_input[None], input_grad[None], score_grad.reshape(1, tok, 1)


def solution(mesh):
    placed = (
        P("section", "expert", None),
        P("section", None, None, "expert"),
        P("section", None, None, "expert"),
        P("section", "expert", None),
        P("section", "expert", None),
        P("section", "expert", None),
        P("section", "expert", None),
        P("section", "expert", None),
        P("section", None, "expert"),
        P("section", None, "expert"),
        P("section", "expert", None),
    )
    return jax.shard_map(
        body,
        mesh=mesh,
        in_specs=placed,
        out_specs=(
            P("section", "expert", None),
            P("section", "expert", None),
            P("section", "expert", None),
        ),
        check_vma=False,
    )
```

```python
import functools

import jax
import jax.numpy as jnp
from jax import lax
from jax.experimental import pallas as pl
from jax.experimental.pallas import tpu as pltpu
from jax.sharding import PartitionSpec as P

EXPERTS = 2
LANES = 128
PIECES = 2
F32 = jnp.float32
BF16 = jnp.bfloat16
NT = (((1,), (1,)), ((), ()))


class Sizes:
    def __init__(self, cap, depth, count, slices, tok):
        self.cap, self.depth, self.count, self.slices, self.tok = cap, depth, count, slices, tok
        self.main = cap // 16 * 16
        self.extra = cap - self.main
        self.folds = depth // LANES
        assert self.folds + 4 <= self.main and depth % LANES == 0
        assert max(cap, tok) <= LANES
        self.width = depth + LANES * self.extra
        self.blocks = count * slices
        self.tail_rows = -(-(self.blocks * self.extra) // 16) * 16
        self.rows = self.blocks * self.main + self.tail_rows


def from_behind(block, axis, distance):
    devices = range(lax.axis_size(axis))
    route = [((i - distance) % len(devices), i) for i in devices]
    return lax.ppermute(block, axis, route)


def to_next(block, distance, s):
    sections, own = lax.axis_size("section"), s.count * s.slices
    route = [
        (
            l * own + e * s.slices + j,
            (l + 1) % sections * own + (e + distance) % s.count * s.slices + j,
        )
        for l in range(sections)
        for e in range(s.count)
        for j in range(s.slices)
    ]
    return lax.ppermute(block, ("section", "expert"), route)


def across(block, distance, s):
    route = [
        (e * s.slices + j, (e + distance) % s.count * s.slices + j)
        for e in range(s.count)
        for j in range(s.slices)
    ]
    return lax.ppermute(block, "expert", route)


def beside(block, distance, s):
    route = [
        (e * s.slices + j, e * s.slices + (j + distance) % s.slices)
        for e in range(s.count)
        for j in range(s.slices)
    ]
    return lax.ppermute(block, "expert", route)


def iota(shape, dim):
    return lax.broadcasted_iota(jnp.int32, shape, dim).astype(F32)


def as_column(row):
    n = row.shape[1]
    return jnp.sum(
        jnp.where(iota((n, n), 0) == iota((n, n), 1), row, 0.0), axis=1, keepdims=True
    )


def own_expert(s):
    return lax.axis_index("expert") // s.slices


def expert_at(s, distance):
    return ((own_expert(s) + distance) % s.count).astype(F32)


def slot_rows(route_row, s):
    col = as_column(route_row)
    n = s.tok
    same = (col == route_row) & (iota((n, n), 0) < iota((n, n), 1))
    return jnp.sum(jnp.where(same, 1.0, 0.0), axis=0, keepdims=True)


def slot_columns(route_row, s):
    col = as_column(route_row)
    n = s.tok
    same = (col == route_row) & (iota((n, n), 1) < iota((n, n), 0))
    return col, jnp.sum(jnp.where(same, 1.0, 0.0), axis=1, keepdims=True)


def fold(values_ref, first, tail_ref, s):
    for j in range(s.extra):
        for r in range(s.folds):
            tail_ref[r : r + 1, j * LANES : (j + 1) * LANES] = values_ref[
                first + j : first + j + 1, r * LANES : (r + 1) * LANES
            ]


def unfold(tail_ref, values_ref, first, s):
    for j in range(s.extra):
        for r in range(s.folds):
            values_ref[first + j : first + j + 1, r * LANES : (r + 1) * LANES] = tail_ref[
                r : r + 1, j * LANES : (j + 1) * LANES
            ]


def put_scores(route_row, score_row, expert, tail_ref, s):
    col, rank = slot_columns(route_row, s)
    hit = (col == expert) & (rank == iota((s.tok, LANES), 1))
    row = jnp.sum(jnp.where(hit, as_column(score_row), 0.0), axis=0, keepdims=True)
    for p, piece in enumerate(split_three(row)):
        at = s.folds + 1 + p
        tail_ref[at : at + 1, :LANES] = piece


def get_gates(tail, s):
    at = s.folds + 1
    row = 2.5 * (tail[at : at + 1] + tail[at + 1 : at + 2] + tail[at + 2 : at + 3])
    lane = iota((s.main, LANES), 1)
    main = jnp.sum(jnp.where(lane == iota((s.main, LANES), 0), row, 0.0), axis=1, keepdims=True)
    extra = [
        jnp.sum(jnp.where(lane[:1] == float(s.main + j), row, 0.0), axis=1, keepdims=True)
        for j in range(s.extra)
    ]
    return main, extra


def add_gated(out_ref, base, main, extra, total, s):
    d = s.depth
    out_ref[:, :d] = (read(base, 0, d).astype(F32) + main * total[:, :d]).astype(BF16)
    for j in range(s.extra):
        at = slice(d + j * LANES, d + (j + 1) * LANES)
        value = read(base, at.start, at.stop).astype(F32) + extra[j] * total[:, at]
        out_ref[:, at] = value.astype(BF16)


def read(pieces, low, high):
    found, at = [], 0
    for piece in pieces:
        width = piece.shape[1]
        a, b = max(low, at), min(high, at + width)
        if a < b:
            found.append(piece[:, a - at : b - at])
        at += width
    return found[0] if len(found) == 1 else jnp.concatenate(found, axis=1)


def write(pieces, low, value):
    at = 0
    for piece in pieces:
        width = piece.shape[1]
        a, b = max(low, at), min(low + value.shape[1], at + width)
        if a < b:
            piece[:, a - at : b - at] = value[:, a - low : b - low]
        at += width


def grouped(refs, s, pieces):
    one = 1 + (s.count - 1) * pieces
    packs = []
    for first in range(0, len(refs), one):
        packs.append(refs[first : first + 1])
        for at in range(first + 1, first + one, pieces):
            packs.append(refs[at : at + pieces])
    return packs


def pack_rows(s, route_row, x, outs, extra_ref, tail_ref, score_row=None):
    rank = slot_rows(route_row, s)
    slots = iota((s.main + 16, s.tok), 0)
    tail_ref[...] = jnp.zeros_like(tail_ref)
    for d in range(s.count):
        hit = route_row == expert_at(s, d)
        table = jnp.where(hit & (rank == slots), 1.0, 0.0).astype(BF16)
        rows = jnp.dot(table, x, preferred_element_type=F32)
        write(outs[d], 0, rows[: s.main].astype(BF16))
        extra_ref[...] = rows[s.main :]
        fold(extra_ref, 0, tail_ref, s)
        if score_row is not None:
            put_scores(route_row, score_row, expert_at(s, d), tail_ref, s)
        write(outs[d], s.depth, tail_ref[...].astype(BF16))


def first_kernel(s, route_hbm, score_hbm, x_hbm, *rest):
    outs = grouped(rest[:-6], s, PIECES)
    route_ref, score_ref, x_ref, extra_ref, tail_ref, sems = rest[-6:]
    copies = [
        pltpu.make_async_copy(src, dst, sems.at[i])
        for i, (src, dst) in enumerate(
            ((route_hbm, route_ref), (score_hbm, score_ref), (x_hbm, x_ref))
        )
    ]
    for copy in copies:
        copy.start()
    for copy in copies:
        copy.wait()
    route_row = route_ref[...].astype(F32)
    pack_rows(s, route_row, x_ref[...], outs, extra_ref, tail_ref, score_ref[...])


def pack_kernel(s, route_ref, x_ref, *rest):
    outs, (extra_ref, tail_ref) = grouped(rest[:-2], s, 1), rest[-2:]
    pack_rows(s, route_ref[...].astype(F32), x_ref[...], outs, extra_ref, tail_ref)


def load_kernel(*refs):
    sems = refs[-1]
    n = (len(refs) - 1) // 2
    copies = [pltpu.make_async_copy(refs[i], refs[n + i], sems.at[i]) for i in range(n)]
    for copy in copies:
        copy.start()
    for copy in copies:
        copy.wait()


def gather_packs(packs, rows_ref, extra_ref, tail_ref, s):
    extra_ref[...] = jnp.zeros_like(extra_ref)
    for i, pack in enumerate(packs):
        rows_ref[i * s.main : (i + 1) * s.main, :] = read(pack, 0, s.depth)
        tail_ref[...] = read(pack, s.depth, s.width).astype(F32)
        unfold(tail_ref, extra_ref, i * s.extra, s)
    rows_ref[s.blocks * s.main :, :] = extra_ref[...].astype(BF16)


def put(outs, i, at, value, s):
    if i < s.count:
        outs[i][:, at] = value
        return
    n = (len(outs) - s.count) // (s.blocks - s.count)
    rows = s.main // n
    for h in range(n):
        outs[s.count + (i - s.count) * n + h][:, at] = value[h * rows : (h + 1) * rows]


def scatter_chunk(value, outs, extra_ref, at, s):
    for i in range(s.blocks):
        put(outs, i, at, value[i * s.main : (i + 1) * s.main].astype(BF16), s)
    extra_ref[:, at] = value[s.blocks * s.main :].astype(F32)


def scatter_tails(outs, extra_ref, tail_ref, s):
    for i in range(s.blocks):
        fold(extra_ref, i * s.extra, tail_ref, s)
        put(outs, i, slice(s.depth, s.width), tail_ref[...].astype(BF16), s)


def chunk_of(depth):
    for chunk in (512, 256, 128):
        if depth % chunk == 0:
            return chunk


def forward_kernel(s, *refs):
    n = s.slices * (1 + (s.count - 1) * PIECES)
    packs = grouped(refs[:n], s, PIECES)
    wg, wu, wd = refs[n : n + 3]
    outs = refs[n + 3 : -3]
    rows_ref, extra_ref, tail_ref = refs[-3:]
    chunk = chunk_of(s.depth)
    gather_packs(packs, rows_ref, extra_ref, tail_ref, s)
    g = u = None
    for c in range(0, s.depth, chunk):
        lhs = rows_ref[:, c : c + chunk]
        more_g = jnp.dot(lhs, wg[c : c + chunk, :], preferred_element_type=F32)
        more_u = jnp.dot(lhs, wu[c : c + chunk, :], preferred_element_type=F32)
        g = more_g if g is None else g + more_g
        u = more_u if u is None else u + more_u
    hidden = (g * jax.nn.sigmoid(g) * u).astype(BF16)
    tail_ref[...] = jnp.zeros_like(tail_ref)
    for c in range(0, s.depth, chunk):
        part = jnp.dot(hidden, wd[:, c : c + chunk], preferred_element_type=F32)
        scatter_chunk(part, outs, extra_ref, slice(c, c + chunk), s)
    scatter_tails(outs, extra_ref, tail_ref, s)


def saved_kernel(s, gate_ref, up_ref, c1_ref, c2_ref, hb_ref, g_ref, u_ref):
    me = lax.axis_index("expert")
    e, j = me // s.slices, me % s.slices
    g_ref[...] = jnp.zeros_like(g_ref)
    u_ref[...] = jnp.zeros_like(u_ref)
    for i in range(s.blocks):
        k, d = i // s.count, i % s.count
        source = (e + s.count - d) % s.count * s.slices + (j + s.slices - k) % s.slices
        for src, dst in ((gate_ref, g_ref), (up_ref, u_ref)):
            rows = src[source].astype(F32)
            dst[i * s.main : (i + 1) * s.main, :] = rows[: s.main]
            first = s.blocks * s.main + i * s.extra
            dst[first : first + s.extra, :] = rows[s.main :]
    g = g_ref[...]
    u = u_ref[...]
    sig = jax.nn.sigmoid(g)
    c1_ref[...] = (u * sig * (1.0 + g * (1.0 - sig))).T
    c2_ref[...] = (g * sig).T
    hb_ref[...] = (g * sig * u).astype(BF16).astype(F32).T


def split_three(value):
    high = value.astype(BF16).astype(F32)
    rest = value - high
    mid = rest.astype(BF16).astype(F32)
    return high, mid, (rest - mid).astype(BF16).astype(F32)


def put_inner(main, extra, s):
    lane = iota((s.main, LANES), 1)
    row = iota((s.main, LANES), 0)
    out = jnp.zeros((s.main, LANES), F32)
    for p, piece in enumerate(split_three(main)):
        out = jnp.where(lane == float(p), piece, out)
    for j in range(s.extra):
        for p, piece in enumerate(split_three(extra[j])):
            out = jnp.where((lane == float(3 + p)) & (row == float(j)), piece, out)
    return out.astype(BF16)


def get_inner(block, s):
    lane = iota((s.main, LANES), 1)
    row = iota((s.main, LANES), 0)
    main = jnp.sum(jnp.where(lane < 3.0, block, 0.0), axis=1, keepdims=True)
    second = jnp.sum(
        jnp.where((lane >= 3.0) & (lane < 6.0), block, 0.0), axis=1, keepdims=True
    )
    extra = [
        jnp.sum(jnp.where(row[:, :1] == float(j), second, 0.0), axis=0, keepdims=True)
        for j in range(s.extra)
    ]
    return main, extra


def backward_kernel(s, *refs):
    packs = grouped(refs[: s.blocks], s, 1)
    c1, c2, hb, wg, wu, wd = refs[s.blocks : s.blocks + 6]
    outs = refs[s.blocks + 6 : -3]
    rows_ref, extra_ref, tail_ref = refs[-3:]
    chunk = chunk_of(s.depth)
    gather_packs(packs, rows_ref, extra_ref, tail_ref, s)
    a = None
    for c in range(0, s.depth, chunk):
        more = lax.dot_general(
            wd[:, c : c + chunk], rows_ref[:, c : c + chunk], NT, preferred_element_type=F32
        )
        a = more if a is None else a + more
    dgp = (a * c1[...]).astype(BF16)
    dup = (a * c2[...]).astype(BF16)
    inner = as_column(jnp.sum(a * hb[...], axis=0, keepdims=True))
    for i in range(s.blocks):
        first = s.blocks * s.main + i * s.extra
        outs[i][:, s.width :] = put_inner(
            inner[i * s.main : (i + 1) * s.main],
            [inner[first + j : first + j + 1] for j in range(s.extra)],
            s,
        )
    tail_ref[...] = jnp.zeros_like(tail_ref)
    for c in range(0, s.depth, chunk):
        part = jnp.dot(wg[c : c + chunk, :], dgp, preferred_element_type=F32) + jnp.dot(
            wu[c : c + chunk, :], dup, preferred_element_type=F32
        )
        scatter_chunk(part.astype(BF16).T, outs, extra_ref, slice(c, c + chunk), s)
    scatter_tails(outs, extra_ref, tail_ref, s)


def total_of(parts, d, s):
    total = parts[d][...].astype(F32)
    n = (len(parts) - s.count) // (s.blocks - s.count)
    for i in range(s.count + d, s.blocks, s.count):
        first = s.count + (i - s.count) * n
        found = [part[...].astype(F32) for part in parts[first : first + n]]
        total = total + (found[0] if n == 1 else jnp.concatenate(found, axis=0))
    return total


def forward_sum_kernel(s, *refs):
    n = s.count + (s.blocks - s.count) * PIECES
    parts, bases = refs[:n], grouped(refs[n : n + 1 + (s.count - 1) * PIECES], s, PIECES)
    route_ref, outs = refs[-1 - s.count], refs[-s.count :]
    for d in range(s.count - 1, -1, -1):
        tail = read(bases[d], s.depth, s.depth + LANES).astype(F32)
        main, extra = get_gates(tail, s)
        add_gated(outs[d], bases[d], main, extra, total_of(parts, d, s), s)
        spare = outs[d].shape[1] - s.width
        if spare:
            outs[d][:, s.width :] = jnp.zeros((s.main, spare), BF16)
    at = s.folds
    outs[0][at : at + 1, s.depth : s.depth + s.tok] = route_ref[...].astype(F32).astype(BF16)


def tokens_of(packs, route_row, rows_ref, extra_ref, tail_ref, s):
    extra_ref[...] = jnp.zeros_like(extra_ref)
    for d, pack in enumerate(packs):
        rows_ref[d * s.main : (d + 1) * s.main, :] = pack[:, : s.depth]
        tail_ref[...] = pack[:, s.depth : s.width].astype(F32)
        unfold(tail_ref, extra_ref, d * s.extra, s)
    rows_ref[s.count * s.main :, :] = extra_ref[...].astype(BF16)
    col, rank = slot_columns(route_row, s)
    high = rows_ref.shape[0]
    place = jnp.full((s.tok, 1), -1.0, F32)
    for d in range(s.count):
        at = jnp.where(
            rank < float(s.main),
            rank + float(d * s.main),
            rank + float(s.count * s.main + d * s.extra - s.main),
        )
        place = jnp.where(col == expert_at(s, d), at, place)
    table = jnp.where(place == iota((s.tok, high), 1), 1.0, 0.0).astype(BF16)
    return jnp.dot(table, rows_ref[...], preferred_element_type=F32)


def forward_end_kernel(s, *refs):
    packs = refs[: s.count]
    out_ref, rows_ref, extra_ref, tail_ref, row_ref = refs[s.count :]
    row_ref[...] = packs[0][:, s.depth : s.depth + LANES].astype(F32)
    route_row = row_ref[s.folds : s.folds + 1, : s.tok]
    out_ref[...] = tokens_of(packs, route_row, rows_ref, extra_ref, tail_ref, s).astype(BF16)


def backward_sum_kernel(s, *refs):
    parts, outs = refs[: -s.count], refs[-s.count :]
    for d in range(s.count - 1, -1, -1):
        total = total_of(parts, d, s)
        outs[d][:, : s.width] = total[:, : s.width].astype(BF16)
        main, extra = get_inner(total[:, s.width :], s)
        outs[d][:, s.width :] = put_inner(main, extra, s)


def backward_end_kernel(s, *refs):
    packs = refs[: s.count]
    dy_ref, route_ref, score_ref, out_ref, grad_ref = refs[s.count : s.count + 5]
    rows_ref, extra_ref, tail_ref = refs[s.count + 5 :]
    route_row = route_ref[...].astype(F32)
    rows = tokens_of(packs, route_row, rows_ref, extra_ref, tail_ref, s)
    gate = as_column(2.5 * score_ref[...])
    out_ref[...] = (dy_ref[...].astype(F32) + gate * rows).astype(BF16)
    rank = slot_rows(route_row, s)
    dgate = jnp.zeros((1, s.tok), F32)
    for d in range(s.count):
        hit = route_row == expert_at(s, d)
        main, extra = get_inner(packs[d][:, s.width :].astype(F32), s)
        dgate += jnp.sum(
            jnp.where(hit & (rank == iota((s.main, s.tok), 0)), main, 0.0), axis=0, keepdims=True
        )
        for j in range(s.extra):
            dgate += jnp.where(hit & (rank == float(s.main + j)), extra[j], 0.0)
    grad_ref[...] = 2.5 * dgate


VMEM = pl.BlockSpec(memory_space=pltpu.VMEM)
HBM = pl.BlockSpec(memory_space=pltpu.HBM)


def call(kernel, name, outs, scratch, ins, *args, mib=16):
    shapes = [jax.ShapeDtypeStruct(shape, kind) for shape, kind in outs]
    args = [
        pltpu.with_memory_space_constraint(a, pltpu.HBM) if spec is HBM else a
        for a, spec in zip(args, ins)
    ]
    return pl.pallas_call(
        kernel,
        out_shape=shapes,
        in_specs=ins,
        out_specs=[VMEM] * len(shapes),
        scratch_shapes=scratch,
        compiler_params=pltpu.CompilerParams(vmem_limit_bytes=mib << 20),
        cost_estimate=pl.CostEstimate(flops=0, bytes_accessed=0, transcendentals=0),
        name=name,
    )(*args)


def tail_scratch(s, rows):
    return [
        pltpu.VMEM((rows, s.depth), F32),
        pltpu.VMEM((s.main, LANES * s.extra), F32),
    ]


def load(*arrays):
    return call(
        load_kernel,
        "load",
        [(a.shape, a.dtype) for a in arrays],
        [pltpu.SemaphoreType.DMA((len(arrays),))],
        [HBM] * len(arrays),
        *arrays,
    )


def row_scratch(s):
    return [pltpu.VMEM((s.rows, s.depth), BF16), *tail_scratch(s, s.tail_rows)]


def cross(s, packs, pieces):
    return [packs[0]] + [across(p, 1 + i // pieces, s) for i, p in enumerate(packs[1:])]


def spread(s, got):
    return list(got) + [beside(b, k, s) for k in range(1, s.slices) for b in got]


def hold(values, *after):
    return lax.optimization_barrier((values, after))[0]


def parts_shape(s, width, pieces):
    kept = [((s.main, width), BF16)] * s.count
    return kept + [((s.main // pieces, width), BF16)] * ((s.blocks - s.count) * pieces)


def gather_parts(s, parts):
    n = (len(parts) - s.count) // (s.blocks - s.count)
    moved = [beside(p, -(i // n // s.count + 1), s) for i, p in enumerate(parts[s.count :])]
    return list(parts[: s.count]) + moved


def step(routes, run, *args):
    like = jax.eval_shape(run, *args)
    skip = lambda *_: jax.tree.map(lambda a: jnp.zeros(a.shape, a.dtype), like)
    return lax.cond(routes[0, 0] < EXPERTS, run, skip, *args)


def end_scratch(s):
    low = -(-(s.count * s.extra) // 16) * 16
    return [pltpu.VMEM((s.count * s.main + low, s.depth), BF16), *tail_scratch(s, low)]


def body(
    x_fwd,
    saved_gate,
    saved_up,
    grad_next,
    routes_fwd,
    routes_bwd,
    scores_fwd,
    scores_bwd,
    w_gate,
    w_up,
    w_down,
):
    groups = lax.axis_size("expert")
    tok, depth = x_fwd.shape[1:]
    s = Sizes(saved_gate.shape[2], depth, EXPERTS, groups // EXPERTS, tok)
    hidden = w_gate.shape[2]
    route_a = routes_fwd.reshape(1, tok)
    route_b = routes_bwd.reshape(1, tok)
    score_a = scores_fwd.reshape(1, tok)
    score_b = scores_bwd.reshape(1, tok)

    packed = [((s.main, s.width), BF16)] * s.count
    sent_a = call(
        functools.partial(first_kernel, s),
        "first",
        packed[:1] + [((s.main, s.width // PIECES), BF16)] * (PIECES * (s.count - 1)),
        [
            pltpu.VMEM((1, tok), jnp.int32),
            pltpu.VMEM((1, tok), F32),
            pltpu.VMEM((tok, depth), BF16),
            *tail_scratch(s, 16),
            pltpu.SemaphoreType.DMA((3,)),
        ],
        [HBM] * 3,
        route_a,
        score_a,
        x_fwd[0],
    )
    upstream = from_behind(grad_next, "section", -1)[0]
    wg, wu, wd, route_a, route_b, score_b = load(
        w_gate[0], w_up[0], w_down[0], route_a, route_b, score_b
    )
    factors = call(
        functools.partial(saved_kernel, s),
        "saved",
        [((hidden, s.rows), F32)] * 3,
        [pltpu.VMEM((s.rows, hidden), F32)] * 2,
        [VMEM] * 2,
        saved_gate[0],
        saved_up[0],
    )
    wide = s.width + LANES

    def backward(got, *rest):
        parts = call(
            functools.partial(backward_kernel, s),
            "backward",
            [((s.main, wide), BF16)] * s.blocks,
            row_scratch(s),
            [VMEM] * (s.blocks + 6),
            *spread(s, got),
            *rest,
        )
        sums = call(
            functools.partial(backward_sum_kernel, s),
            "backward_sum",
            [((s.main, wide), BF16)] * s.count,
            [],
            [VMEM] * s.blocks,
            *gather_parts(s, parts),
        )
        return tuple(sums)

    got = cross(s, sent_a, PIECES)
    got[1:] = hold(got[1:], route_a, factors)
    rows_a = spread(s, got)
    sent_b = call(
        functools.partial(pack_kernel, s),
        "pack",
        packed,
        tail_scratch(s, 16),
        [VMEM] * 2,
        route_b,
        hold(upstream, got[1:]),
    )
    got_b = cross(s, sent_b, 1)
    parts_a = call(
        functools.partial(forward_kernel, s),
        "forward",
        parts_shape(s, s.width, PIECES),
        row_scratch(s),
        [VMEM] * (len(rows_a) + 3),
        *hold(rows_a, sent_b),
        wg,
        wu,
        wd,
    )
    parts_a = gather_parts(s, parts_a)
    sums_a = call(
        functools.partial(forward_sum_kernel, s),
        "forward_sum",
        [((s.main, wide), BF16)] * s.count,
        [],
        [VMEM] * (len(parts_a) + len(got) + 1),
        *parts_a,
        *got,
        route_a,
    )
    moved = [to_next(y, -d, s) for d, y in enumerate(sums_a)]
    got_b[1:] = hold(got_b[1:], sums_a)
    sums_b = step(route_b, backward, got_b, *factors, wg, wu, wd)
    back_b = [sums_b[0]] + [across(sums_b[d], -d, s) for d in range(1, s.count)]
    next_input = call(
        functools.partial(forward_end_kernel, s),
        "forward_end",
        [((tok, depth), BF16)],
        end_scratch(s) + [pltpu.VMEM((s.main, LANES), F32)],
        [VMEM] * s.count,
        *moved,
    )[0]
    input_grad, score_grad = call(
        functools.partial(backward_end_kernel, s),
        "backward_end",
        [((tok, depth), BF16), ((1, tok), F32)],
        end_scratch(s),
        [VMEM] * (s.count + 3),
        *hold(back_b, next_input),
        upstream,
        route_b,
        score_b,
    )
    return next_input[None], input_grad[None], score_grad.reshape(1, tok, 1)


def solution(mesh):
    placed = (
        P("section", "expert", None),
        P("section", None, None, "expert"),
        P("section", None, None, "expert"),
        P("section", "expert", None),
        P("section", "expert", None),
        P("section", "expert", None),
        P("section", "expert", None),
        P("section", "expert", None),
        P("section", None, "expert"),
        P("section", None, "expert"),
        P("section", "expert", None),
    )
    return jax.shard_map(
        body,
        mesh=mesh,
        in_specs=placed,
        out_specs=(
            P("section", "expert", None),
            P("section", "expert", None),
            P("section", "expert", None),
        ),
        check_vma=False,
    )
```

```python
import functools

import jax
import jax.numpy as jnp
from jax import lax
from jax.experimental import pallas as pl
from jax.experimental.pallas import tpu as pltpu
from jax.sharding import PartitionSpec as P

EXPERTS = 2
LANES = 128
PIECES = 2
F32 = jnp.float32
BF16 = jnp.bfloat16
NT = (((1,), (1,)), ((), ()))


class Sizes:
    def __init__(self, cap, depth, count, slices, tok):
        self.cap, self.depth, self.count, self.slices, self.tok = cap, depth, count, slices, tok
        self.main = cap // 16 * 16
        self.extra = cap - self.main
        self.folds = depth // LANES
        assert self.folds + 4 <= self.main and depth % LANES == 0
        assert max(cap, tok) <= LANES
        self.width = depth + LANES * self.extra
        self.blocks = count * slices
        self.tail_rows = -(-(self.blocks * self.extra) // 16) * 16
        self.rows = self.blocks * self.main + self.tail_rows


def from_behind(block, axis, distance):
    devices = range(lax.axis_size(axis))
    route = [((i - distance) % len(devices), i) for i in devices]
    return lax.ppermute(block, axis, route)


def to_next(block, distance, s):
    sections, own = lax.axis_size("section"), s.count * s.slices
    route = [
        (
            l * own + e * s.slices + j,
            (l + 1) % sections * own + (e + distance) % s.count * s.slices + j,
        )
        for l in range(sections)
        for e in range(s.count)
        for j in range(s.slices)
    ]
    return lax.ppermute(block, ("section", "expert"), route)


def across(block, distance, s):
    route = [
        (e * s.slices + j, (e + distance) % s.count * s.slices + j)
        for e in range(s.count)
        for j in range(s.slices)
    ]
    return lax.ppermute(block, "expert", route)


def beside(block, distance, s):
    route = [
        (e * s.slices + j, e * s.slices + (j + distance) % s.slices)
        for e in range(s.count)
        for j in range(s.slices)
    ]
    return lax.ppermute(block, "expert", route)


def iota(shape, dim):
    return lax.broadcasted_iota(jnp.int32, shape, dim).astype(F32)


def as_column(row):
    n = row.shape[1]
    return jnp.sum(
        jnp.where(iota((n, n), 0) == iota((n, n), 1), row, 0.0), axis=1, keepdims=True
    )


def own_expert(s):
    return lax.axis_index("expert") // s.slices


def expert_at(s, distance):
    return ((own_expert(s) + distance) % s.count).astype(F32)


def slot_rows(route_row, s):
    col = as_column(route_row)
    n = s.tok
    same = (col == route_row) & (iota((n, n), 0) < iota((n, n), 1))
    return jnp.sum(jnp.where(same, 1.0, 0.0), axis=0, keepdims=True)


def slot_columns(route_row, s):
    col = as_column(route_row)
    n = s.tok
    same = (col == route_row) & (iota((n, n), 1) < iota((n, n), 0))
    return col, jnp.sum(jnp.where(same, 1.0, 0.0), axis=1, keepdims=True)


def fold(values_ref, first, tail_ref, s):
    for j in range(s.extra):
        for r in range(s.folds):
            tail_ref[r : r + 1, j * LANES : (j + 1) * LANES] = values_ref[
                first + j : first + j + 1, r * LANES : (r + 1) * LANES
            ]


def unfold(tail_ref, values_ref, first, s):
    for j in range(s.extra):
        for r in range(s.folds):
            values_ref[first + j : first + j + 1, r * LANES : (r + 1) * LANES] = tail_ref[
                r : r + 1, j * LANES : (j + 1) * LANES
            ]


def put_scores(route_row, score_row, expert, tail_ref, s):
    col, rank = slot_columns(route_row, s)
    hit = (col == expert) & (rank == iota((s.tok, LANES), 1))
    row = jnp.sum(jnp.where(hit, as_column(score_row), 0.0), axis=0, keepdims=True)
    put_row(row, tail_ref, s)


def add_gated(out_ref, base, main, extra, total, s):
    d = s.depth
    out_ref[:, :d] = (read(base, 0, d).astype(F32) + main * total[:, :d]).astype(BF16)
    for j in range(s.extra):
        at = slice(d + j * LANES, d + (j + 1) * LANES)
        value = read(base, at.start, at.stop).astype(F32) + extra[j] * total[:, at]
        out_ref[:, at] = value.astype(BF16)


def read(pieces, low, high):
    found, at = [], 0
    for piece in pieces:
        width = piece.shape[1]
        a, b = max(low, at), min(high, at + width)
        if a < b:
            found.append(piece[:, a - at : b - at])
        at += width
    return found[0] if len(found) == 1 else jnp.concatenate(found, axis=1)


def write(pieces, low, value):
    at = 0
    for piece in pieces:
        width = piece.shape[1]
        a, b = max(low, at), min(low + value.shape[1], at + width)
        if a < b:
            piece[:, a - at : b - at] = value[:, a - low : b - low]
        at += width


def grouped(refs, s, pieces):
    one = 1 + (s.count - 1) * pieces
    packs = []
    for first in range(0, len(refs), one):
        packs.append(refs[first : first + 1])
        for at in range(first + 1, first + one, pieces):
            packs.append(refs[at : at + pieces])
    return packs


def pack_rows(s, route_row, x, outs, extra_ref, tail_ref, score_row=None):
    rank = slot_rows(route_row, s)
    slots = iota((s.main + 16, s.tok), 0)
    tail_ref[...] = jnp.zeros_like(tail_ref)
    for d in range(s.count):
        hit = route_row == expert_at(s, d)
        table = jnp.where(hit & (rank == slots), 1.0, 0.0).astype(BF16)
        rows = jnp.dot(table, x, preferred_element_type=F32)
        write(outs[d], 0, rows[: s.main].astype(BF16))
        extra_ref[...] = rows[s.main :]
        fold(extra_ref, 0, tail_ref, s)
        if score_row is not None:
            put_scores(route_row, score_row, expert_at(s, d), tail_ref, s)
        write(outs[d], s.depth, tail_ref[...].astype(BF16))


def first_kernel(s, route_hbm, score_hbm, x_hbm, *rest):
    outs = grouped(rest[:-6], s, PIECES)
    route_ref, score_ref, x_ref, extra_ref, tail_ref, sems = rest[-6:]
    copies = [
        pltpu.make_async_copy(src, dst, sems.at[i])
        for i, (src, dst) in enumerate(
            ((route_hbm, route_ref), (score_hbm, score_ref), (x_hbm, x_ref))
        )
    ]
    for copy in copies:
        copy.start()
    for copy in copies:
        copy.wait()
    route_row = route_ref[...].astype(F32)
    pack_rows(s, route_row, x_ref[...], outs, extra_ref, tail_ref, score_ref[...])


def pack_kernel(s, route_ref, x_ref, *rest):
    outs, (extra_ref, tail_ref) = grouped(rest[:-2], s, 1), rest[-2:]
    pack_rows(s, route_ref[...].astype(F32), x_ref[...], outs, extra_ref, tail_ref)


def load_kernel(*refs):
    sems = refs[-1]
    n = (len(refs) - 1) // 2
    copies = [pltpu.make_async_copy(refs[i], refs[n + i], sems.at[i]) for i in range(n)]
    for copy in copies:
        copy.start()
    for copy in copies:
        copy.wait()


def gather_packs(packs, rows_ref, extra_ref, tail_ref, s):
    extra_ref[...] = jnp.zeros_like(extra_ref)
    for i, pack in enumerate(packs):
        rows_ref[i * s.main : (i + 1) * s.main, :] = read(pack, 0, s.depth)
        tail_ref[...] = read(pack, s.depth, s.width).astype(F32)
        unfold(tail_ref, extra_ref, i * s.extra, s)
    rows_ref[s.blocks * s.main :, :] = extra_ref[...].astype(BF16)


def put(outs, i, at, value, s):
    if i < s.count:
        outs[i][:, at] = value
        return
    n = (len(outs) - s.count) // (s.blocks - s.count)
    rows = s.main // n
    for h in range(n):
        outs[s.count + (i - s.count) * n + h][:, at] = value[h * rows : (h + 1) * rows]


def scatter_chunk(value, outs, extra_ref, at, s):
    for i in range(s.blocks):
        put(outs, i, at, value[i * s.main : (i + 1) * s.main].astype(BF16), s)
    extra_ref[:, at] = value[s.blocks * s.main :]


def scatter_tails(outs, extra_ref, tail_ref, s, inner=None):
    for i in range(s.blocks):
        fold(extra_ref, i * s.extra, tail_ref, s)
        if inner is not None:
            first = s.blocks * s.main + i * s.extra
            extra = [inner[first + j : first + j + 1] for j in range(s.extra)]
            put_inner(inner[i * s.main : (i + 1) * s.main], extra, tail_ref, s)
        put(outs, i, slice(s.depth, s.width), tail_ref[...].astype(BF16), s)


def chunk_of(depth):
    for chunk in (512, 256, 128):
        if depth % chunk == 0:
            return chunk


def forward_kernel(s, *refs):
    n = s.slices * (1 + (s.count - 1) * PIECES)
    packs = grouped(refs[:n], s, PIECES)
    wg, wu, wd = refs[n : n + 3]
    outs = refs[n + 3 : -3]
    rows_ref, extra_ref, tail_ref = refs[-3:]
    chunk = chunk_of(s.depth)
    gather_packs(packs, rows_ref, extra_ref, tail_ref, s)
    g = u = None
    for c in range(0, s.depth, chunk):
        lhs = rows_ref[:, c : c + chunk]
        more_g = jnp.dot(lhs, wg[c : c + chunk, :], preferred_element_type=F32)
        more_u = jnp.dot(lhs, wu[c : c + chunk, :], preferred_element_type=F32)
        g = more_g if g is None else g + more_g
        u = more_u if u is None else u + more_u
    hidden = (g * jax.nn.sigmoid(g) * u).astype(BF16)
    tail_ref[...] = jnp.zeros_like(tail_ref)
    for c in range(0, s.depth, chunk):
        part = jnp.dot(hidden, wd[:, c : c + chunk], preferred_element_type=F32)
        scatter_chunk(part, outs, extra_ref, slice(c, c + chunk), s)
    scatter_tails(outs, extra_ref, tail_ref, s)


def saved_kernel(s, gate_ref, up_ref, c1_ref, c2_ref, hb_ref, g_ref, u_ref):
    me = lax.axis_index("expert")
    e, j = me // s.slices, me % s.slices
    g_ref[...] = jnp.zeros_like(g_ref)
    u_ref[...] = jnp.zeros_like(u_ref)
    for i in range(s.blocks):
        k, d = i // s.count, i % s.count
        source = (e + s.count - d) % s.count * s.slices + (j + s.slices - k) % s.slices
        for src, dst in ((gate_ref, g_ref), (up_ref, u_ref)):
            rows = src[source].astype(F32)
            dst[i * s.main : (i + 1) * s.main, :] = rows[: s.main]
            first = s.blocks * s.main + i * s.extra
            dst[first : first + s.extra, :] = rows[s.main :]
    g = g_ref[...]
    u = u_ref[...]
    sig = jax.nn.sigmoid(g)
    c1_ref[...] = u * sig * (1.0 + g * (1.0 - sig))
    c2_ref[...] = g * sig
    hb_ref[...] = (g * sig * u).astype(BF16).astype(F32)


def split_three(value):
    high = value.astype(BF16).astype(F32)
    rest = value - high
    mid = rest.astype(BF16).astype(F32)
    return high, mid, (rest - mid).astype(BF16).astype(F32)


def put_inner(main, extra, tail_ref, s):
    lane = iota((s.main, LANES), 1)
    row = jnp.sum(jnp.where(lane == iota((s.main, LANES), 0), main, 0.0), axis=0, keepdims=True)
    for j in range(s.extra):
        row = jnp.where(lane[:1] == float(s.main + j), extra[j], row)
    put_row(row, tail_ref, s)


def put_row(row, tail_ref, s):
    for p, piece in enumerate(split_three(row)):
        at = s.folds + 1 + p
        tail_ref[at : at + 1, :LANES] = piece


def get_row(tail, s):
    at = s.folds + 1
    return tail[at : at + 1] + tail[at + 1 : at + 2] + tail[at + 2 : at + 3]


def get_slots(row, s):
    lane = iota((s.main, LANES), 1)
    main = jnp.sum(jnp.where(lane == iota((s.main, LANES), 0), row, 0.0), axis=1, keepdims=True)
    extra = [
        jnp.sum(jnp.where(lane[:1] == float(s.main + j), row, 0.0), axis=1, keepdims=True)
        for j in range(s.extra)
    ]
    return main, extra


def backward_kernel(s, *refs):
    packs = grouped(refs[: s.blocks], s, 1)
    c1, c2, hb, wg, wu, wd = refs[s.blocks : s.blocks + 6]
    outs = refs[s.blocks + 6 : -3]
    rows_ref, extra_ref, tail_ref = refs[-3:]
    chunk = chunk_of(s.depth)
    gather_packs(packs, rows_ref, extra_ref, tail_ref, s)
    a = None
    for c in range(0, s.depth, chunk):
        more = lax.dot_general(
            rows_ref[:, c : c + chunk], wd[:, c : c + chunk], NT, preferred_element_type=F32
        )
        a = more if a is None else a + more
    dgp = (a * c1[...]).astype(BF16)
    dup = (a * c2[...]).astype(BF16)
    inner = jnp.sum(a * hb[...], axis=1, keepdims=True)
    tail_ref[...] = jnp.zeros_like(tail_ref)
    for c in range(0, s.depth, chunk):
        part = lax.dot_general(
            dgp, wg[c : c + chunk, :], NT, preferred_element_type=F32
        ) + lax.dot_general(dup, wu[c : c + chunk, :], NT, preferred_element_type=F32)
        scatter_chunk(part, outs, extra_ref, slice(c, c + chunk), s)
    scatter_tails(outs, extra_ref, tail_ref, s, inner)


def total_of(parts, d, s):
    total = parts[d][...].astype(F32)
    n = (len(parts) - s.count) // (s.blocks - s.count)
    for i in range(s.count + d, s.blocks, s.count):
        first = s.count + (i - s.count) * n
        found = [part[...].astype(F32) for part in parts[first : first + n]]
        total = total + (found[0] if n == 1 else jnp.concatenate(found, axis=0))
    return total


def forward_sum_kernel(s, *refs):
    n = s.count + (s.blocks - s.count) * PIECES
    parts, bases = refs[:n], grouped(refs[n : n + 1 + (s.count - 1) * PIECES], s, PIECES)
    route_ref, outs = refs[-1 - s.count], refs[-s.count :]
    for d in range(s.count - 1, -1, -1):
        tail = read(bases[d], s.depth, s.depth + LANES).astype(F32)
        main, extra = get_slots(2.5 * get_row(tail, s), s)
        add_gated(outs[d], bases[d], main, extra, total_of(parts, d, s), s)
        spare = outs[d].shape[1] - s.width
        if spare:
            outs[d][:, s.width :] = jnp.zeros((s.main, spare), BF16)
    at = s.folds
    outs[0][at : at + 1, s.depth : s.depth + s.tok] = route_ref[...].astype(F32).astype(BF16)


def tokens_of(packs, route_row, rows_ref, extra_ref, tail_ref, s):
    extra_ref[...] = jnp.zeros_like(extra_ref)
    for d, pack in enumerate(packs):
        rows_ref[d * s.main : (d + 1) * s.main, :] = pack[:, : s.depth].astype(BF16)
        tail_ref[...] = pack[:, s.depth : s.width].astype(F32)
        unfold(tail_ref, extra_ref, d * s.extra, s)
    rows_ref[s.count * s.main :, :] = extra_ref[...].astype(BF16)
    col, rank = slot_columns(route_row, s)
    high = rows_ref.shape[0]
    place = jnp.full((s.tok, 1), -1.0, F32)
    for d in range(s.count):
        at = jnp.where(
            rank < float(s.main),
            rank + float(d * s.main),
            rank + float(s.count * s.main + d * s.extra - s.main),
        )
        place = jnp.where(col == expert_at(s, d), at, place)
    table = jnp.where(place == iota((s.tok, high), 1), 1.0, 0.0).astype(BF16)
    return jnp.dot(table, rows_ref[...], preferred_element_type=F32)


def forward_end_kernel(s, *refs):
    packs = refs[: s.count]
    out_ref, rows_ref, extra_ref, tail_ref, row_ref = refs[s.count + 1 :]
    row_ref[...] = packs[0][:, s.depth : s.depth + LANES].astype(F32)
    route_row = row_ref[s.folds : s.folds + 1, : s.tok]
    out_ref[...] = tokens_of(packs, route_row, rows_ref, extra_ref, tail_ref, s).astype(BF16)


def backward_sum_kernel(s, *refs):
    n = s.count - 1
    parts, outs, tail_ref = refs[: n * s.slices], refs[-1 - n : -1], refs[-1]
    for d in range(n):
        total = parts[d][...].astype(F32)
        for part in parts[n + d :: n]:
            total = total + part[...].astype(F32)
        outs[d][:, : s.depth] = total[:, : s.depth].astype(BF16)
        tail_ref[...] = total[:, s.depth :]
        put_row(get_row(total[:, s.depth : s.depth + LANES], s), tail_ref, s)
        outs[d][:, s.depth :] = tail_ref[...].astype(BF16)


def backward_end_kernel(s, *refs):
    own, packs = refs[: s.slices], refs[s.slices : s.slices + s.count - 1]
    n = s.slices + s.count - 1
    dy_ref, route_ref, score_ref, out_ref, grad_ref, token_ref = refs[n : n + 6]
    rows_ref, extra_ref, tail_ref = refs[n + 6 :]
    token_ref[...] = jnp.zeros_like(token_ref)
    total = own[0][...].astype(F32)
    for part in own[1:]:
        total = total + part[...].astype(F32)
    packs = [total, *packs]
    route_row = route_ref[...].astype(F32)
    rows = tokens_of(packs, route_row, rows_ref, extra_ref, tail_ref, s)
    gate = as_column(2.5 * score_ref[...])
    out_ref[...] = (dy_ref[...].astype(F32) + gate * rows).astype(BF16)
    rank = slot_rows(route_row, s)
    dgate = jnp.zeros((1, s.tok), F32)
    for d in range(s.count):
        hit = route_row == expert_at(s, d)
        tail = packs[d][:, s.depth : s.depth + LANES].astype(F32)
        main, extra = get_slots(get_row(tail, s), s)
        dgate += jnp.sum(
            jnp.where(hit & (rank == iota((s.main, s.tok), 0)), main, 0.0), axis=0, keepdims=True
        )
        for j in range(s.extra):
            dgate += jnp.where(hit & (rank == float(s.main + j)), extra[j], 0.0)
    grad_ref[...] = 2.5 * dgate


VMEM = pl.BlockSpec(memory_space=pltpu.VMEM)
HBM = pl.BlockSpec(memory_space=pltpu.HBM)


def call(kernel, name, outs, scratch, ins, *args, mib=16):
    shapes = [jax.ShapeDtypeStruct(shape, kind) for shape, kind in outs]
    args = [
        pltpu.with_memory_space_constraint(a, pltpu.HBM) if spec is HBM else a
        for a, spec in zip(args, ins)
    ]
    return pl.pallas_call(
        kernel,
        out_shape=shapes,
        in_specs=ins,
        out_specs=[VMEM] * len(shapes),
        scratch_shapes=scratch,
        compiler_params=pltpu.CompilerParams(vmem_limit_bytes=mib << 20),
        cost_estimate=pl.CostEstimate(flops=0, bytes_accessed=0, transcendentals=0),
        name=name,
    )(*args)


def tail_scratch(s, rows):
    return [
        pltpu.VMEM((rows, s.depth), F32),
        pltpu.VMEM((s.main, LANES * s.extra), F32),
    ]


def load(*arrays):
    return call(
        load_kernel,
        "load",
        [(a.shape, a.dtype) for a in arrays],
        [pltpu.SemaphoreType.DMA((len(arrays),))],
        [HBM] * len(arrays),
        *arrays,
    )


def row_scratch(s):
    return [pltpu.VMEM((s.rows, s.depth), BF16), *tail_scratch(s, s.tail_rows)]


def cross(s, packs, pieces):
    return [packs[0]] + [across(p, 1 + i // pieces, s) for i, p in enumerate(packs[1:])]


def spread(s, got):
    return list(got) + [beside(b, k, s) for k in range(1, s.slices) for b in got]


def hold(values, *after):
    return lax.optimization_barrier((values, after))[0]


def parts_shape(s, width, pieces):
    kept = [((s.main, width), BF16)] * s.count
    return kept + [((s.main // pieces, width), BF16)] * ((s.blocks - s.count) * pieces)


def gather_parts(s, parts):
    n = (len(parts) - s.count) // (s.blocks - s.count)
    moved = [beside(p, -(i // n // s.count + 1), s) for i, p in enumerate(parts[s.count :])]
    return list(parts[: s.count]) + moved


def step(routes, run, *args):
    like = jax.eval_shape(run, *args)
    skip = lambda *_: jax.tree.map(lambda a: jnp.zeros(a.shape, a.dtype), like)
    return lax.cond(routes[0, 0] < EXPERTS, run, skip, *args)


def end_scratch(s):
    low = -(-(s.count * s.extra) // 16) * 16
    return [pltpu.VMEM((s.count * s.main + low, s.depth), BF16), *tail_scratch(s, low)]


def body(
    x_fwd,
    saved_gate,
    saved_up,
    grad_next,
    routes_fwd,
    routes_bwd,
    scores_fwd,
    scores_bwd,
    w_gate,
    w_up,
    w_down,
):
    groups = lax.axis_size("expert")
    tok, depth = x_fwd.shape[1:]
    s = Sizes(saved_gate.shape[2], depth, EXPERTS, groups // EXPERTS, tok)
    hidden = w_gate.shape[2]
    route_a = routes_fwd.reshape(1, tok)
    route_b = routes_bwd.reshape(1, tok)
    score_a = scores_fwd.reshape(1, tok)
    score_b = scores_bwd.reshape(1, tok)

    packed = [((s.main, s.width), BF16)] * s.count
    sent_a = call(
        functools.partial(first_kernel, s),
        "first",
        packed[:1] + [((s.main, s.width // PIECES), BF16)] * (PIECES * (s.count - 1)),
        [
            pltpu.VMEM((1, tok), jnp.int32),
            pltpu.VMEM((1, tok), F32),
            pltpu.VMEM((tok, depth), BF16),
            *tail_scratch(s, 16),
            pltpu.SemaphoreType.DMA((3,)),
        ],
        [HBM] * 3,
        route_a,
        score_a,
        x_fwd[0],
    )
    upstream = from_behind(grad_next, "section", -1)[0]
    wg, wu, wd, route_a, route_b, score_b = load(
        w_gate[0], w_up[0], w_down[0], route_a, route_b, score_b
    )
    factors = call(
        functools.partial(saved_kernel, s),
        "saved",
        [((s.rows, hidden), F32)] * 3,
        [pltpu.VMEM((s.rows, hidden), F32)] * 2,
        [VMEM] * 2,
        saved_gate[0],
        saved_up[0],
    )
    wide = s.width + LANES

    def backward(got, *rest):
        rows = spread(s, got)
        parts = call(
            functools.partial(backward_kernel, s),
            "backward",
            packed * s.slices,
            row_scratch(s),
            [VMEM] * (s.blocks + 6),
            *rows,
            *rest,
        )
        others = [p for i, p in enumerate(parts) if i % s.count]
        others = [beside(p, -(i // (s.count - 1)), s) if i >= s.count - 1 else p for i, p in enumerate(others)]
        sums = call(
            functools.partial(backward_sum_kernel, s),
            "backward_sum",
            packed[1:],
            [pltpu.VMEM((s.main, LANES * s.extra), F32)],
            [VMEM] * len(others),
            *others,
        )
        return tuple(parts[:: s.count]), tuple(sums)

    got = cross(s, sent_a, PIECES)
    got[1:] = hold(got[1:], route_a, factors)
    rows_a = spread(s, got)
    sent_b = call(
        functools.partial(pack_kernel, s),
        "pack",
        packed,
        tail_scratch(s, 16),
        [VMEM] * 2,
        route_b,
        hold(upstream, got[1:]),
    )
    got_b = cross(s, sent_b, 1)
    parts_a = call(
        functools.partial(forward_kernel, s),
        "forward",
        parts_shape(s, s.width, PIECES),
        row_scratch(s),
        [VMEM] * (len(rows_a) + 3),
        *hold(rows_a, sent_b),
        wg,
        wu,
        wd,
    )
    parts_a = gather_parts(s, parts_a)
    sums_a = call(
        functools.partial(forward_sum_kernel, s),
        "forward_sum",
        [((s.main, wide), BF16)] * s.count,
        [],
        [VMEM] * (len(parts_a) + len(got) + 1),
        *parts_a,
        *got,
        route_a,
    )
    moved = [to_next(y, -d, s) for d, y in enumerate(sums_a)]
    got_b[1:] = hold(got_b[1:], sums_a)
    own_b, sums_b = step(route_b, backward, got_b, *factors, wg, wu, wd)
    back_b = [across(y, -1 - d, s) for d, y in enumerate(sums_b)]
    own_b = [beside(p, -k, s) if k else p for k, p in enumerate(own_b)]
    input_grad, score_grad, token = call(
        functools.partial(backward_end_kernel, s),
        "backward_end",
        [((tok, depth), BF16), ((1, tok), F32), ((8, LANES), F32)],
        end_scratch(s),
        [VMEM] * (s.blocks // s.count + s.count - 1 + 3),
        *own_b,
        *back_b,
        upstream,
        route_b,
        score_b,
    )
    next_input = call(
        functools.partial(forward_end_kernel, s),
        "forward_end",
        [((tok, depth), BF16)],
        end_scratch(s) + [pltpu.VMEM((s.main, LANES), F32)],
        [VMEM] * (s.count + 1),
        *moved,
        token,
    )[0]
    return next_input[None], input_grad[None], score_grad.reshape(1, tok, 1)


def solution(mesh):
    placed = (
        P("section", "expert", None),
        P("section", None, None, "expert"),
        P("section", None, None, "expert"),
        P("section", "expert", None),
        P("section", "expert", None),
        P("section", "expert", None),
        P("section", "expert", None),
        P("section", "expert", None),
        P("section", None, "expert"),
        P("section", None, "expert"),
        P("section", "expert", None),
    )
    return jax.shard_map(
        body,
        mesh=mesh,
        in_specs=placed,
        out_specs=(
            P("section", "expert", None),
            P("section", "expert", None),
            P("section", "expert", None),
        ),
        check_vma=False,
    )
```

```python
import functools

import jax
import jax.numpy as jnp
from jax import lax
from jax.experimental import pallas as pl
from jax.experimental.pallas import tpu as pltpu
from jax.sharding import PartitionSpec as P

EXPERTS = 2
LANES = 128
PIECES = 2
F32 = jnp.float32
BF16 = jnp.bfloat16
NT = (((1,), (1,)), ((), ()))


class Sizes:
    def __init__(self, cap, depth, count, slices, tok):
        self.cap, self.depth, self.count, self.slices, self.tok = cap, depth, count, slices, tok
        self.main = cap // 16 * 16
        self.extra = cap - self.main
        self.folds = depth // LANES
        assert self.folds + 4 <= self.main and depth % LANES == 0
        assert max(cap, tok) <= LANES
        self.width = depth + LANES * self.extra
        self.blocks = count * slices
        self.tail_rows = -(-(self.blocks * self.extra) // 16) * 16
        self.rows = self.blocks * self.main + self.tail_rows


def from_behind(block, axis, distance):
    devices = range(lax.axis_size(axis))
    route = [((i - distance) % len(devices), i) for i in devices]
    return lax.ppermute(block, axis, route)


def to_next(block, distance, s):
    sections, own = lax.axis_size("section"), s.count * s.slices
    route = [
        (
            l * own + e * s.slices + j,
            (l + 1) % sections * own + (e + distance) % s.count * s.slices + j,
        )
        for l in range(sections)
        for e in range(s.count)
        for j in range(s.slices)
    ]
    return lax.ppermute(block, ("section", "expert"), route)


def across(block, distance, s):
    route = [
        (e * s.slices + j, (e + distance) % s.count * s.slices + j)
        for e in range(s.count)
        for j in range(s.slices)
    ]
    return lax.ppermute(block, "expert", route)


def beside(block, distance, s):
    route = [
        (e * s.slices + j, e * s.slices + (j + distance) % s.slices)
        for e in range(s.count)
        for j in range(s.slices)
    ]
    return lax.ppermute(block, "expert", route)


def iota(shape, dim):
    return lax.broadcasted_iota(jnp.int32, shape, dim).astype(F32)


def as_column(row):
    n = row.shape[1]
    return jnp.sum(
        jnp.where(iota((n, n), 0) == iota((n, n), 1), row, 0.0), axis=1, keepdims=True
    )


def own_expert(s):
    return lax.axis_index("expert") // s.slices


def expert_at(s, distance):
    return ((own_expert(s) + distance) % s.count).astype(F32)


def slot_rows(route_row, s):
    col = as_column(route_row)
    n = s.tok
    same = (col == route_row) & (iota((n, n), 0) < iota((n, n), 1))
    return jnp.sum(jnp.where(same, 1.0, 0.0), axis=0, keepdims=True)


def slot_columns(route_row, s):
    col = as_column(route_row)
    n = s.tok
    same = (col == route_row) & (iota((n, n), 1) < iota((n, n), 0))
    return col, jnp.sum(jnp.where(same, 1.0, 0.0), axis=1, keepdims=True)


def fold(values_ref, first, tail_ref, s):
    for j in range(s.extra):
        for r in range(s.folds):
            tail_ref[r : r + 1, j * LANES : (j + 1) * LANES] = values_ref[
                first + j : first + j + 1, r * LANES : (r + 1) * LANES
            ]


def unfold(tail_ref, values_ref, first, s):
    for j in range(s.extra):
        for r in range(s.folds):
            values_ref[first + j : first + j + 1, r * LANES : (r + 1) * LANES] = tail_ref[
                r : r + 1, j * LANES : (j + 1) * LANES
            ]


def put_scores(route_row, score_row, expert, tail_ref, s):
    col, rank = slot_columns(route_row, s)
    hit = (col == expert) & (rank == iota((s.tok, LANES), 1))
    row = jnp.sum(jnp.where(hit, as_column(score_row), 0.0), axis=0, keepdims=True)
    put_row(row, tail_ref, s)


def add_gated(out_ref, base, main, extra, total, s):
    d = s.depth
    out_ref[:, :d] = (read(base, 0, d).astype(F32) + main * total[:, :d]).astype(BF16)
    for j in range(s.extra):
        at = slice(d + j * LANES, d + (j + 1) * LANES)
        value = read(base, at.start, at.stop).astype(F32) + extra[j] * total[:, at]
        out_ref[:, at] = value.astype(BF16)


def read(pieces, low, high):
    found, at = [], 0
    for piece in pieces:
        width = piece.shape[1]
        a, b = max(low, at), min(high, at + width)
        if a < b:
            found.append(piece[:, a - at : b - at])
        at += width
    return found[0] if len(found) == 1 else jnp.concatenate(found, axis=1)


def write(pieces, low, value):
    at = 0
    for piece in pieces:
        width = piece.shape[1]
        a, b = max(low, at), min(low + value.shape[1], at + width)
        if a < b:
            piece[:, a - at : b - at] = value[:, a - low : b - low]
        at += width


def grouped(refs, s, pieces):
    one = 1 + (s.count - 1) * pieces
    packs = []
    for first in range(0, len(refs), one):
        packs.append(refs[first : first + 1])
        for at in range(first + 1, first + one, pieces):
            packs.append(refs[at : at + pieces])
    return packs


def pack_rows(s, route_row, x, outs, extra_ref, tail_ref, score_row=None):
    rank = slot_rows(route_row, s)
    slots = iota((s.main + 16, s.tok), 0)
    tail_ref[...] = jnp.zeros_like(tail_ref)
    for d in range(s.count):
        hit = route_row == expert_at(s, d)
        table = jnp.where(hit & (rank == slots), 1.0, 0.0).astype(BF16)
        rows = jnp.dot(table, x, preferred_element_type=F32)
        write(outs[d], 0, rows[: s.main].astype(BF16))
        extra_ref[...] = rows[s.main :]
        fold(extra_ref, 0, tail_ref, s)
        if score_row is not None:
            put_scores(route_row, score_row, expert_at(s, d), tail_ref, s)
        write(outs[d], s.depth, tail_ref[...].astype(BF16))


def first_kernel(s, route_hbm, score_hbm, x_hbm, *rest):
    outs = grouped(rest[:-6], s, PIECES)
    route_ref, score_ref, x_ref, extra_ref, tail_ref, sems = rest[-6:]
    copies = [
        pltpu.make_async_copy(src, dst, sems.at[i])
        for i, (src, dst) in enumerate(
            ((route_hbm, route_ref), (score_hbm, score_ref), (x_hbm, x_ref))
        )
    ]
    for copy in copies:
        copy.start()
    for copy in copies:
        copy.wait()
    route_row = route_ref[...].astype(F32)
    pack_rows(s, route_row, x_ref[...], outs, extra_ref, tail_ref, score_ref[...])


def pack_kernel(s, route_ref, x_ref, *rest):
    outs, (extra_ref, tail_ref) = grouped(rest[:-2], s, 1), rest[-2:]
    pack_rows(s, route_ref[...].astype(F32), x_ref[...], outs, extra_ref, tail_ref)


def load_kernel(*refs):
    sems = refs[-1]
    n = (len(refs) - 1) // 2
    copies = [pltpu.make_async_copy(refs[i], refs[n + i], sems.at[i]) for i in range(n)]
    for copy in copies:
        copy.start()
    for copy in copies:
        copy.wait()


def gather_packs(packs, rows_ref, extra_ref, tail_ref, s):
    extra_ref[...] = jnp.zeros_like(extra_ref)
    for i, pack in enumerate(packs):
        rows_ref[i * s.main : (i + 1) * s.main, :] = read(pack, 0, s.depth)
        tail_ref[...] = read(pack, s.depth, s.width).astype(F32)
        unfold(tail_ref, extra_ref, i * s.extra, s)
    rows_ref[s.blocks * s.main :, :] = extra_ref[...].astype(BF16)


def put(outs, i, at, value, s):
    if i < s.count:
        outs[i][:, at] = value
        return
    n = (len(outs) - s.count) // (s.blocks - s.count)
    rows = s.main // n
    for h in range(n):
        outs[s.count + (i - s.count) * n + h][:, at] = value[h * rows : (h + 1) * rows]


def scatter_chunk(value, outs, extra_ref, at, s):
    for i in range(s.blocks):
        put(outs, i, at, value[i * s.main : (i + 1) * s.main].astype(BF16), s)
    extra_ref[:, at] = value[s.blocks * s.main :]


def scatter_tails(outs, extra_ref, tail_ref, s, inner=None):
    for i in range(s.blocks):
        fold(extra_ref, i * s.extra, tail_ref, s)
        if inner is not None:
            first = s.blocks * s.main + i * s.extra
            extra = [inner[first + j : first + j + 1] for j in range(s.extra)]
            put_inner(inner[i * s.main : (i + 1) * s.main], extra, tail_ref, s)
        put(outs, i, slice(s.depth, s.width), tail_ref[...].astype(BF16), s)


def chunk_of(depth):
    for chunk in (512, 256, 128):
        if depth % chunk == 0:
            return chunk


def forward_kernel(s, *refs):
    n = s.slices * (1 + (s.count - 1) * PIECES)
    packs = grouped(refs[:n], s, PIECES)
    wg, wu, wd = refs[n : n + 3]
    outs = refs[n + 3 : -3]
    rows_ref, extra_ref, tail_ref = refs[-3:]
    chunk = chunk_of(s.depth)
    gather_packs(packs, rows_ref, extra_ref, tail_ref, s)
    g = u = None
    for c in range(0, s.depth, chunk):
        lhs = rows_ref[:, c : c + chunk]
        more_g = jnp.dot(lhs, wg[c : c + chunk, :], preferred_element_type=F32)
        more_u = jnp.dot(lhs, wu[c : c + chunk, :], preferred_element_type=F32)
        g = more_g if g is None else g + more_g
        u = more_u if u is None else u + more_u
    hidden = (g * jax.nn.sigmoid(g) * u).astype(BF16)
    tail_ref[...] = jnp.zeros_like(tail_ref)
    for c in range(0, s.depth, chunk):
        part = jnp.dot(hidden, wd[:, c : c + chunk], preferred_element_type=F32)
        scatter_chunk(part, outs, extra_ref, slice(c, c + chunk), s)
    scatter_tails(outs, extra_ref, tail_ref, s)


def saved_kernel(s, gate_ref, up_ref, c1_ref, c2_ref, hb_ref, g_ref, u_ref):
    me = lax.axis_index("expert")
    e, j = me // s.slices, me % s.slices
    g_ref[...] = jnp.zeros_like(g_ref)
    u_ref[...] = jnp.zeros_like(u_ref)
    for i in range(s.blocks):
        k, d = i // s.count, i % s.count
        source = (e + s.count - d) % s.count * s.slices + (j + s.slices - k) % s.slices
        for src, dst in ((gate_ref, g_ref), (up_ref, u_ref)):
            rows = src[source].astype(F32)
            dst[i * s.main : (i + 1) * s.main, :] = rows[: s.main]
            first = s.blocks * s.main + i * s.extra
            dst[first : first + s.extra, :] = rows[s.main :]
    g = g_ref[...]
    u = u_ref[...]
    sig = jax.nn.sigmoid(g)
    c1_ref[...] = u * sig * (1.0 + g * (1.0 - sig))
    c2_ref[...] = g * sig
    hb_ref[...] = (g * sig * u).astype(BF16).astype(F32)


def split_three(value):
    high = value.astype(BF16).astype(F32)
    rest = value - high
    mid = rest.astype(BF16).astype(F32)
    return high, mid, (rest - mid).astype(BF16).astype(F32)


def put_inner(main, extra, tail_ref, s):
    lane = iota((s.main, LANES), 1)
    row = jnp.sum(jnp.where(lane == iota((s.main, LANES), 0), main, 0.0), axis=0, keepdims=True)
    for j in range(s.extra):
        row = jnp.where(lane[:1] == float(s.main + j), extra[j], row)
    put_row(row, tail_ref, s)


def put_row(row, tail_ref, s):
    for p, piece in enumerate(split_three(row)):
        at = s.folds + 1 + p
        tail_ref[at : at + 1, :LANES] = piece


def get_row(tail, s):
    at = s.folds + 1
    return tail[at : at + 1] + tail[at + 1 : at + 2] + tail[at + 2 : at + 3]


def get_slots(row, s):
    lane = iota((s.main, LANES), 1)
    main = jnp.sum(jnp.where(lane == iota((s.main, LANES), 0), row, 0.0), axis=1, keepdims=True)
    extra = [
        jnp.sum(jnp.where(lane[:1] == float(s.main + j), row, 0.0), axis=1, keepdims=True)
        for j in range(s.extra)
    ]
    return main, extra


def backward_kernel(s, *refs):
    packs = grouped(refs[: s.blocks], s, 1)
    c1, c2, hb, wg, wu, wd = refs[s.blocks : s.blocks + 6]
    outs = refs[s.blocks + 6 : -3]
    rows_ref, extra_ref, tail_ref = refs[-3:]
    chunk = chunk_of(s.depth)
    gather_packs(packs, rows_ref, extra_ref, tail_ref, s)
    a = None
    for c in range(0, s.depth, chunk):
        more = lax.dot_general(
            rows_ref[:, c : c + chunk], wd[:, c : c + chunk], NT, preferred_element_type=F32
        )
        a = more if a is None else a + more
    dgp = (a * c1[...]).astype(BF16)
    dup = (a * c2[...]).astype(BF16)
    inner = jnp.sum(a * hb[...], axis=1, keepdims=True)
    tail_ref[...] = jnp.zeros_like(tail_ref)
    for c in range(0, s.depth, chunk):
        part = lax.dot_general(
            dgp, wg[c : c + chunk, :], NT, preferred_element_type=F32
        ) + lax.dot_general(dup, wu[c : c + chunk, :], NT, preferred_element_type=F32)
        scatter_chunk(part, outs, extra_ref, slice(c, c + chunk), s)
    scatter_tails(outs, extra_ref, tail_ref, s, inner)


def total_of(parts, d, s):
    total = parts[d][...].astype(F32)
    n = (len(parts) - s.count) // (s.blocks - s.count)
    for i in range(s.count + d, s.blocks, s.count):
        first = s.count + (i - s.count) * n
        found = [part[...].astype(F32) for part in parts[first : first + n]]
        total = total + (found[0] if n == 1 else jnp.concatenate(found, axis=0))
    return total


def forward_sum_kernel(s, *refs):
    n = s.count + (s.blocks - s.count) * PIECES
    parts, bases = refs[:n], grouped(refs[n : n + 1 + (s.count - 1) * PIECES], s, PIECES)
    route_ref, outs = refs[-1 - s.count], refs[-s.count :]
    for d in range(s.count - 1, -1, -1):
        tail = read(bases[d], s.depth, s.depth + LANES).astype(F32)
        main, extra = get_slots(2.5 * get_row(tail, s), s)
        add_gated(outs[d], bases[d], main, extra, total_of(parts, d, s), s)
        spare = outs[d].shape[1] - s.width
        if spare:
            outs[d][:, s.width :] = jnp.zeros((s.main, spare), BF16)
    at = s.folds
    outs[0][at : at + 1, s.depth : s.depth + s.tok] = route_ref[...].astype(F32).astype(BF16)


def tokens_of(packs, route_row, rows_ref, extra_ref, tail_ref, s):
    extra_ref[...] = jnp.zeros_like(extra_ref)
    for d, pack in enumerate(packs):
        rows_ref[d * s.main : (d + 1) * s.main, :] = pack[:, : s.depth].astype(BF16)
        tail_ref[...] = pack[:, s.depth : s.width].astype(F32)
        unfold(tail_ref, extra_ref, d * s.extra, s)
    rows_ref[s.count * s.main :, :] = extra_ref[...].astype(BF16)
    col, rank = slot_columns(route_row, s)
    high = rows_ref.shape[0]
    place = jnp.full((s.tok, 1), -1.0, F32)
    for d in range(s.count):
        at = jnp.where(
            rank < float(s.main),
            rank + float(d * s.main),
            rank + float(s.count * s.main + d * s.extra - s.main),
        )
        place = jnp.where(col == expert_at(s, d), at, place)
    table = jnp.where(place == iota((s.tok, high), 1), 1.0, 0.0).astype(BF16)
    return jnp.dot(table, rows_ref[...], preferred_element_type=F32)


def forward_end_kernel(s, *refs):
    packs = refs[: s.count]
    out_ref, token_ref, rows_ref, extra_ref, tail_ref, row_ref = refs[s.count :]
    token_ref[...] = jnp.zeros_like(token_ref)
    row_ref[...] = packs[0][:, s.depth : s.depth + LANES].astype(F32)
    route_row = row_ref[s.folds : s.folds + 1, : s.tok]
    out_ref[...] = tokens_of(packs, route_row, rows_ref, extra_ref, tail_ref, s).astype(BF16)


def backward_sum_kernel(s, *refs):
    n = s.count - 1
    parts, outs, tail_ref = refs[: n * s.slices], refs[-1 - n : -1], refs[-1]
    for d in range(n):
        total = parts[d][...].astype(F32)
        for part in parts[n + d :: n]:
            total = total + part[...].astype(F32)
        outs[d][:, : s.depth] = total[:, : s.depth].astype(BF16)
        tail_ref[...] = total[:, s.depth :]
        put_row(get_row(total[:, s.depth : s.depth + LANES], s), tail_ref, s)
        outs[d][:, s.depth :] = tail_ref[...].astype(BF16)


def backward_end_kernel(s, *refs):
    own, packs = refs[: s.slices], refs[s.slices : s.slices + s.count - 1]
    n = s.slices + s.count - 1
    dy_ref, route_ref, score_ref, _, out_ref, grad_ref = refs[n : n + 6]
    rows_ref, extra_ref, tail_ref = refs[n + 6 :]
    total = own[0][...].astype(F32)
    for part in own[1:]:
        total = total + part[...].astype(F32)
    packs = [total, *packs]
    route_row = route_ref[...].astype(F32)
    rows = tokens_of(packs, route_row, rows_ref, extra_ref, tail_ref, s)
    gate = as_column(2.5 * score_ref[...])
    out_ref[...] = (dy_ref[...].astype(F32) + gate * rows).astype(BF16)
    rank = slot_rows(route_row, s)
    dgate = jnp.zeros((1, s.tok), F32)
    for d in range(s.count):
        hit = route_row == expert_at(s, d)
        tail = packs[d][:, s.depth : s.depth + LANES].astype(F32)
        main, extra = get_slots(get_row(tail, s), s)
        dgate += jnp.sum(
            jnp.where(hit & (rank == iota((s.main, s.tok), 0)), main, 0.0), axis=0, keepdims=True
        )
        for j in range(s.extra):
            dgate += jnp.where(hit & (rank == float(s.main + j)), extra[j], 0.0)
    grad_ref[...] = 2.5 * dgate


VMEM = pl.BlockSpec(memory_space=pltpu.VMEM)
HBM = pl.BlockSpec(memory_space=pltpu.HBM)


def call(kernel, name, outs, scratch, ins, *args, mib=16):
    shapes = [jax.ShapeDtypeStruct(shape, kind) for shape, kind in outs]
    args = [
        pltpu.with_memory_space_constraint(a, pltpu.HBM) if spec is HBM else a
        for a, spec in zip(args, ins)
    ]
    return pl.pallas_call(
        kernel,
        out_shape=shapes,
        in_specs=ins,
        out_specs=[VMEM] * len(shapes),
        scratch_shapes=scratch,
        compiler_params=pltpu.CompilerParams(vmem_limit_bytes=mib << 20),
        cost_estimate=pl.CostEstimate(flops=0, bytes_accessed=0, transcendentals=0),
        name=name,
    )(*args)


def tail_scratch(s, rows):
    return [
        pltpu.VMEM((rows, s.depth), F32),
        pltpu.VMEM((s.main, LANES * s.extra), F32),
    ]


def load(*arrays):
    return call(
        load_kernel,
        "load",
        [(a.shape, a.dtype) for a in arrays],
        [pltpu.SemaphoreType.DMA((len(arrays),))],
        [HBM] * len(arrays),
        *arrays,
    )


def row_scratch(s):
    return [pltpu.VMEM((s.rows, s.depth), BF16), *tail_scratch(s, s.tail_rows)]


def cross(s, packs, pieces):
    return [packs[0]] + [across(p, 1 + i // pieces, s) for i, p in enumerate(packs[1:])]


def spread(s, got):
    return list(got) + [beside(b, k, s) for k in range(1, s.slices) for b in got]


def hold(values, *after):
    return lax.optimization_barrier((values, after))[0]


def parts_shape(s, width, pieces):
    kept = [((s.main, width), BF16)] * s.count
    return kept + [((s.main // pieces, width), BF16)] * ((s.blocks - s.count) * pieces)


def gather_parts(s, parts):
    n = (len(parts) - s.count) // (s.blocks - s.count)
    moved = [beside(p, -(i // n // s.count + 1), s) for i, p in enumerate(parts[s.count :])]
    return list(parts[: s.count]) + moved


def step(routes, run, *args):
    like = jax.eval_shape(run, *args)
    skip = lambda *_: jax.tree.map(lambda a: jnp.zeros(a.shape, a.dtype), like)
    return lax.cond(routes[0, 0] < EXPERTS, run, skip, *args)


def end_scratch(s):
    low = -(-(s.count * s.extra) // 16) * 16
    return [pltpu.VMEM((s.count * s.main + low, s.depth), BF16), *tail_scratch(s, low)]


def body(
    x_fwd,
    saved_gate,
    saved_up,
    grad_next,
    routes_fwd,
    routes_bwd,
    scores_fwd,
    scores_bwd,
    w_gate,
    w_up,
    w_down,
):
    groups = lax.axis_size("expert")
    tok, depth = x_fwd.shape[1:]
    s = Sizes(saved_gate.shape[2], depth, EXPERTS, groups // EXPERTS, tok)
    hidden = w_gate.shape[2]
    route_a = routes_fwd.reshape(1, tok)
    route_b = routes_bwd.reshape(1, tok)
    score_a = scores_fwd.reshape(1, tok)
    score_b = scores_bwd.reshape(1, tok)

    packed = [((s.main, s.width), BF16)] * s.count
    sent_a = call(
        functools.partial(first_kernel, s),
        "first",
        packed[:1] + [((s.main, s.width // PIECES), BF16)] * (PIECES * (s.count - 1)),
        [
            pltpu.VMEM((1, tok), jnp.int32),
            pltpu.VMEM((1, tok), F32),
            pltpu.VMEM((tok, depth), BF16),
            *tail_scratch(s, 16),
            pltpu.SemaphoreType.DMA((3,)),
        ],
        [HBM] * 3,
        route_a,
        score_a,
        x_fwd[0],
    )
    upstream = from_behind(grad_next, "section", -1)[0]
    wg, wu, wd, route_a, route_b, score_b = load(
        w_gate[0], w_up[0], w_down[0], route_a, route_b, score_b
    )
    factors = call(
        functools.partial(saved_kernel, s),
        "saved",
        [((s.rows, hidden), F32)] * 3,
        [pltpu.VMEM((s.rows, hidden), F32)] * 2,
        [VMEM] * 2,
        saved_gate[0],
        saved_up[0],
    )
    wide = s.width + LANES

    def backward(got, *rest):
        rows = spread(s, got)
        parts = call(
            functools.partial(backward_kernel, s),
            "backward",
            packed * s.slices,
            row_scratch(s),
            [VMEM] * (s.blocks + 6),
            *rows,
            *rest,
        )
        others = [p for i, p in enumerate(parts) if i % s.count]
        others = [beside(p, -(i // (s.count - 1)), s) if i >= s.count - 1 else p for i, p in enumerate(others)]
        sums = call(
            functools.partial(backward_sum_kernel, s),
            "backward_sum",
            packed[1:],
            [pltpu.VMEM((s.main, LANES * s.extra), F32)],
            [VMEM] * len(others),
            *others,
        )
        return tuple(parts[:: s.count]), tuple(sums)

    got = cross(s, sent_a, PIECES)
    got[1:] = hold(got[1:], route_a, factors)
    rows_a = spread(s, got)
    sent_b = call(
        functools.partial(pack_kernel, s),
        "pack",
        packed,
        tail_scratch(s, 16),
        [VMEM] * 2,
        route_b,
        hold(upstream, got[1:]),
    )
    got_b = cross(s, sent_b, 1)
    parts_a = call(
        functools.partial(forward_kernel, s),
        "forward",
        parts_shape(s, s.width, PIECES),
        row_scratch(s),
        [VMEM] * (len(rows_a) + 3),
        *hold(rows_a, sent_b),
        wg,
        wu,
        wd,
    )
    parts_a = gather_parts(s, parts_a)
    sums_a = call(
        functools.partial(forward_sum_kernel, s),
        "forward_sum",
        packed[:1] + [((s.main, wide), BF16)] * (s.count - 1),
        [],
        [VMEM] * (len(parts_a) + len(got) + 1),
        *parts_a,
        *got,
        route_a,
    )
    moved = [to_next(y, -d, s) for d, y in enumerate(sums_a)]
    got_b[1:] = hold(got_b[1:], sums_a)
    own_b, sums_b = step(route_b, backward, got_b, *factors, wg, wu, wd)
    back_b = [across(y, -1 - d, s) for d, y in enumerate(sums_b)]
    own_b = [beside(p, -k, s) if k else p for k, p in enumerate(own_b)]
    next_input, token = call(
        functools.partial(forward_end_kernel, s),
        "forward_end",
        [((tok, depth), BF16), ((8, LANES), F32)],
        end_scratch(s) + [pltpu.VMEM((s.main, LANES), F32)],
        [VMEM] * s.count,
        *moved,
    )
    input_grad, score_grad = call(
        functools.partial(backward_end_kernel, s),
        "backward_end",
        [((tok, depth), BF16), ((1, tok), F32)],
        end_scratch(s),
        [VMEM] * (s.slices + s.count - 1 + 4),
        *own_b,
        *back_b,
        upstream,
        route_b,
        score_b,
        token,
    )
    return next_input[None], input_grad[None], score_grad.reshape(1, tok, 1)


def solution(mesh):
    placed = (
        P("section", "expert", None),
        P("section", None, None, "expert"),
        P("section", None, None, "expert"),
        P("section", "expert", None),
        P("section", "expert", None),
        P("section", "expert", None),
        P("section", "expert", None),
        P("section", "expert", None),
        P("section", None, "expert"),
        P("section", None, "expert"),
        P("section", "expert", None),
    )
    return jax.shard_map(
        body,
        mesh=mesh,
        in_specs=placed,
        out_specs=(
            P("section", "expert", None),
            P("section", "expert", None),
            P("section", "expert", None),
        ),
        check_vma=False,
    )
```

```python
import functools

import jax
import jax.numpy as jnp
from jax import lax
from jax.experimental import pallas as pl
from jax.experimental.pallas import tpu as pltpu
from jax.sharding import PartitionSpec as P

EXPERTS = 2
LANES = 128
PIECES = 2
F32 = jnp.float32
BF16 = jnp.bfloat16
NT = (((1,), (1,)), ((), ()))


class Sizes:
    def __init__(self, cap, depth, count, slices, tok):
        self.cap, self.depth, self.count, self.slices, self.tok = cap, depth, count, slices, tok
        self.main = cap // 16 * 16
        self.extra = cap - self.main
        self.folds = depth // LANES
        assert self.folds + 4 <= self.main and depth % LANES == 0
        assert max(cap, tok) <= LANES
        self.width = depth + LANES * self.extra
        self.blocks = count * slices
        self.tail_rows = -(-(self.blocks * self.extra) // 16) * 16
        self.rows = self.blocks * self.main + self.tail_rows


def from_behind(block, axis, distance):
    devices = range(lax.axis_size(axis))
    route = [((i - distance) % len(devices), i) for i in devices]
    return lax.ppermute(block, axis, route)


def to_next(block, distance, s):
    sections, own = lax.axis_size("section"), s.count * s.slices
    route = [
        (
            l * own + e * s.slices + j,
            (l + 1) % sections * own + (e + distance) % s.count * s.slices + j,
        )
        for l in range(sections)
        for e in range(s.count)
        for j in range(s.slices)
    ]
    return lax.ppermute(block, ("section", "expert"), route)


def across(block, distance, s):
    route = [
        (e * s.slices + j, (e + distance) % s.count * s.slices + j)
        for e in range(s.count)
        for j in range(s.slices)
    ]
    return lax.ppermute(block, "expert", route)


def beside(block, distance, s):
    route = [
        (e * s.slices + j, e * s.slices + (j + distance) % s.slices)
        for e in range(s.count)
        for j in range(s.slices)
    ]
    return lax.ppermute(block, "expert", route)


def iota(shape, dim):
    return lax.broadcasted_iota(jnp.int32, shape, dim).astype(F32)


def as_column(row):
    n = row.shape[1]
    return jnp.sum(
        jnp.where(iota((n, n), 0) == iota((n, n), 1), row, 0.0), axis=1, keepdims=True
    )


def own_expert(s):
    return lax.axis_index("expert") // s.slices


def expert_at(s, distance):
    return ((own_expert(s) + distance) % s.count).astype(F32)


def slot_rows(route_row, s):
    col = as_column(route_row)
    n = s.tok
    same = (col == route_row) & (iota((n, n), 0) < iota((n, n), 1))
    return jnp.sum(jnp.where(same, 1.0, 0.0), axis=0, keepdims=True)


def slot_columns(route_row, s):
    col = as_column(route_row)
    n = s.tok
    same = (col == route_row) & (iota((n, n), 1) < iota((n, n), 0))
    return col, jnp.sum(jnp.where(same, 1.0, 0.0), axis=1, keepdims=True)


def fold(values_ref, first, tail_ref, s):
    for j in range(s.extra):
        for r in range(s.folds):
            tail_ref[r : r + 1, j * LANES : (j + 1) * LANES] = values_ref[
                first + j : first + j + 1, r * LANES : (r + 1) * LANES
            ]


def unfold(tail_ref, values_ref, first, s):
    for j in range(s.extra):
        for r in range(s.folds):
            values_ref[first + j : first + j + 1, r * LANES : (r + 1) * LANES] = tail_ref[
                r : r + 1, j * LANES : (j + 1) * LANES
            ]


def put_scores(route_row, score_row, expert, tail_ref, s):
    col, rank = slot_columns(route_row, s)
    hit = (col == expert) & (rank == iota((s.tok, LANES), 1))
    row = jnp.sum(jnp.where(hit, as_column(score_row), 0.0), axis=0, keepdims=True)
    put_row(row, tail_ref, s)


def add_gated(out_ref, base, main, extra, total, s):
    d = s.depth
    out_ref[:, :d] = (read(base, 0, d).astype(F32) + main * total[:, :d]).astype(BF16)
    for j in range(s.extra):
        at = slice(d + j * LANES, d + (j + 1) * LANES)
        value = read(base, at.start, at.stop).astype(F32) + extra[j] * total[:, at]
        out_ref[:, at] = value.astype(BF16)


def read(pieces, low, high):
    found, at = [], 0
    for piece in pieces:
        width = piece.shape[1]
        a, b = max(low, at), min(high, at + width)
        if a < b:
            found.append(piece[:, a - at : b - at])
        at += width
    return found[0] if len(found) == 1 else jnp.concatenate(found, axis=1)


def write(pieces, low, value):
    at = 0
    for piece in pieces:
        width = piece.shape[1]
        a, b = max(low, at), min(low + value.shape[1], at + width)
        if a < b:
            piece[:, a - at : b - at] = value[:, a - low : b - low]
        at += width


def grouped(refs, s, pieces):
    one = 1 + (s.count - 1) * pieces
    packs = []
    for first in range(0, len(refs), one):
        packs.append(refs[first : first + 1])
        for at in range(first + 1, first + one, pieces):
            packs.append(refs[at : at + pieces])
    return packs


def pack_rows(s, route_row, x, outs, extra_ref, tail_ref, score_row=None):
    rank = slot_rows(route_row, s)
    slots = iota((s.main + 16, s.tok), 0)
    tail_ref[...] = jnp.zeros_like(tail_ref)
    for d in range(s.count):
        hit = route_row == expert_at(s, d)
        table = jnp.where(hit & (rank == slots), 1.0, 0.0).astype(BF16)
        rows = jnp.dot(table, x, preferred_element_type=F32)
        write(outs[d], 0, rows[: s.main].astype(BF16))
        extra_ref[...] = rows[s.main :]
        fold(extra_ref, 0, tail_ref, s)
        if score_row is not None:
            put_scores(route_row, score_row, expert_at(s, d), tail_ref, s)
        write(outs[d], s.depth, tail_ref[...].astype(BF16))


def first_kernel(s, route_hbm, score_hbm, x_hbm, *rest):
    outs = grouped(rest[:-6], s, PIECES)
    route_ref, score_ref, x_ref, extra_ref, tail_ref, sems = rest[-6:]
    copies = [
        pltpu.make_async_copy(src, dst, sems.at[i])
        for i, (src, dst) in enumerate(
            ((route_hbm, route_ref), (score_hbm, score_ref), (x_hbm, x_ref))
        )
    ]
    for copy in copies:
        copy.start()
    for copy in copies:
        copy.wait()
    route_row = route_ref[...].astype(F32)
    pack_rows(s, route_row, x_ref[...], outs, extra_ref, tail_ref, score_ref[...])


def pack_kernel(s, route_ref, x_ref, *rest):
    outs, (extra_ref, tail_ref) = grouped(rest[:-2], s, 1), rest[-2:]
    pack_rows(s, route_ref[...].astype(F32), x_ref[...], outs, extra_ref, tail_ref)


def load_kernel(*refs):
    sems = refs[-1]
    n = (len(refs) - 1) // 2
    copies = [pltpu.make_async_copy(refs[i], refs[n + i], sems.at[i]) for i in range(n)]
    for copy in copies:
        copy.start()
    for copy in copies:
        copy.wait()


def gather_packs(packs, rows_ref, extra_ref, tail_ref, s):
    extra_ref[...] = jnp.zeros_like(extra_ref)
    for i, pack in enumerate(packs):
        rows_ref[i * s.main : (i + 1) * s.main, :] = read(pack, 0, s.depth)
        tail_ref[...] = read(pack, s.depth, s.width).astype(F32)
        unfold(tail_ref, extra_ref, i * s.extra, s)
    rows_ref[s.blocks * s.main :, :] = extra_ref[...].astype(BF16)


def put(outs, i, at, value, s):
    if i < s.count:
        outs[i][:, at] = value
        return
    n = (len(outs) - s.count) // (s.blocks - s.count)
    rows = s.main // n
    for h in range(n):
        outs[s.count + (i - s.count) * n + h][:, at] = value[h * rows : (h + 1) * rows]


def scatter_chunk(value, outs, extra_ref, at, s):
    for i in range(s.blocks):
        put(outs, i, at, value[i * s.main : (i + 1) * s.main].astype(BF16), s)
    extra_ref[:, at] = value[s.blocks * s.main :]


def scatter_tails(outs, extra_ref, tail_ref, s, inner=None):
    for i in range(s.blocks):
        fold(extra_ref, i * s.extra, tail_ref, s)
        if inner is not None:
            first = s.blocks * s.main + i * s.extra
            extra = [inner[first + j : first + j + 1] for j in range(s.extra)]
            put_inner(inner[i * s.main : (i + 1) * s.main], extra, tail_ref, s)
        put(outs, i, slice(s.depth, s.width), tail_ref[...].astype(BF16), s)


def chunk_of(depth):
    for chunk in (512, 256, 128):
        if depth % chunk == 0:
            return chunk


def forward_kernel(s, *refs):
    n = s.slices * (1 + (s.count - 1) * PIECES)
    packs = grouped(refs[:n], s, PIECES)
    wg, wu, wd = refs[n : n + 3]
    outs = refs[n + 3 : -3]
    rows_ref, extra_ref, tail_ref = refs[-3:]
    chunk = chunk_of(s.depth)
    gather_packs(packs, rows_ref, extra_ref, tail_ref, s)
    g = u = None
    for c in range(0, s.depth, chunk):
        lhs = rows_ref[:, c : c + chunk]
        more_g = jnp.dot(lhs, wg[c : c + chunk, :], preferred_element_type=F32)
        more_u = jnp.dot(lhs, wu[c : c + chunk, :], preferred_element_type=F32)
        g = more_g if g is None else g + more_g
        u = more_u if u is None else u + more_u
    hidden = (g * jax.nn.sigmoid(g) * u).astype(BF16)
    tail_ref[...] = jnp.zeros_like(tail_ref)
    for c in range(0, s.depth, chunk):
        part = jnp.dot(hidden, wd[:, c : c + chunk], preferred_element_type=F32)
        scatter_chunk(part, outs, extra_ref, slice(c, c + chunk), s)
    scatter_tails(outs, extra_ref, tail_ref, s)


def saved_kernel(s, gate_ref, up_ref, c1_ref, c2_ref, hb_ref, g_ref, u_ref):
    me = lax.axis_index("expert")
    e, j = me // s.slices, me % s.slices
    g_ref[...] = jnp.zeros_like(g_ref)
    u_ref[...] = jnp.zeros_like(u_ref)
    for i in range(s.blocks):
        k, d = i // s.count, i % s.count
        source = (e + s.count - d) % s.count * s.slices + (j + s.slices - k) % s.slices
        for src, dst in ((gate_ref, g_ref), (up_ref, u_ref)):
            rows = src[source].astype(F32)
            dst[i * s.main : (i + 1) * s.main, :] = rows[: s.main]
            first = s.blocks * s.main + i * s.extra
            dst[first : first + s.extra, :] = rows[s.main :]
    g = g_ref[...]
    u = u_ref[...]
    sig = jax.nn.sigmoid(g)
    c1_ref[...] = u * sig * (1.0 + g * (1.0 - sig))
    c2_ref[...] = g * sig
    hb_ref[...] = (g * sig * u).astype(BF16).astype(F32)


def split_three(value):
    high = value.astype(BF16).astype(F32)
    rest = value - high
    mid = rest.astype(BF16).astype(F32)
    return high, mid, (rest - mid).astype(BF16).astype(F32)


def put_inner(main, extra, tail_ref, s):
    lane = iota((s.main, LANES), 1)
    row = jnp.sum(jnp.where(lane == iota((s.main, LANES), 0), main, 0.0), axis=0, keepdims=True)
    for j in range(s.extra):
        row = jnp.where(lane[:1] == float(s.main + j), extra[j], row)
    put_row(row, tail_ref, s)


def put_row(row, tail_ref, s):
    for p, piece in enumerate(split_three(row)):
        at = s.folds + 1 + p
        tail_ref[at : at + 1, :LANES] = piece


def get_row(tail, s):
    at = s.folds + 1
    return tail[at : at + 1] + tail[at + 1 : at + 2] + tail[at + 2 : at + 3]


def get_slots(row, s):
    lane = iota((s.main, LANES), 1)
    main = jnp.sum(jnp.where(lane == iota((s.main, LANES), 0), row, 0.0), axis=1, keepdims=True)
    extra = [
        jnp.sum(jnp.where(lane[:1] == float(s.main + j), row, 0.0), axis=1, keepdims=True)
        for j in range(s.extra)
    ]
    return main, extra


def backward_kernel(s, *refs):
    packs = grouped(refs[: s.blocks], s, 1)
    c1, c2, hb, wg, wu, wd = refs[s.blocks : s.blocks + 6]
    outs = refs[s.blocks + 6 : -3]
    rows_ref, extra_ref, tail_ref = refs[-3:]
    chunk = chunk_of(s.depth)
    gather_packs(packs, rows_ref, extra_ref, tail_ref, s)
    a = None
    for c in range(0, s.depth, chunk):
        more = lax.dot_general(
            rows_ref[:, c : c + chunk], wd[:, c : c + chunk], NT, preferred_element_type=F32
        )
        a = more if a is None else a + more
    dgp = (a * c1[...]).astype(BF16)
    dup = (a * c2[...]).astype(BF16)
    inner = jnp.sum(a * hb[...], axis=1, keepdims=True)
    tail_ref[...] = jnp.zeros_like(tail_ref)
    for c in range(0, s.depth, chunk):
        part = lax.dot_general(
            dgp, wg[c : c + chunk, :], NT, preferred_element_type=F32
        ) + lax.dot_general(dup, wu[c : c + chunk, :], NT, preferred_element_type=F32)
        scatter_chunk(part, outs, extra_ref, slice(c, c + chunk), s)
    scatter_tails(outs, extra_ref, tail_ref, s, inner)


def total_of(parts, d, s):
    total = parts[d][...].astype(F32)
    n = (len(parts) - s.count) // (s.blocks - s.count)
    for i in range(s.count + d, s.blocks, s.count):
        first = s.count + (i - s.count) * n
        found = [part[...].astype(F32) for part in parts[first : first + n]]
        total = total + (found[0] if n == 1 else jnp.concatenate(found, axis=0))
    return total


def forward_sum_kernel(s, *refs):
    n = s.count + (s.blocks - s.count) * PIECES
    parts, bases = refs[:n], grouped(refs[n : n + 1 + (s.count - 1) * PIECES], s, PIECES)
    route_ref, outs = refs[-1 - s.count], refs[-s.count :]
    for d in range(s.count - 1, -1, -1):
        tail = read(bases[d], s.depth, s.depth + LANES).astype(F32)
        main, extra = get_slots(2.5 * get_row(tail, s), s)
        add_gated(outs[d], bases[d], main, extra, total_of(parts, d, s), s)
        spare = outs[d].shape[1] - s.width
        if spare:
            outs[d][:, s.width :] = jnp.zeros((s.main, spare), BF16)
    at = s.folds
    outs[0][at : at + 1, s.depth : s.depth + s.tok] = route_ref[...].astype(F32).astype(BF16)


def tokens_of(packs, route_row, rows_ref, extra_ref, tail_ref, s):
    extra_ref[...] = jnp.zeros_like(extra_ref)
    for d, pack in enumerate(packs):
        rows_ref[d * s.main : (d + 1) * s.main, :] = pack[:, : s.depth].astype(BF16)
        tail_ref[...] = pack[:, s.depth : s.width].astype(F32)
        unfold(tail_ref, extra_ref, d * s.extra, s)
    rows_ref[s.count * s.main :, :] = extra_ref[...].astype(BF16)
    col, rank = slot_columns(route_row, s)
    high = rows_ref.shape[0]
    place = jnp.full((s.tok, 1), -1.0, F32)
    for d in range(s.count):
        at = jnp.where(
            rank < float(s.main),
            rank + float(d * s.main),
            rank + float(s.count * s.main + d * s.extra - s.main),
        )
        place = jnp.where(col == expert_at(s, d), at, place)
    table = jnp.where(place == iota((s.tok, high), 1), 1.0, 0.0).astype(BF16)
    return jnp.dot(table, rows_ref[...], preferred_element_type=F32)


def forward_end_kernel(s, *refs):
    packs = refs[: s.count]
    out_ref, token_ref, rows_ref, extra_ref, tail_ref, row_ref = refs[s.count :]
    token_ref[...] = jnp.zeros_like(token_ref)
    row_ref[...] = packs[0][:, s.depth : s.depth + LANES].astype(F32)
    route_row = row_ref[s.folds : s.folds + 1, : s.tok]
    out_ref[...] = tokens_of(packs, route_row, rows_ref, extra_ref, tail_ref, s).astype(BF16)


def backward_sum_kernel(s, *refs):
    n = s.count - 1
    parts, outs, tail_ref = refs[: n * s.slices], refs[-1 - n : -1], refs[-1]
    for d in range(n):
        total = parts[d][...].astype(F32)
        for part in parts[n + d :: n]:
            total = total + part[...].astype(F32)
        outs[d][:, : s.depth] = total[:, : s.depth].astype(BF16)
        tail_ref[...] = total[:, s.depth :]
        put_row(get_row(total[:, s.depth : s.depth + LANES], s), tail_ref, s)
        outs[d][:, s.depth :] = tail_ref[...].astype(BF16)


def backward_end_kernel(s, *refs):
    own, packs = refs[: s.slices], refs[s.slices : s.slices + s.count - 1]
    n = s.slices + s.count - 1
    dy_ref, route_ref, score_ref, _, out_ref, grad_ref = refs[n : n + 6]
    rows_ref, extra_ref, tail_ref = refs[n + 6 :]
    total = own[0][...].astype(F32)
    for part in own[1:]:
        total = total + part[...].astype(F32)
    packs = [total, *packs]
    route_row = route_ref[...].astype(F32)
    rows = tokens_of(packs, route_row, rows_ref, extra_ref, tail_ref, s)
    gate = as_column(2.5 * score_ref[...])
    out_ref[...] = (dy_ref[...].astype(F32) + gate * rows).astype(BF16)
    rank = slot_rows(route_row, s)
    dgate = jnp.zeros((1, s.tok), F32)
    for d in range(s.count):
        hit = route_row == expert_at(s, d)
        tail = packs[d][:, s.depth : s.depth + LANES].astype(F32)
        main, extra = get_slots(get_row(tail, s), s)
        dgate += jnp.sum(
            jnp.where(hit & (rank == iota((s.main, s.tok), 0)), main, 0.0), axis=0, keepdims=True
        )
        for j in range(s.extra):
            dgate += jnp.where(hit & (rank == float(s.main + j)), extra[j], 0.0)
    grad_ref[...] = 2.5 * dgate


VMEM = pl.BlockSpec(memory_space=pltpu.VMEM)
HBM = pl.BlockSpec(memory_space=pltpu.HBM)


def call(kernel, name, outs, scratch, ins, *args, mib=16, place=jax.ShapeDtypeStruct):
    shapes = [place(shape, kind) for shape, kind in outs]
    args = [
        pltpu.with_memory_space_constraint(a, pltpu.HBM) if spec is HBM else a
        for a, spec in zip(args, ins)
    ]
    return pl.pallas_call(
        kernel,
        out_shape=shapes,
        in_specs=ins,
        out_specs=[VMEM] * len(shapes),
        scratch_shapes=scratch,
        compiler_params=pltpu.CompilerParams(vmem_limit_bytes=mib << 20),
        cost_estimate=pl.CostEstimate(flops=0, bytes_accessed=0, transcendentals=0),
        name=name,
    )(*args)


def tail_scratch(s, rows):
    return [
        pltpu.VMEM((rows, s.depth), F32),
        pltpu.VMEM((s.main, LANES * s.extra), F32),
    ]


def load(*arrays):
    return call(
        load_kernel,
        "load",
        [(a.shape, a.dtype) for a in arrays],
        [pltpu.SemaphoreType.DMA((len(arrays),))],
        [HBM] * len(arrays),
        *arrays,
    )


def row_scratch(s):
    return [pltpu.VMEM((s.rows, s.depth), BF16), *tail_scratch(s, s.tail_rows)]


def cross(s, packs, pieces):
    return [packs[0]] + [across(p, 1 + i // pieces, s) for i, p in enumerate(packs[1:])]


def spread(s, got):
    return list(got) + [beside(b, k, s) for k in range(1, s.slices) for b in got]


def hold(values, *after):
    return lax.optimization_barrier((values, after))[0]


def parts_shape(s, width, pieces):
    kept = [((s.main, width), BF16)] * s.count
    return kept + [((s.main // pieces, width), BF16)] * ((s.blocks - s.count) * pieces)


def gather_parts(s, parts):
    n = (len(parts) - s.count) // (s.blocks - s.count)
    moved = [beside(p, -(i // n // s.count + 1), s) for i, p in enumerate(parts[s.count :])]
    return list(parts[: s.count]) + moved


def step(routes, run, *args):
    like = jax.eval_shape(run, *args)
    skip = lambda *_: jax.tree.map(lambda a: jnp.zeros(a.shape, a.dtype), like)
    return lax.cond(routes[0, 0] < EXPERTS, run, skip, *args)


def end_scratch(s):
    low = -(-(s.count * s.extra) // 16) * 16
    return [pltpu.VMEM((s.count * s.main + low, s.depth), BF16), *tail_scratch(s, low)]


def body(
    x_fwd,
    saved_gate,
    saved_up,
    grad_next,
    routes_fwd,
    routes_bwd,
    scores_fwd,
    scores_bwd,
    w_gate,
    w_up,
    w_down,
):
    groups = lax.axis_size("expert")
    tok, depth = x_fwd.shape[1:]
    s = Sizes(saved_gate.shape[2], depth, EXPERTS, groups // EXPERTS, tok)
    hidden = w_gate.shape[2]
    route_a = routes_fwd.reshape(1, tok)
    route_b = routes_bwd.reshape(1, tok)
    score_a = scores_fwd.reshape(1, tok)
    score_b = scores_bwd.reshape(1, tok)

    packed = [((s.main, s.width), BF16)] * s.count
    sent_a = call(
        functools.partial(first_kernel, s),
        "first",
        packed[:1] + [((s.main, s.width // PIECES), BF16)] * (PIECES * (s.count - 1)),
        [
            pltpu.VMEM((1, tok), jnp.int32),
            pltpu.VMEM((1, tok), F32),
            pltpu.VMEM((tok, depth), BF16),
            *tail_scratch(s, 16),
            pltpu.SemaphoreType.DMA((3,)),
        ],
        [HBM] * 3,
        route_a,
        score_a,
        x_fwd[0],
    )
    upstream = from_behind(grad_next, "section", -1)[0]
    wg, wu, wd, route_a, route_b, score_b = load(
        w_gate[0], w_up[0], w_down[0], route_a, route_b, score_b
    )
    factors = call(
        functools.partial(saved_kernel, s),
        "saved",
        [((s.rows, hidden), F32)] * 3,
        [pltpu.VMEM((s.rows, hidden), F32)] * 2,
        [VMEM] * 2,
        saved_gate[0],
        saved_up[0],
    )
    wide = s.width + LANES

    def backward(got, *rest):
        rows = spread(s, got)
        parts = call(
            functools.partial(backward_kernel, s),
            "backward",
            packed * s.slices,
            row_scratch(s),
            [VMEM] * (s.blocks + 6),
            *rows,
            *rest,
        )
        others = [p for i, p in enumerate(parts) if i % s.count]
        others = [beside(p, -(i // (s.count - 1)), s) if i >= s.count - 1 else p for i, p in enumerate(others)]
        sums = call(
            functools.partial(backward_sum_kernel, s),
            "backward_sum",
            packed[1:],
            [pltpu.VMEM((s.main, LANES * s.extra), F32)],
            [VMEM] * len(others),
            *others,
            place=pltpu.VMEM,
        )
        return tuple(parts[:: s.count]), tuple(sums)

    got = cross(s, sent_a, PIECES)
    got[1:] = hold(got[1:], route_a, factors)
    rows_a = spread(s, got)
    sent_b = call(
        functools.partial(pack_kernel, s),
        "pack",
        packed,
        tail_scratch(s, 16),
        [VMEM] * 2,
        route_b,
        hold(upstream, got[1:]),
    )
    got_b = cross(s, sent_b, 1)
    parts_a = call(
        functools.partial(forward_kernel, s),
        "forward",
        parts_shape(s, s.width, PIECES),
        row_scratch(s),
        [VMEM] * (len(rows_a) + 3),
        *hold(rows_a, sent_b),
        wg,
        wu,
        wd,
    )
    parts_a = gather_parts(s, parts_a)
    sums_a = call(
        functools.partial(forward_sum_kernel, s),
        "forward_sum",
        [((s.main, wide), BF16)] * s.count,
        [],
        [VMEM] * (len(parts_a) + len(got) + 1),
        *parts_a,
        *got,
        route_a,
    )
    moved = [to_next(y, -d, s) for d, y in enumerate(sums_a)]
    got_b[1:] = hold(got_b[1:], sums_a)
    own_b, sums_b = step(route_b, backward, got_b, *factors, wg, wu, wd)
    back_b = [across(y, -1 - d, s) for d, y in enumerate(sums_b)]
    own_b = [beside(p, -k, s) if k else p for k, p in enumerate(own_b)]
    next_input, token = call(
        functools.partial(forward_end_kernel, s),
        "forward_end",
        [((tok, depth), BF16), ((8, LANES), F32)],
        end_scratch(s) + [pltpu.VMEM((s.main, LANES), F32)],
        [VMEM] * s.count,
        *moved,
    )
    input_grad, score_grad = call(
        functools.partial(backward_end_kernel, s),
        "backward_end",
        [((tok, depth), BF16), ((1, tok), F32)],
        end_scratch(s),
        [VMEM] * (s.slices + s.count - 1 + 4),
        *own_b,
        *back_b,
        upstream,
        route_b,
        score_b,
        token,
    )
    return next_input[None], input_grad[None], score_grad.reshape(1, tok, 1)


def solution(mesh):
    placed = (
        P("section", "expert", None),
        P("section", None, None, "expert"),
        P("section", None, None, "expert"),
        P("section", "expert", None),
        P("section", "expert", None),
        P("section", "expert", None),
        P("section", "expert", None),
        P("section", "expert", None),
        P("section", None, "expert"),
        P("section", None, "expert"),
        P("section", "expert", None),
    )
    return jax.shard_map(
        body,
        mesh=mesh,
        in_specs=placed,
        out_specs=(
            P("section", "expert", None),
            P("section", "expert", None),
            P("section", "expert", None),
        ),
        check_vma=False,
    )
```

```python
import functools

import jax
import jax.numpy as jnp
from jax import lax
from jax.experimental import pallas as pl
from jax.experimental.pallas import tpu as pltpu
from jax.sharding import PartitionSpec as P

EXPERTS = 2
LANES = 128
PIECES = 2
F32 = jnp.float32
BF16 = jnp.bfloat16
NT = (((1,), (1,)), ((), ()))


class Sizes:
    def __init__(self, cap, depth, count, slices, tok):
        self.cap, self.depth, self.count, self.slices, self.tok = cap, depth, count, slices, tok
        self.main = cap // 16 * 16
        self.extra = cap - self.main
        self.folds = depth // LANES
        assert self.folds + 4 <= self.main and depth % LANES == 0
        assert max(cap, tok) <= LANES
        self.width = depth + LANES * self.extra
        self.blocks = count * slices
        self.tail_rows = -(-(self.blocks * self.extra) // 16) * 16
        self.rows = self.blocks * self.main + self.tail_rows


def from_behind(block, axis, distance):
    devices = range(lax.axis_size(axis))
    route = [((i - distance) % len(devices), i) for i in devices]
    return lax.ppermute(block, axis, route)


def turn_of(i, last, s):
    return s.count - 1 - i if last else i


def to_next(block, i, s):
    sections, own = lax.axis_size("section"), s.count * s.slices
    route = [
        (
            l * own + e * s.slices + j,
            (l + 1) % sections * own
            + (e - turn_of(i, l == sections - 1, s)) % s.count * s.slices
            + j,
        )
        for l in range(sections)
        for e in range(s.count)
        for j in range(s.slices)
    ]
    return lax.ppermute(block, ("section", "expert"), route)


def across(block, distance, s):
    route = [
        (e * s.slices + j, (e + distance) % s.count * s.slices + j)
        for e in range(s.count)
        for j in range(s.slices)
    ]
    return lax.ppermute(block, "expert", route)


def beside(block, distance, s):
    route = [
        (e * s.slices + j, e * s.slices + (j + distance) % s.slices)
        for e in range(s.count)
        for j in range(s.slices)
    ]
    return lax.ppermute(block, "expert", route)


def iota(shape, dim):
    return lax.broadcasted_iota(jnp.int32, shape, dim).astype(F32)


def as_column(row):
    n = row.shape[1]
    return jnp.sum(
        jnp.where(iota((n, n), 0) == iota((n, n), 1), row, 0.0), axis=1, keepdims=True
    )


def own_expert(s):
    return lax.axis_index("expert") // s.slices


def expert_at(s, distance):
    return ((own_expert(s) + distance) % s.count).astype(F32)


def slot_rows(route_row, s):
    col = as_column(route_row)
    n = s.tok
    same = (col == route_row) & (iota((n, n), 0) < iota((n, n), 1))
    return jnp.sum(jnp.where(same, 1.0, 0.0), axis=0, keepdims=True)


def slot_columns(route_row, s):
    col = as_column(route_row)
    n = s.tok
    same = (col == route_row) & (iota((n, n), 1) < iota((n, n), 0))
    return col, jnp.sum(jnp.where(same, 1.0, 0.0), axis=1, keepdims=True)


def fold(values_ref, first, tail_ref, s):
    for j in range(s.extra):
        for r in range(s.folds):
            tail_ref[r : r + 1, j * LANES : (j + 1) * LANES] = values_ref[
                first + j : first + j + 1, r * LANES : (r + 1) * LANES
            ]


def unfold(tail_ref, values_ref, first, s):
    for j in range(s.extra):
        for r in range(s.folds):
            values_ref[first + j : first + j + 1, r * LANES : (r + 1) * LANES] = tail_ref[
                r : r + 1, j * LANES : (j + 1) * LANES
            ]


def put_scores(route_row, score_row, expert, tail_ref, s):
    col, rank = slot_columns(route_row, s)
    hit = (col == expert) & (rank == iota((s.tok, LANES), 1))
    row = jnp.sum(jnp.where(hit, as_column(score_row), 0.0), axis=0, keepdims=True)
    put_row(row, tail_ref, s)


def add_gated(out_ref, base, main, extra, total, s):
    d = s.depth
    out_ref[:, :d] = (read(base, 0, d).astype(F32) + main * total[:, :d]).astype(BF16)
    for j in range(s.extra):
        at = slice(d + j * LANES, d + (j + 1) * LANES)
        value = read(base, at.start, at.stop).astype(F32) + extra[j] * total[:, at]
        out_ref[:, at] = value.astype(BF16)


def read(pieces, low, high):
    found, at = [], 0
    for piece in pieces:
        width = piece.shape[1]
        a, b = max(low, at), min(high, at + width)
        if a < b:
            found.append(piece[:, a - at : b - at])
        at += width
    return found[0] if len(found) == 1 else jnp.concatenate(found, axis=1)


def write(pieces, low, value):
    at = 0
    for piece in pieces:
        width = piece.shape[1]
        a, b = max(low, at), min(low + value.shape[1], at + width)
        if a < b:
            piece[:, a - at : b - at] = value[:, a - low : b - low]
        at += width


def grouped(refs, s, pieces):
    one = 1 + (s.count - 1) * pieces
    packs = []
    for first in range(0, len(refs), one):
        packs.append(refs[first : first + 1])
        for at in range(first + 1, first + one, pieces):
            packs.append(refs[at : at + pieces])
    return packs


def pack_rows(s, route_row, x, outs, extra_ref, tail_ref, score_row=None):
    rank = slot_rows(route_row, s)
    slots = iota((s.main + 16, s.tok), 0)
    tail_ref[...] = jnp.zeros_like(tail_ref)
    for d in range(s.count):
        hit = route_row == expert_at(s, d)
        table = jnp.where(hit & (rank == slots), 1.0, 0.0).astype(BF16)
        rows = jnp.dot(table, x, preferred_element_type=F32)
        write(outs[d], 0, rows[: s.main].astype(BF16))
        extra_ref[...] = rows[s.main :]
        fold(extra_ref, 0, tail_ref, s)
        if score_row is not None:
            put_scores(route_row, score_row, expert_at(s, d), tail_ref, s)
        write(outs[d], s.depth, tail_ref[...].astype(BF16))


def first_kernel(s, route_hbm, score_hbm, x_hbm, *rest):
    outs = grouped(rest[:-6], s, PIECES)
    route_ref, score_ref, x_ref, extra_ref, tail_ref, sems = rest[-6:]
    copies = [
        pltpu.make_async_copy(src, dst, sems.at[i])
        for i, (src, dst) in enumerate(
            ((route_hbm, route_ref), (score_hbm, score_ref), (x_hbm, x_ref))
        )
    ]
    for copy in copies:
        copy.start()
    for copy in copies:
        copy.wait()
    route_row = route_ref[...].astype(F32)
    pack_rows(s, route_row, x_ref[...], outs, extra_ref, tail_ref, score_ref[...])


def pack_kernel(s, route_ref, x_ref, *rest):
    outs, (extra_ref, tail_ref) = grouped(rest[:-2], s, 1), rest[-2:]
    pack_rows(s, route_ref[...].astype(F32), x_ref[...], outs, extra_ref, tail_ref)


def load_kernel(*refs):
    sems = refs[-1]
    n = (len(refs) - 1) // 2
    copies = [pltpu.make_async_copy(refs[i], refs[n + i], sems.at[i]) for i in range(n)]
    for copy in copies:
        copy.start()
    for copy in copies:
        copy.wait()


def gather_packs(packs, rows_ref, extra_ref, tail_ref, s):
    extra_ref[...] = jnp.zeros_like(extra_ref)
    for i, pack in enumerate(packs):
        rows_ref[i * s.main : (i + 1) * s.main, :] = read(pack, 0, s.depth)
        tail_ref[...] = read(pack, s.depth, s.width).astype(F32)
        unfold(tail_ref, extra_ref, i * s.extra, s)
    rows_ref[s.blocks * s.main :, :] = extra_ref[...].astype(BF16)


def put(outs, i, at, value, s):
    if i < s.count:
        outs[i][:, at] = value
        return
    n = (len(outs) - s.count) // (s.blocks - s.count)
    rows = s.main // n
    for h in range(n):
        outs[s.count + (i - s.count) * n + h][:, at] = value[h * rows : (h + 1) * rows]


def scatter_chunk(value, outs, extra_ref, at, s):
    for i in range(s.blocks):
        put(outs, i, at, value[i * s.main : (i + 1) * s.main].astype(BF16), s)
    extra_ref[:, at] = value[s.blocks * s.main :]


def scatter_tails(outs, extra_ref, tail_ref, s, inner=None):
    for i in range(s.blocks):
        fold(extra_ref, i * s.extra, tail_ref, s)
        if inner is not None:
            first = s.blocks * s.main + i * s.extra
            extra = [inner[first + j : first + j + 1] for j in range(s.extra)]
            put_inner(inner[i * s.main : (i + 1) * s.main], extra, tail_ref, s)
        put(outs, i, slice(s.depth, s.width), tail_ref[...].astype(BF16), s)


def chunk_of(depth):
    for chunk in (512, 256, 128):
        if depth % chunk == 0:
            return chunk


def forward_kernel(s, *refs):
    n = s.slices * (1 + (s.count - 1) * PIECES)
    packs = grouped(refs[:n], s, PIECES)
    wg, wu, wd = refs[n : n + 3]
    outs = refs[n + 3 : -3]
    rows_ref, extra_ref, tail_ref = refs[-3:]
    chunk = chunk_of(s.depth)
    gather_packs(packs, rows_ref, extra_ref, tail_ref, s)
    g = u = None
    for c in range(0, s.depth, chunk):
        lhs = rows_ref[:, c : c + chunk]
        more_g = jnp.dot(lhs, wg[c : c + chunk, :], preferred_element_type=F32)
        more_u = jnp.dot(lhs, wu[c : c + chunk, :], preferred_element_type=F32)
        g = more_g if g is None else g + more_g
        u = more_u if u is None else u + more_u
    hidden = (g * jax.nn.sigmoid(g) * u).astype(BF16)
    tail_ref[...] = jnp.zeros_like(tail_ref)
    for c in range(0, s.depth, chunk):
        part = jnp.dot(hidden, wd[:, c : c + chunk], preferred_element_type=F32)
        scatter_chunk(part, outs, extra_ref, slice(c, c + chunk), s)
    scatter_tails(outs, extra_ref, tail_ref, s)


def saved_kernel(s, gate_ref, up_ref, c1_ref, c2_ref, hb_ref, g_ref, u_ref):
    me = lax.axis_index("expert")
    e, j = me // s.slices, me % s.slices
    g_ref[...] = jnp.zeros_like(g_ref)
    u_ref[...] = jnp.zeros_like(u_ref)
    for i in range(s.blocks):
        k, d = i // s.count, i % s.count
        source = (e + s.count - d) % s.count * s.slices + (j + s.slices - k) % s.slices
        for src, dst in ((gate_ref, g_ref), (up_ref, u_ref)):
            rows = src[source].astype(F32)
            dst[i * s.main : (i + 1) * s.main, :] = rows[: s.main]
            first = s.blocks * s.main + i * s.extra
            dst[first : first + s.extra, :] = rows[s.main :]
    g = g_ref[...]
    u = u_ref[...]
    sig = jax.nn.sigmoid(g)
    c1_ref[...] = u * sig * (1.0 + g * (1.0 - sig))
    c2_ref[...] = g * sig
    hb_ref[...] = (g * sig * u).astype(BF16).astype(F32)


def split_three(value):
    high = value.astype(BF16).astype(F32)
    rest = value - high
    mid = rest.astype(BF16).astype(F32)
    return high, mid, (rest - mid).astype(BF16).astype(F32)


def put_inner(main, extra, tail_ref, s):
    lane = iota((s.main, LANES), 1)
    row = jnp.sum(jnp.where(lane == iota((s.main, LANES), 0), main, 0.0), axis=0, keepdims=True)
    for j in range(s.extra):
        row = jnp.where(lane[:1] == float(s.main + j), extra[j], row)
    put_row(row, tail_ref, s)


def put_row(row, tail_ref, s):
    for p, piece in enumerate(split_three(row)):
        at = s.folds + 1 + p
        tail_ref[at : at + 1, :LANES] = piece


def get_row(tail, s):
    at = s.folds + 1
    return tail[at : at + 1] + tail[at + 1 : at + 2] + tail[at + 2 : at + 3]


def get_slots(row, s):
    lane = iota((s.main, LANES), 1)
    main = jnp.sum(jnp.where(lane == iota((s.main, LANES), 0), row, 0.0), axis=1, keepdims=True)
    extra = [
        jnp.sum(jnp.where(lane[:1] == float(s.main + j), row, 0.0), axis=1, keepdims=True)
        for j in range(s.extra)
    ]
    return main, extra


def backward_kernel(s, *refs):
    packs = grouped(refs[: s.blocks], s, 1)
    c1, c2, hb, wg, wu, wd = refs[s.blocks : s.blocks + 6]
    outs = refs[s.blocks + 6 : -3]
    rows_ref, extra_ref, tail_ref = refs[-3:]
    chunk = chunk_of(s.depth)
    gather_packs(packs, rows_ref, extra_ref, tail_ref, s)
    a = None
    for c in range(0, s.depth, chunk):
        more = lax.dot_general(
            rows_ref[:, c : c + chunk], wd[:, c : c + chunk], NT, preferred_element_type=F32
        )
        a = more if a is None else a + more
    dgp = (a * c1[...]).astype(BF16)
    dup = (a * c2[...]).astype(BF16)
    inner = jnp.sum(a * hb[...], axis=1, keepdims=True)
    tail_ref[...] = jnp.zeros_like(tail_ref)
    for c in range(0, s.depth, chunk):
        part = lax.dot_general(
            dgp, wg[c : c + chunk, :], NT, preferred_element_type=F32
        ) + lax.dot_general(dup, wu[c : c + chunk, :], NT, preferred_element_type=F32)
        scatter_chunk(part, outs, extra_ref, slice(c, c + chunk), s)
    scatter_tails(outs, extra_ref, tail_ref, s, inner)


def total_of(parts, d, s):
    total = parts[d][...].astype(F32)
    n = (len(parts) - s.count) // (s.blocks - s.count)
    for i in range(s.count + d, s.blocks, s.count):
        first = s.count + (i - s.count) * n
        found = [part[...].astype(F32) for part in parts[first : first + n]]
        total = total + (found[0] if n == 1 else jnp.concatenate(found, axis=0))
    return total


def forward_sum_kernel(s, *refs):
    n = s.count + (s.blocks - s.count) * PIECES
    parts, bases = refs[:n], grouped(refs[n : n + 1 + (s.count - 1) * PIECES], s, PIECES)
    route_ref, outs = refs[-1 - s.count], refs[-s.count :]
    at = s.folds

    def fill(last):
        for i in range(s.count):
            d = turn_of(i, last, s)
            tail = read(bases[d], s.depth, s.depth + LANES).astype(F32)
            main, extra = get_slots(2.5 * get_row(tail, s), s)
            add_gated(outs[i], bases[d], main, extra, total_of(parts, d, s), s)
            spare = outs[i].shape[1] - s.width
            outs[i][:, s.width :] = jnp.zeros((s.main, spare), BF16)
            if d == 0:
                row = route_ref[...].astype(F32).astype(BF16)
                outs[i][at : at + 1, s.depth : s.depth + s.tok] = row

    last = lax.axis_index("section") == lax.axis_size("section") - 1
    pl.when(last)(functools.partial(fill, True))
    pl.when(jnp.logical_not(last))(functools.partial(fill, False))


def tokens_of(packs, route_row, rows_ref, extra_ref, tail_ref, s):
    extra_ref[...] = jnp.zeros_like(extra_ref)
    for d, pack in enumerate(packs):
        rows_ref[d * s.main : (d + 1) * s.main, :] = pack[:, : s.depth].astype(BF16)
        tail_ref[...] = pack[:, s.depth : s.width].astype(F32)
        unfold(tail_ref, extra_ref, d * s.extra, s)
    rows_ref[s.count * s.main :, :] = extra_ref[...].astype(BF16)
    col, rank = slot_columns(route_row, s)
    high = rows_ref.shape[0]
    place = jnp.full((s.tok, 1), -1.0, F32)
    for d in range(s.count):
        at = jnp.where(
            rank < float(s.main),
            rank + float(d * s.main),
            rank + float(s.count * s.main + d * s.extra - s.main),
        )
        place = jnp.where(col == expert_at(s, d), at, place)
    table = jnp.where(place == iota((s.tok, high), 1), 1.0, 0.0).astype(BF16)
    return jnp.dot(table, rows_ref[...], preferred_element_type=F32)


def forward_end_kernel(s, *refs):
    packs = refs[: s.count]
    out_ref, token_ref, rows_ref, extra_ref, tail_ref, row_ref = refs[s.count :]
    token_ref[...] = jnp.zeros_like(token_ref)

    def fill(last):
        mine = [packs[turn_of(d, last, s)] for d in range(s.count)]
        row_ref[...] = mine[0][:, s.depth : s.depth + LANES].astype(F32)
        route_row = row_ref[s.folds : s.folds + 1, : s.tok]
        out_ref[...] = tokens_of(mine, route_row, rows_ref, extra_ref, tail_ref, s).astype(BF16)

    first = lax.axis_index("section") == 0
    pl.when(first)(functools.partial(fill, True))
    pl.when(jnp.logical_not(first))(functools.partial(fill, False))


def backward_sum_kernel(s, *refs):
    n = s.count - 1
    parts, outs, tail_ref = refs[: n * s.slices], refs[-1 - n : -1], refs[-1]
    for d in range(n):
        total = parts[d][...].astype(F32)
        for part in parts[n + d :: n]:
            total = total + part[...].astype(F32)
        outs[d][:, : s.depth] = total[:, : s.depth].astype(BF16)
        tail_ref[...] = total[:, s.depth :]
        put_row(get_row(total[:, s.depth : s.depth + LANES], s), tail_ref, s)
        outs[d][:, s.depth :] = tail_ref[...].astype(BF16)


def backward_end_kernel(s, *refs):
    own, packs = refs[: s.slices], refs[s.slices : s.slices + s.count - 1]
    n = s.slices + s.count - 1
    dy_ref, route_ref, score_ref, _, out_ref, grad_ref = refs[n : n + 6]
    rows_ref, extra_ref, tail_ref = refs[n + 6 :]
    total = own[0][...].astype(F32)
    for part in own[1:]:
        total = total + part[...].astype(F32)
    packs = [total, *packs]
    route_row = route_ref[...].astype(F32)
    rows = tokens_of(packs, route_row, rows_ref, extra_ref, tail_ref, s)
    gate = as_column(2.5 * score_ref[...])
    out_ref[...] = (dy_ref[...].astype(F32) + gate * rows).astype(BF16)
    rank = slot_rows(route_row, s)
    dgate = jnp.zeros((1, s.tok), F32)
    for d in range(s.count):
        hit = route_row == expert_at(s, d)
        tail = packs[d][:, s.depth : s.depth + LANES].astype(F32)
        main, extra = get_slots(get_row(tail, s), s)
        dgate += jnp.sum(
            jnp.where(hit & (rank == iota((s.main, s.tok), 0)), main, 0.0), axis=0, keepdims=True
        )
        for j in range(s.extra):
            dgate += jnp.where(hit & (rank == float(s.main + j)), extra[j], 0.0)
    grad_ref[...] = 2.5 * dgate


VMEM = pl.BlockSpec(memory_space=pltpu.VMEM)
HBM = pl.BlockSpec(memory_space=pltpu.HBM)


def call(kernel, name, outs, scratch, ins, *args, mib=16, place=jax.ShapeDtypeStruct):
    shapes = [place(shape, kind) for shape, kind in outs]
    args = [
        pltpu.with_memory_space_constraint(a, pltpu.HBM) if spec is HBM else a
        for a, spec in zip(args, ins)
    ]
    return pl.pallas_call(
        kernel,
        out_shape=shapes,
        in_specs=ins,
        out_specs=[VMEM] * len(shapes),
        scratch_shapes=scratch,
        compiler_params=pltpu.CompilerParams(vmem_limit_bytes=mib << 20),
        cost_estimate=pl.CostEstimate(flops=0, bytes_accessed=0, transcendentals=0),
        name=name,
    )(*args)


def tail_scratch(s, rows):
    return [
        pltpu.VMEM((rows, s.depth), F32),
        pltpu.VMEM((s.main, LANES * s.extra), F32),
    ]


def load(*arrays):
    return call(
        load_kernel,
        "load",
        [(a.shape, a.dtype) for a in arrays],
        [pltpu.SemaphoreType.DMA((len(arrays),))],
        [HBM] * len(arrays),
        *arrays,
    )


def row_scratch(s):
    return [pltpu.VMEM((s.rows, s.depth), BF16), *tail_scratch(s, s.tail_rows)]


def cross(s, packs, pieces):
    return [packs[0]] + [across(p, 1 + i // pieces, s) for i, p in enumerate(packs[1:])]


def spread(s, got):
    return list(got) + [beside(b, k, s) for k in range(1, s.slices) for b in got]


def hold(values, *after):
    return lax.optimization_barrier((values, after))[0]


def parts_shape(s, width, pieces):
    kept = [((s.main, width), BF16)] * s.count
    return kept + [((s.main // pieces, width), BF16)] * ((s.blocks - s.count) * pieces)


def gather_parts(s, parts):
    n = (len(parts) - s.count) // (s.blocks - s.count)
    moved = [beside(p, -(i // n // s.count + 1), s) for i, p in enumerate(parts[s.count :])]
    return list(parts[: s.count]) + moved


def step(routes, run, *args):
    like = jax.eval_shape(run, *args)
    skip = lambda *_: jax.tree.map(lambda a: jnp.zeros(a.shape, a.dtype), like)
    return lax.cond(routes[0, 0] < EXPERTS, run, skip, *args)


def end_scratch(s):
    low = -(-(s.count * s.extra) // 16) * 16
    return [pltpu.VMEM((s.count * s.main + low, s.depth), BF16), *tail_scratch(s, low)]


def body(
    x_fwd,
    saved_gate,
    saved_up,
    grad_next,
    routes_fwd,
    routes_bwd,
    scores_fwd,
    scores_bwd,
    w_gate,
    w_up,
    w_down,
):
    groups = lax.axis_size("expert")
    tok, depth = x_fwd.shape[1:]
    s = Sizes(saved_gate.shape[2], depth, EXPERTS, groups // EXPERTS, tok)
    hidden = w_gate.shape[2]
    route_a = routes_fwd.reshape(1, tok)
    route_b = routes_bwd.reshape(1, tok)
    score_a = scores_fwd.reshape(1, tok)
    score_b = scores_bwd.reshape(1, tok)

    packed = [((s.main, s.width), BF16)] * s.count
    sent_a = call(
        functools.partial(first_kernel, s),
        "first",
        packed[:1] + [((s.main, s.width // PIECES), BF16)] * (PIECES * (s.count - 1)),
        [
            pltpu.VMEM((1, tok), jnp.int32),
            pltpu.VMEM((1, tok), F32),
            pltpu.VMEM((tok, depth), BF16),
            *tail_scratch(s, 16),
            pltpu.SemaphoreType.DMA((3,)),
        ],
        [HBM] * 3,
        route_a,
        score_a,
        x_fwd[0],
    )
    upstream = from_behind(grad_next, "section", -1)[0]
    wg, wu, wd, route_a, route_b, score_b = load(
        w_gate[0], w_up[0], w_down[0], route_a, route_b, score_b
    )
    factors = call(
        functools.partial(saved_kernel, s),
        "saved",
        [((s.rows, hidden), F32)] * 3,
        [pltpu.VMEM((s.rows, hidden), F32)] * 2,
        [VMEM] * 2,
        saved_gate[0],
        saved_up[0],
    )
    wide = s.width + LANES

    def backward(got, *rest):
        rows = spread(s, got)
        parts = call(
            functools.partial(backward_kernel, s),
            "backward",
            packed * s.slices,
            row_scratch(s),
            [VMEM] * (s.blocks + 6),
            *rows,
            *rest,
        )
        others = [p for i, p in enumerate(parts) if i % s.count]
        others = [beside(p, -(i // (s.count - 1)), s) if i >= s.count - 1 else p for i, p in enumerate(others)]
        sums = call(
            functools.partial(backward_sum_kernel, s),
            "backward_sum",
            packed[1:],
            [pltpu.VMEM((s.main, LANES * s.extra), F32)],
            [VMEM] * len(others),
            *others,
            place=pltpu.VMEM,
        )
        return tuple(parts[:: s.count]), tuple(sums)

    got = cross(s, sent_a, PIECES)
    got[1:] = hold(got[1:], route_a, factors)
    rows_a = spread(s, got)
    sent_b = call(
        functools.partial(pack_kernel, s),
        "pack",
        packed,
        tail_scratch(s, 16),
        [VMEM] * 2,
        route_b,
        hold(upstream, got[1:]),
    )
    got_b = cross(s, sent_b, 1)
    parts_a = call(
        functools.partial(forward_kernel, s),
        "forward",
        parts_shape(s, s.width, PIECES),
        row_scratch(s),
        [VMEM] * (len(rows_a) + 3),
        *hold(rows_a, sent_b),
        wg,
        wu,
        wd,
    )
    parts_a = gather_parts(s, parts_a)
    sums_a = call(
        functools.partial(forward_sum_kernel, s),
        "forward_sum",
        [((s.main, wide), BF16)] * s.count,
        [],
        [VMEM] * (len(parts_a) + len(got) + 1),
        *parts_a,
        *got,
        route_a,
    )
    moved = [to_next(y, i, s) for i, y in enumerate(sums_a)]
    got_b[1:] = hold(got_b[1:], sums_a)
    own_b, sums_b = step(route_b, backward, got_b, *factors, wg, wu, wd)
    back_b = [across(y, -1 - d, s) for d, y in enumerate(sums_b)]
    own_b = [beside(p, -k, s) if k else p for k, p in enumerate(own_b)]
    next_input, token = call(
        functools.partial(forward_end_kernel, s),
        "forward_end",
        [((tok, depth), BF16), ((8, LANES), F32)],
        end_scratch(s) + [pltpu.VMEM((s.main, LANES), F32)],
        [VMEM] * s.count,
        *moved,
    )
    input_grad, score_grad = call(
        functools.partial(backward_end_kernel, s),
        "backward_end",
        [((tok, depth), BF16), ((1, tok), F32)],
        end_scratch(s),
        [VMEM] * (s.slices + s.count - 1 + 4),
        *own_b,
        *back_b,
        upstream,
        route_b,
        score_b,
        token,
    )
    return next_input[None], input_grad[None], score_grad.reshape(1, tok, 1)


def solution(mesh):
    placed = (
        P("section", "expert", None),
        P("section", None, None, "expert"),
        P("section", None, None, "expert"),
        P("section", "expert", None),
        P("section", "expert", None),
        P("section", "expert", None),
        P("section", "expert", None),
        P("section", "expert", None),
        P("section", None, "expert"),
        P("section", None, "expert"),
        P("section", "expert", None),
    )
    return jax.shard_map(
        body,
        mesh=mesh,
        in_specs=placed,
        out_specs=(
            P("section", "expert", None),
            P("section", "expert", None),
            P("section", "expert", None),
        ),
        check_vma=False,
    )
```

```python
import functools

import jax
import jax.numpy as jnp
from jax import lax
from jax.experimental import pallas as pl
from jax.experimental.pallas import tpu as pltpu
from jax.sharding import PartitionSpec as P

EXPERTS = 2
LANES = 128
PIECES = 2
F32 = jnp.float32
BF16 = jnp.bfloat16
NT = (((1,), (1,)), ((), ()))


class Sizes:
    def __init__(self, cap, depth, count, slices, tok):
        self.cap, self.depth, self.count, self.slices, self.tok = cap, depth, count, slices, tok
        self.main = cap // 16 * 16
        self.extra = cap - self.main
        self.folds = depth // LANES
        assert self.folds + 4 <= self.main and depth % LANES == 0
        assert max(cap, tok) <= LANES
        self.width = depth + LANES * self.extra
        self.blocks = count * slices
        self.tail_rows = -(-(self.blocks * self.extra) // 16) * 16
        self.rows = self.blocks * self.main + self.tail_rows


def from_behind(block, axis, distance):
    devices = range(lax.axis_size(axis))
    route = [((i - distance) % len(devices), i) for i in devices]
    return lax.ppermute(block, axis, route)


def turn_of(i, last, s):
    return s.count - 1 - i if last else i


def to_next(block, i, s):
    sections, own = lax.axis_size("section"), s.count * s.slices
    route = [
        (
            l * own + e * s.slices + j,
            (l + 1) % sections * own
            + (e - turn_of(i, l == sections - 1, s)) % s.count * s.slices
            + j,
        )
        for l in range(sections)
        for e in range(s.count)
        for j in range(s.slices)
    ]
    return lax.ppermute(block, ("section", "expert"), route)


def across(block, distance, s):
    route = [
        (e * s.slices + j, (e + distance) % s.count * s.slices + j)
        for e in range(s.count)
        for j in range(s.slices)
    ]
    return lax.ppermute(block, "expert", route)


def beside(block, distance, s):
    route = [
        (e * s.slices + j, e * s.slices + (j + distance) % s.slices)
        for e in range(s.count)
        for j in range(s.slices)
    ]
    return lax.ppermute(block, "expert", route)


def iota(shape, dim):
    return lax.broadcasted_iota(jnp.int32, shape, dim).astype(F32)


def as_column(row):
    n = row.shape[1]
    return jnp.sum(
        jnp.where(iota((n, n), 0) == iota((n, n), 1), row, 0.0), axis=1, keepdims=True
    )


def own_expert(s):
    return lax.axis_index("expert") // s.slices


def expert_at(s, distance):
    return ((own_expert(s) + distance) % s.count).astype(F32)


def slot_rows(route_row, s):
    col = as_column(route_row)
    n = s.tok
    same = (col == route_row) & (iota((n, n), 0) < iota((n, n), 1))
    return jnp.sum(jnp.where(same, 1.0, 0.0), axis=0, keepdims=True)


def slot_columns(route_row, s):
    col = as_column(route_row)
    n = s.tok
    same = (col == route_row) & (iota((n, n), 1) < iota((n, n), 0))
    return col, jnp.sum(jnp.where(same, 1.0, 0.0), axis=1, keepdims=True)


def fold(values_ref, first, tail_ref, s):
    for j in range(s.extra):
        for r in range(s.folds):
            tail_ref[r : r + 1, j * LANES : (j + 1) * LANES] = values_ref[
                first + j : first + j + 1, r * LANES : (r + 1) * LANES
            ]


def unfold(tail_ref, values_ref, first, s):
    for j in range(s.extra):
        for r in range(s.folds):
            values_ref[first + j : first + j + 1, r * LANES : (r + 1) * LANES] = tail_ref[
                r : r + 1, j * LANES : (j + 1) * LANES
            ]


def put_scores(route_row, score_row, expert, tail_ref, s):
    col, rank = slot_columns(route_row, s)
    hit = (col == expert) & (rank == iota((s.tok, LANES), 1))
    row = jnp.sum(jnp.where(hit, as_column(score_row), 0.0), axis=0, keepdims=True)
    put_row(row, tail_ref, s)


def add_gated(out_ref, base, main, extra, total, s):
    d = s.depth
    out_ref[:, :d] = (read(base, 0, d).astype(F32) + main * total[:, :d]).astype(BF16)
    for j in range(s.extra):
        at = slice(d + j * LANES, d + (j + 1) * LANES)
        value = read(base, at.start, at.stop).astype(F32) + extra[j] * total[:, at]
        out_ref[:, at] = value.astype(BF16)


def read(pieces, low, high):
    found, at = [], 0
    for piece in pieces:
        width = piece.shape[1]
        a, b = max(low, at), min(high, at + width)
        if a < b:
            found.append(piece[:, a - at : b - at])
        at += width
    return found[0] if len(found) == 1 else jnp.concatenate(found, axis=1)


def write(pieces, low, value):
    at = 0
    for piece in pieces:
        width = piece.shape[1]
        a, b = max(low, at), min(low + value.shape[1], at + width)
        if a < b:
            piece[:, a - at : b - at] = value[:, a - low : b - low]
        at += width


def grouped(refs, s, pieces):
    one = 1 + (s.count - 1) * pieces
    packs = []
    for first in range(0, len(refs), one):
        packs.append(refs[first : first + 1])
        for at in range(first + 1, first + one, pieces):
            packs.append(refs[at : at + pieces])
    return packs


def pack_rows(s, route_row, x, outs, extra_ref, tail_ref, score_row=None):
    rank = slot_rows(route_row, s)
    slots = iota((s.main + 16, s.tok), 0)
    tail_ref[...] = jnp.zeros_like(tail_ref)
    for d in range(s.count):
        hit = route_row == expert_at(s, d)
        table = jnp.where(hit & (rank == slots), 1.0, 0.0).astype(BF16)
        rows = jnp.dot(table, x, preferred_element_type=F32)
        write(outs[d], 0, rows[: s.main].astype(BF16))
        extra_ref[...] = rows[s.main :]
        fold(extra_ref, 0, tail_ref, s)
        if score_row is not None:
            put_scores(route_row, score_row, expert_at(s, d), tail_ref, s)
        write(outs[d], s.depth, tail_ref[...].astype(BF16))


def first_kernel(s, route_hbm, score_hbm, x_hbm, *rest):
    outs = grouped(rest[:-6], s, PIECES)
    route_ref, score_ref, x_ref, extra_ref, tail_ref, sems = rest[-6:]
    copies = [
        pltpu.make_async_copy(src, dst, sems.at[i])
        for i, (src, dst) in enumerate(
            ((route_hbm, route_ref), (score_hbm, score_ref), (x_hbm, x_ref))
        )
    ]
    for copy in copies:
        copy.start()
    for copy in copies:
        copy.wait()
    route_row = route_ref[...].astype(F32)
    pack_rows(s, route_row, x_ref[...], outs, extra_ref, tail_ref, score_ref[...])


def pack_kernel(s, route_ref, x_ref, *rest):
    outs, (extra_ref, tail_ref) = grouped(rest[:-2], s, 1), rest[-2:]
    pack_rows(s, route_ref[...].astype(F32), x_ref[...], outs, extra_ref, tail_ref)


def load_kernel(*refs):
    sems = refs[-1]
    n = (len(refs) - 1) // 2
    copies = [pltpu.make_async_copy(refs[i], refs[n + i], sems.at[i]) for i in range(n)]
    for copy in copies:
        copy.start()
    for copy in copies:
        copy.wait()


def gather_packs(packs, rows_ref, extra_ref, tail_ref, s):
    extra_ref[...] = jnp.zeros_like(extra_ref)
    for i, pack in enumerate(packs):
        rows_ref[i * s.main : (i + 1) * s.main, :] = read(pack, 0, s.depth)
        tail_ref[...] = read(pack, s.depth, s.width).astype(F32)
        unfold(tail_ref, extra_ref, i * s.extra, s)
    rows_ref[s.blocks * s.main :, :] = extra_ref[...].astype(BF16)


def put(outs, i, at, value, s):
    if i < s.count:
        outs[i][:, at] = value
        return
    n = (len(outs) - s.count) // (s.blocks - s.count)
    rows = s.main // n
    for h in range(n):
        outs[s.count + (i - s.count) * n + h][:, at] = value[h * rows : (h + 1) * rows]


def scatter_chunk(value, outs, extra_ref, at, s):
    for i in range(s.blocks):
        put(outs, i, at, value[i * s.main : (i + 1) * s.main].astype(BF16), s)
    extra_ref[:, at] = value[s.blocks * s.main :]


def scatter_tails(outs, extra_ref, tail_ref, s, inner=None):
    for i in range(s.blocks):
        fold(extra_ref, i * s.extra, tail_ref, s)
        if inner is not None:
            first = s.blocks * s.main + i * s.extra
            extra = [inner[first + j : first + j + 1] for j in range(s.extra)]
            put_inner(inner[i * s.main : (i + 1) * s.main], extra, tail_ref, s)
        put(outs, i, slice(s.depth, s.width), tail_ref[...].astype(BF16), s)


def chunk_of(depth):
    for chunk in (512, 256, 128):
        if depth % chunk == 0:
            return chunk


def forward_kernel(s, *refs):
    n = s.slices * (1 + (s.count - 1) * PIECES)
    packs = grouped(refs[:n], s, PIECES)
    wg, wu, wd = refs[n : n + 3]
    outs = refs[n + 3 : -3]
    rows_ref, extra_ref, tail_ref = refs[-3:]
    chunk = chunk_of(s.depth)
    gather_packs(packs, rows_ref, extra_ref, tail_ref, s)
    g = u = None
    for c in range(0, s.depth, chunk):
        lhs = rows_ref[:, c : c + chunk]
        more_g = jnp.dot(lhs, wg[c : c + chunk, :], preferred_element_type=F32)
        more_u = jnp.dot(lhs, wu[c : c + chunk, :], preferred_element_type=F32)
        g = more_g if g is None else g + more_g
        u = more_u if u is None else u + more_u
    hidden = (g * jax.nn.sigmoid(g) * u).astype(BF16)
    tail_ref[...] = jnp.zeros_like(tail_ref)
    for c in range(0, s.depth, chunk):
        part = jnp.dot(hidden, wd[:, c : c + chunk], preferred_element_type=F32)
        scatter_chunk(part, outs, extra_ref, slice(c, c + chunk), s)
    scatter_tails(outs, extra_ref, tail_ref, s)


def saved_kernel(s, gate_ref, up_ref, c1_ref, c2_ref, hb_ref, g_ref, u_ref):
    me = lax.axis_index("expert")
    e, j = me // s.slices, me % s.slices
    g_ref[...] = jnp.zeros_like(g_ref)
    u_ref[...] = jnp.zeros_like(u_ref)
    for i in range(s.blocks):
        k, d = i // s.count, i % s.count
        source = (e + s.count - d) % s.count * s.slices + (j + s.slices - k) % s.slices
        for src, dst in ((gate_ref, g_ref), (up_ref, u_ref)):
            rows = src[source].astype(F32)
            dst[i * s.main : (i + 1) * s.main, :] = rows[: s.main]
            first = s.blocks * s.main + i * s.extra
            dst[first : first + s.extra, :] = rows[s.main :]
    g = g_ref[...]
    u = u_ref[...]
    sig = jax.nn.sigmoid(g)
    c1_ref[...] = u * sig * (1.0 + g * (1.0 - sig))
    c2_ref[...] = g * sig
    hb_ref[...] = (g * sig * u).astype(BF16).astype(F32)


def split_three(value):
    high = value.astype(BF16).astype(F32)
    rest = value - high
    mid = rest.astype(BF16).astype(F32)
    return high, mid, (rest - mid).astype(BF16).astype(F32)


def put_inner(main, extra, tail_ref, s):
    lane = iota((s.main, LANES), 1)
    row = jnp.sum(jnp.where(lane == iota((s.main, LANES), 0), main, 0.0), axis=0, keepdims=True)
    for j in range(s.extra):
        row = jnp.where(lane[:1] == float(s.main + j), extra[j], row)
    put_row(row, tail_ref, s)


def put_row(row, tail_ref, s):
    for p, piece in enumerate(split_three(row)):
        at = s.folds + 1 + p
        tail_ref[at : at + 1, :LANES] = piece


def get_row(tail, s):
    at = s.folds + 1
    return tail[at : at + 1] + tail[at + 1 : at + 2] + tail[at + 2 : at + 3]


def get_slots(row, s):
    lane = iota((s.main, LANES), 1)
    main = jnp.sum(jnp.where(lane == iota((s.main, LANES), 0), row, 0.0), axis=1, keepdims=True)
    extra = [
        jnp.sum(jnp.where(lane[:1] == float(s.main + j), row, 0.0), axis=1, keepdims=True)
        for j in range(s.extra)
    ]
    return main, extra


def backward_kernel(s, *refs):
    packs = grouped(refs[: s.blocks], s, 1)
    c1, c2, hb, wg, wu, wd = refs[s.blocks : s.blocks + 6]
    outs = refs[s.blocks + 6 : -3]
    rows_ref, extra_ref, tail_ref = refs[-3:]
    chunk = chunk_of(s.depth)
    gather_packs(packs, rows_ref, extra_ref, tail_ref, s)
    a = None
    for c in range(0, s.depth, chunk):
        more = lax.dot_general(
            rows_ref[:, c : c + chunk], wd[:, c : c + chunk], NT, preferred_element_type=F32
        )
        a = more if a is None else a + more
    dgp = (a * c1[...]).astype(BF16)
    dup = (a * c2[...]).astype(BF16)
    inner = jnp.sum(a * hb[...], axis=1, keepdims=True)
    tail_ref[...] = jnp.zeros_like(tail_ref)
    for c in range(0, s.depth, chunk):
        part = lax.dot_general(
            dgp, wg[c : c + chunk, :], NT, preferred_element_type=F32
        ) + lax.dot_general(dup, wu[c : c + chunk, :], NT, preferred_element_type=F32)
        scatter_chunk(part, outs, extra_ref, slice(c, c + chunk), s)
    scatter_tails(outs, extra_ref, tail_ref, s, inner)


def total_of(parts, d, s):
    total = parts[d][...].astype(F32)
    n = (len(parts) - s.count) // (s.blocks - s.count)
    for i in range(s.count + d, s.blocks, s.count):
        first = s.count + (i - s.count) * n
        found = [part[...].astype(F32) for part in parts[first : first + n]]
        total = total + (found[0] if n == 1 else jnp.concatenate(found, axis=0))
    return total


def forward_sum_kernel(s, *refs):
    n = s.count + (s.blocks - s.count) * PIECES
    parts, bases = refs[:n], grouped(refs[n : n + 1 + (s.count - 1) * PIECES], s, PIECES)
    route_ref, outs = refs[-1 - s.count], refs[-s.count :]
    at = s.folds

    def fill(last):
        for i in range(s.count):
            d = turn_of(i, last, s)
            tail = read(bases[d], s.depth, s.depth + LANES).astype(F32)
            main, extra = get_slots(2.5 * get_row(tail, s), s)
            add_gated(outs[i], bases[d], main, extra, total_of(parts, d, s), s)
            spare = outs[i].shape[1] - s.width
            outs[i][:, s.width :] = jnp.zeros((s.main, spare), BF16)
            if d == 0:
                row = route_ref[...].astype(F32).astype(BF16)
                outs[i][at : at + 1, s.depth : s.depth + s.tok] = row

    last = lax.axis_index("section") == lax.axis_size("section") - 1
    pl.when(last)(functools.partial(fill, True))
    pl.when(jnp.logical_not(last))(functools.partial(fill, False))


def tokens_of(packs, route_row, rows_ref, extra_ref, tail_ref, s):
    extra_ref[...] = jnp.zeros_like(extra_ref)
    for d, pack in enumerate(packs):
        rows_ref[d * s.main : (d + 1) * s.main, :] = pack[:, : s.depth].astype(BF16)
        tail_ref[...] = pack[:, s.depth : s.width].astype(F32)
        unfold(tail_ref, extra_ref, d * s.extra, s)
    rows_ref[s.count * s.main :, :] = extra_ref[...].astype(BF16)
    col, rank = slot_columns(route_row, s)
    high = rows_ref.shape[0]
    place = jnp.full((s.tok, 1), -1.0, F32)
    for d in range(s.count):
        at = jnp.where(
            rank < float(s.main),
            rank + float(d * s.main),
            rank + float(s.count * s.main + d * s.extra - s.main),
        )
        place = jnp.where(col == expert_at(s, d), at, place)
    return jnp.where(place == iota((s.tok, high), 1), 1.0, 0.0).astype(BF16)


def send_out(value_of, out_hbm, chunks_ref, sems):
    n, _, width = chunks_ref.shape
    copies = []
    for c in range(n):
        at = slice(c * width, (c + 1) * width)
        chunks_ref[c] = value_of(at).astype(BF16)
        to = out_hbm.at[:, pl.ds(c * width, width)]
        copies.append(pltpu.make_async_copy(chunks_ref.at[c], to, sems.at[c]))
        copies[-1].start()
    for copy in copies:
        copy.wait()


def forward_end_kernel(s, *refs):
    packs = refs[: s.count]
    out_ref, token_ref, rows_ref, extra_ref, tail_ref, chunks_ref, sems, row_ref = refs[s.count :]
    token_ref[...] = jnp.zeros_like(token_ref)

    def fill(last):
        mine = [packs[turn_of(d, last, s)] for d in range(s.count)]
        row_ref[...] = mine[0][:, s.depth : s.depth + LANES].astype(F32)
        route_row = row_ref[s.folds : s.folds + 1, : s.tok]
        table = tokens_of(mine, route_row, rows_ref, extra_ref, tail_ref, s)

        def rows(at):
            return jnp.dot(table, rows_ref[:, at], preferred_element_type=F32)

        send_out(rows, out_ref, chunks_ref, sems)

    first = lax.axis_index("section") == 0
    pl.when(first)(functools.partial(fill, True))
    pl.when(jnp.logical_not(first))(functools.partial(fill, False))


def backward_sum_kernel(s, *refs):
    n = s.count - 1
    parts, outs, tail_ref = refs[: n * s.slices], refs[-1 - n : -1], refs[-1]
    for d in range(n):
        total = parts[d][...].astype(F32)
        for part in parts[n + d :: n]:
            total = total + part[...].astype(F32)
        outs[d][:, : s.depth] = total[:, : s.depth].astype(BF16)
        tail_ref[...] = total[:, s.depth :]
        put_row(get_row(total[:, s.depth : s.depth + LANES], s), tail_ref, s)
        outs[d][:, s.depth :] = tail_ref[...].astype(BF16)


def backward_end_kernel(s, *refs):
    own, packs = refs[: s.slices], refs[s.slices : s.slices + s.count - 1]
    n = s.slices + s.count - 1
    dy_ref, route_ref, score_ref, _, out_ref, grad_ref = refs[n : n + 6]
    rows_ref, extra_ref, tail_ref, chunks_ref, sems = refs[n + 6 :]
    total = own[0][...].astype(F32)
    for part in own[1:]:
        total = total + part[...].astype(F32)
    packs = [total, *packs]
    route_row = route_ref[...].astype(F32)
    table = tokens_of(packs, route_row, rows_ref, extra_ref, tail_ref, s)
    gate = as_column(2.5 * score_ref[...])

    def rows(at):
        moved = jnp.dot(table, rows_ref[:, at], preferred_element_type=F32)
        return dy_ref[:, at].astype(F32) + gate * moved

    send_out(rows, out_ref, chunks_ref, sems)
    rank = slot_rows(route_row, s)
    dgate = jnp.zeros((1, s.tok), F32)
    for d in range(s.count):
        hit = route_row == expert_at(s, d)
        tail = packs[d][:, s.depth : s.depth + LANES].astype(F32)
        main, extra = get_slots(get_row(tail, s), s)
        dgate += jnp.sum(
            jnp.where(hit & (rank == iota((s.main, s.tok), 0)), main, 0.0), axis=0, keepdims=True
        )
        for j in range(s.extra):
            dgate += jnp.where(hit & (rank == float(s.main + j)), extra[j], 0.0)
    grad_ref[...] = 2.5 * dgate


VMEM = pl.BlockSpec(memory_space=pltpu.VMEM)
HBM = pl.BlockSpec(memory_space=pltpu.HBM)


def call(kernel, name, outs, scratch, ins, *args, mib=16, place=jax.ShapeDtypeStruct, to=()):
    shapes = [place(shape, kind) for shape, kind in outs]
    args = [
        pltpu.with_memory_space_constraint(a, pltpu.HBM) if spec is HBM else a
        for a, spec in zip(args, ins)
    ]
    return pl.pallas_call(
        kernel,
        out_shape=shapes,
        in_specs=ins,
        out_specs=[HBM if i in to else VMEM for i in range(len(shapes))],
        scratch_shapes=scratch,
        compiler_params=pltpu.CompilerParams(vmem_limit_bytes=mib << 20),
        cost_estimate=pl.CostEstimate(flops=0, bytes_accessed=0, transcendentals=0),
        name=name,
    )(*args)


def tail_scratch(s, rows):
    return [
        pltpu.VMEM((rows, s.depth), F32),
        pltpu.VMEM((s.main, LANES * s.extra), F32),
    ]


def load(*arrays):
    return call(
        load_kernel,
        "load",
        [(a.shape, a.dtype) for a in arrays],
        [pltpu.SemaphoreType.DMA((len(arrays),))],
        [HBM] * len(arrays),
        *arrays,
    )


def row_scratch(s):
    return [pltpu.VMEM((s.rows, s.depth), BF16), *tail_scratch(s, s.tail_rows)]


def cross(s, packs, pieces):
    return [packs[0]] + [across(p, 1 + i // pieces, s) for i, p in enumerate(packs[1:])]


def spread(s, got):
    return list(got) + [beside(b, k, s) for k in range(1, s.slices) for b in got]


def hold(values, *after):
    return lax.optimization_barrier((values, after))[0]


def parts_shape(s, width, pieces):
    kept = [((s.main, width), BF16)] * s.count
    return kept + [((s.main // pieces, width), BF16)] * ((s.blocks - s.count) * pieces)


def gather_parts(s, parts):
    n = (len(parts) - s.count) // (s.blocks - s.count)
    moved = [beside(p, -(i // n // s.count + 1), s) for i, p in enumerate(parts[s.count :])]
    return list(parts[: s.count]) + moved


def step(routes, run, *args):
    like = jax.eval_shape(run, *args)
    skip = lambda *_: jax.tree.map(lambda a: jnp.zeros(a.shape, a.dtype), like)
    return lax.cond(routes[0, 0] < EXPERTS, run, skip, *args)


def end_scratch(s):
    low = -(-(s.count * s.extra) // 16) * 16
    chunks = 4 if s.depth % (4 * LANES) == 0 else 1
    return [
        pltpu.VMEM((s.count * s.main + low, s.depth), BF16),
        *tail_scratch(s, low),
        pltpu.VMEM((chunks, s.tok, s.depth // chunks), BF16),
        pltpu.SemaphoreType.DMA((chunks,)),
    ]


def body(
    x_fwd,
    saved_gate,
    saved_up,
    grad_next,
    routes_fwd,
    routes_bwd,
    scores_fwd,
    scores_bwd,
    w_gate,
    w_up,
    w_down,
):
    groups = lax.axis_size("expert")
    tok, depth = x_fwd.shape[1:]
    s = Sizes(saved_gate.shape[2], depth, EXPERTS, groups // EXPERTS, tok)
    hidden = w_gate.shape[2]
    route_a = routes_fwd.reshape(1, tok)
    route_b = routes_bwd.reshape(1, tok)
    score_a = scores_fwd.reshape(1, tok)
    score_b = scores_bwd.reshape(1, tok)

    packed = [((s.main, s.width), BF16)] * s.count
    sent_a = call(
        functools.partial(first_kernel, s),
        "first",
        packed[:1] + [((s.main, s.width // PIECES), BF16)] * (PIECES * (s.count - 1)),
        [
            pltpu.VMEM((1, tok), jnp.int32),
            pltpu.VMEM((1, tok), F32),
            pltpu.VMEM((tok, depth), BF16),
            *tail_scratch(s, 16),
            pltpu.SemaphoreType.DMA((3,)),
        ],
        [HBM] * 3,
        route_a,
        score_a,
        x_fwd[0],
    )
    upstream = from_behind(grad_next, "section", -1)[0]
    wg, wu, wd, route_a, route_b, score_b = load(
        w_gate[0], w_up[0], w_down[0], route_a, route_b, score_b
    )
    factors = call(
        functools.partial(saved_kernel, s),
        "saved",
        [((s.rows, hidden), F32)] * 3,
        [pltpu.VMEM((s.rows, hidden), F32)] * 2,
        [VMEM] * 2,
        saved_gate[0],
        saved_up[0],
    )
    wide = s.width + LANES

    def backward(got, *rest):
        rows = spread(s, got)
        parts = call(
            functools.partial(backward_kernel, s),
            "backward",
            packed * s.slices,
            row_scratch(s),
            [VMEM] * (s.blocks + 6),
            *rows,
            *rest,
        )
        others = [p for i, p in enumerate(parts) if i % s.count]
        others = [beside(p, -(i // (s.count - 1)), s) if i >= s.count - 1 else p for i, p in enumerate(others)]
        sums = call(
            functools.partial(backward_sum_kernel, s),
            "backward_sum",
            packed[1:],
            [pltpu.VMEM((s.main, LANES * s.extra), F32)],
            [VMEM] * len(others),
            *others,
            place=pltpu.VMEM,
        )
        return tuple(parts[:: s.count]), tuple(sums)

    got = cross(s, sent_a, PIECES)
    got[1:] = hold(got[1:], route_a, factors)
    rows_a = spread(s, got)
    sent_b = call(
        functools.partial(pack_kernel, s),
        "pack",
        packed,
        tail_scratch(s, 16),
        [VMEM] * 2,
        route_b,
        hold(upstream, got[1:]),
    )
    got_b = cross(s, sent_b, 1)
    parts_a = call(
        functools.partial(forward_kernel, s),
        "forward",
        parts_shape(s, s.width, PIECES),
        row_scratch(s),
        [VMEM] * (len(rows_a) + 3),
        *hold(rows_a, sent_b),
        wg,
        wu,
        wd,
    )
    parts_a = gather_parts(s, parts_a)
    sums_a = call(
        functools.partial(forward_sum_kernel, s),
        "forward_sum",
        [((s.main, wide), BF16)] * s.count,
        [],
        [VMEM] * (len(parts_a) + len(got) + 1),
        *parts_a,
        *got,
        route_a,
    )
    moved = [to_next(y, i, s) for i, y in enumerate(sums_a)]
    got_b[1:] = hold(got_b[1:], sums_a)
    own_b, sums_b = step(route_b, backward, got_b, *factors, wg, wu, wd)
    back_b = [across(y, -1 - d, s) for d, y in enumerate(sums_b)]
    own_b = [beside(p, -k, s) if k else p for k, p in enumerate(own_b)]
    next_input, token = call(
        functools.partial(forward_end_kernel, s),
        "forward_end",
        [((tok, depth), BF16), ((8, LANES), F32)],
        end_scratch(s) + [pltpu.VMEM((s.main, LANES), F32)],
        [VMEM] * s.count,
        *moved,
        to=(0,),
    )
    input_grad, score_grad = call(
        functools.partial(backward_end_kernel, s),
        "backward_end",
        [((tok, depth), BF16), ((1, tok), F32)],
        end_scratch(s),
        [VMEM] * (s.slices + s.count - 1 + 4),
        *own_b,
        *back_b,
        upstream,
        route_b,
        score_b,
        token,
        to=(0,),
    )
    return next_input[None], input_grad[None], score_grad.reshape(1, tok, 1)


def solution(mesh):
    placed = (
        P("section", "expert", None),
        P("section", None, None, "expert"),
        P("section", None, None, "expert"),
        P("section", "expert", None),
        P("section", "expert", None),
        P("section", "expert", None),
        P("section", "expert", None),
        P("section", "expert", None),
        P("section", None, "expert"),
        P("section", None, "expert"),
        P("section", "expert", None),
    )
    return jax.shard_map(
        body,
        mesh=mesh,
        in_specs=placed,
        out_specs=(
            P("section", "expert", None),
            P("section", "expert", None),
            P("section", "expert", None),
        ),
        check_vma=False,
    )
```
